32 devices in a mesh: lon: 16 (over z, y, x), lat: 2 (over core).
Axes of the slice: x: 2, y: 2, z: 4, core: 2. Of those that a mesh axis runs over, the one named last changes fastest.
Arguments:
- latent_field: bfloat16 [2, 12, 192, 384], P(None, 'lat', 'lon'), may hold values from -6 to 6
- cotangent: bfloat16 [2, 12, 192, 384], P(None, 'lat', 'lon'), may hold values from -6 to 6
- norm_gain: float32 [384], replicated, may hold values from 0.1 to 1.9
- input_weight: bfloat16 [384, 1152], replicated, may hold values from -0.3125 to 0.3125
- output_weight: bfloat16 [384, 384], replicated, may hold values from -0.3125 to 0.3125
- bias_table: bfloat16 [2, 12, 3312], P('lat'), may hold values from -6 to 256
- regions: int32 [2, 12, 192], P(None, 'lat', 'lon'), may hold values from 0 to 3
Outputs:
- grad_field: bfloat16 [2, 12, 192, 384], P(None, 'lat', 'lon')
- grad_input_weight: bfloat16 [384, 1152], P('lon')
- grad_output_weight: bfloat16 [384, 384], P('lon')
- grad_gain: float32 [384], replicated
- grad_table: float32 [2, 12, 3312], P('lat')
The draws below stay inside these ranges and needn't reach their ends.
Inputs may be any that keep to these rules, and one draw needn't show every extreme that they name: `regions`: two cells of a window attend to each other only where their region ids agree.
All inputs are finite; a program needn't handle non-finite values.
Results may differ from the reference program's by a relative error of at most 0.02.
Values may be sent and summed in bfloat16 or wider, within the bound.
No kernel may reach another device: no remote copies, remote signals or barrier semaphores. Data moves between devices by JAX's collectives and lax.ppermute only.
A program may use at most 128 MiB of HBM per device.

```python
import math
import jax
import jax.numpy as jnp
from jax import lax

D = 384
HEADS = 12
LEV = 2
WIN_LAT = 6
WIN_LON = 12
NLAT = 12
NLON = 192
TOKENS = 4608
TYPES = 2
POS = 3312


def draw_bias_table(key, part):
    key = jax.random.fold_in(key, 17)
    base_key = jax.random.fold_in(key, 0)
    shape_full = (TYPES, HEADS, POS)
    values = jnp.clip(jax.random.normal(base_key, shape_full, jnp.float32), -6.0, 6.0)
    return values.astype(jnp.bfloat16)


def plant(drawn, own_key, low, high):
    longest = drawn.shape.index(max(drawn.shape))
    spots = []
    for shift in (0, 1):
        where = [jax.random.randint(jax.random.fold_in(own_key, axis), (), 0, length) for axis, length in enumerate(drawn.shape)]
        where[longest] = (where[longest] + shift) % drawn.shape[longest]
        spots.append(tuple(where))
    return drawn.at[spots[0]].set(low).at[spots[1]].set(high)


def raised(array, stream_key, source, target, blocks, factor):
    owner, partner = [(jnp.arange(array.shape[axis_at]) // (array.shape[axis_at] // blocks)).reshape([-1 if axis == axis_at else 1 for axis in range(array.ndim)]) for axis_at in (source, target)]
    chosen = jax.random.permutation(stream_key, blocks)[partner]
    strong = (owner == chosen) | (owner == (partner + blocks // 2) % blocks)
    return jnp.where(strong, factor * array, array)


def level_of(own_key, shape, shards, smallest, top_value):
    level = 1.0
    for position, shards_of in shards:
        heights = jax.random.uniform(jax.random.fold_in(jax.random.fold_in(own_key, 6), position), (shards_of,), jnp.float32, smallest / len(shards), top_value / len(shards))
        level = level * jnp.repeat(jnp.exp(heights), shape[position] // shards_of).reshape((-1,) + (1,) * (len(shape) - 1 - position))
    return level


def bell_draw(own_key, extent, scale, limit, shards=(), held_as=jnp.bfloat16):
    loudness = level_of(own_key, extent, shards, -0.22, 0.18) if shards else 1.0
    drawn = jax.random.normal(own_key, extent, jnp.float32) * scale * loudness
    return jnp.minimum(jnp.maximum(drawn, -limit), limit).astype(held_as)


def heavy_noise(key, extent, scale, reach, pieces, heavy, dtype=jnp.bfloat16):
    array = scale * jax.random.normal(key, extent, jnp.float32)
    if pieces:
        array = array * level_of(key, extent, pieces, -0.22, 0.18)
    return jnp.clip(raised(array, jax.random.fold_in(key, 3), *heavy), -reach, reach).astype(dtype)


def setup_inputs(seed: int = 0) -> dict:
    keys = jax.random.split(jax.random.key(seed), 8)
    latent_field = bell_draw(keys[0], (LEV, NLAT, NLON, D), 1.0, 6.0, ((1, 2), (2, 16)))
    cotangent = heavy_noise(keys[1], (LEV, NLAT, NLON, D), 1.0, 6.0, ((1, 2), (2, 16)), (2, 3, 16, 2.0))
    norm_gain = jnp.clip(1.0 + 0.18 * jax.random.normal(keys[2], (D,), jnp.float32), 0.1, 1.9)
    input_weight = bell_draw(keys[3], (D, 3 * D), D ** -0.5, 0.3125)
    output_weight = bell_draw(keys[4], (D, D), D ** -0.5, 0.3125)
    bias_table = draw_bias_table(jax.random.fold_in(keys[7], 71), 0)
    regions = plant(jax.random.randint(keys[6], (LEV, NLAT, NLON), 0, 4), jax.random.fold_in(keys[6], 1), 0, 3).astype(jnp.int32)
    return dict(latent_field=latent_field, cotangent=cotangent, norm_gain=norm_gain, input_weight=input_weight, output_weight=output_weight, bias_table=bias_table, regions=regions)


norm_eps = 1e-05
masked_score = -1000000000.0
highest = lax.Precision.HIGHEST

def product(spec, left_arr, right_arr):
    return jnp.einsum(spec, left_arr.astype(jnp.float32), right_arr.astype(jnp.float32), precision=highest)

def longitude_onehot(span_cells):
    first_index = jnp.arange(span_cells)[:, None, None]
    second_index = jnp.arange(span_cells)[None, :, None]
    offset_index = jnp.arange(2 * span_cells - 1)[None, None, :]
    return (first_index - second_index + span_cells - 1 == offset_index).astype(jnp.float32)

def expand_bias(bias_rows):
    num_bands, num_heads = (bias_rows.shape[0], bias_rows.shape[1])
    shaped = bias_rows.astype(jnp.float32).reshape(num_bands, num_heads, LEV, LEV, WIN_LAT, WIN_LAT, 2 * WIN_LON - 1)
    spread = jnp.einsum('bhxyuvr,cdr->bhxucyvd', shaped, longitude_onehot(WIN_LON), precision=highest)
    window_cells = LEV * WIN_LAT * WIN_LON
    return spread.reshape(num_bands, num_heads, window_cells, window_cells)

def fold_bias(grad_full):
    num_bands, num_heads = (grad_full.shape[0], grad_full.shape[1])
    shaped = grad_full.reshape(num_bands, num_heads, LEV, WIN_LAT, WIN_LON, LEV, WIN_LAT, WIN_LON)
    folded = jnp.einsum('bhxucyvd,cdr->bhxyuvr', shaped, longitude_onehot(WIN_LON), precision=highest)
    return folded.reshape(num_bands, num_heads, -1)

def to_windows(cells_grid):
    levels, row_count, col_count = (cells_grid.shape[0], cells_grid.shape[1], cells_grid.shape[2])
    trailing = cells_grid.shape[3:]
    shaped = cells_grid.reshape((levels, row_count // WIN_LAT, WIN_LAT, col_count // WIN_LON, WIN_LON) + trailing)
    axes_order = (1, 3, 0, 2, 4) + tuple(range(5, 5 + len(trailing)))
    return jnp.transpose(shaped, axes_order).reshape((row_count // WIN_LAT, col_count // WIN_LON, levels * WIN_LAT * WIN_LON) + trailing)

def from_windows(blocks):
    num_bands, num_windows, features = (blocks.shape[0], blocks.shape[1], blocks.shape[3])
    shaped = blocks.reshape(num_bands, num_windows, LEV, WIN_LAT, WIN_LON, features)
    return jnp.transpose(shaped, (2, 0, 3, 1, 4, 5)).reshape(LEV, num_bands * WIN_LAT, num_windows * WIN_LON, features)

def window_grads(normed_win, grad_win, region_win, bias_rows, input_weight, output_weight):
    num_bands, num_windows, window_cells, features = normed_win.shape
    head_dim = features // HEADS
    score_scale = head_dim ** (-0.5)
    flat_normed = normed_win.reshape(-1, features)
    projected = jnp.dot(flat_normed, input_weight, preferred_element_type=jnp.float32).astype(jnp.bfloat16)
    projected = projected.reshape(num_bands, num_windows, window_cells, 3, HEADS, head_dim)
    queries, key_rows, values = (projected[:, :, :, 0], projected[:, :, :, 1], projected[:, :, :, 2])
    scores = product('bwihe,bwjhe->bwhij', queries, key_rows) * score_scale
    scores = scores + expand_bias(bias_rows)[:, None]
    same_region = region_win[:, :, :, None] == region_win[:, :, None, :]
    scores = jnp.where(same_region[:, :, None], scores, masked_score)
    softmax_out = jax.nn.softmax(scores, axis=-1)
    probs_low = softmax_out.astype(jnp.bfloat16)
    attended = product('bwhij,bwjhe->bwihe', probs_low, values).astype(jnp.bfloat16)
    flat_attended = attended.reshape(-1, features)
    flat_grad = grad_win.reshape(-1, features)
    grad_attended = jnp.dot(flat_grad, output_weight.T, preferred_element_type=jnp.float32).astype(jnp.bfloat16)
    grad_attended = grad_attended.reshape(num_bands, num_windows, window_cells, HEADS, head_dim)
    grad_probs = product('bwihe,bwjhe->bwhij', grad_attended, values)
    grad_values = product('bwhij,bwihe->bwjhe', probs_low, grad_attended)
    grad_scores = softmax_out * (grad_probs - lax.optimization_barrier(jnp.sum(softmax_out * grad_probs, axis=-1, keepdims=True)))
    grad_table = fold_bias(lax.optimization_barrier(jnp.sum(grad_scores, axis=1)))
    scores_low = (grad_scores * score_scale).astype(jnp.bfloat16)
    grad_queries = product('bwhij,bwjhe->bwihe', scores_low, key_rows)
    grad_keys = product('bwhij,bwihe->bwjhe', scores_low, queries)
    grad_projected = jnp.stack([grad_queries, grad_keys, grad_values], axis=3).astype(jnp.bfloat16)
    grad_projected = grad_projected.reshape(-1, 3 * features)
    grad_normed = jnp.dot(grad_projected, input_weight.T, preferred_element_type=jnp.float32).astype(jnp.bfloat16)
    return (grad_normed.reshape(normed_win.shape), flat_normed, grad_projected, flat_attended, flat_grad, grad_table)

def reference(latent_field, cotangent, norm_gain, input_weight, output_weight, bias_table, regions):
    field_f32 = latent_field.astype(jnp.float32)
    centred = field_f32 - lax.optimization_barrier(jnp.mean(field_f32, axis=-1, keepdims=True))
    inv_std = lax.rsqrt(lax.optimization_barrier(jnp.mean(centred * centred, axis=-1, keepdims=True)) + norm_eps)
    normalized = centred * inv_std
    normed = (normalized * norm_gain).astype(jnp.bfloat16)
    shifts = (-(LEV // 2), -(WIN_LAT // 2), -(WIN_LON // 2))
    normed_shift = jnp.roll(normed, shifts, axis=(0, 1, 2))
    grad_shift = jnp.roll(cotangent, shifts, axis=(0, 1, 2))
    normed_win = to_windows(normed_shift)
    grad_win = to_windows(grad_shift)
    region_win = to_windows(regions)
    features = latent_field.shape[3]

    def one_band(running, band_item):
        normed_band, grad_band, region_band, table_band = band_item
        results = window_grads(normed_band[None], grad_band[None], region_band[None], table_band[None], input_weight, output_weight)
        grad_normed, flat_normed, grad_projected, flat_attended, flat_grad, grad_table = results
        weight_in = running[0] + jnp.dot(flat_normed.T, grad_projected, preferred_element_type=jnp.float32)
        weight_out = running[1] + jnp.dot(flat_attended.T, flat_grad, preferred_element_type=jnp.float32)
        return ((weight_in, weight_out), (grad_normed[0], grad_table[0]))
    initial = (jnp.zeros((features, 3 * features), jnp.float32), jnp.zeros((features, features), jnp.float32))
    sums, outputs = lax.scan(one_band, initial, (normed_win, grad_win, region_win, bias_table))
    grad_windows, grad_table = outputs
    grad_shifted = from_windows(grad_windows)
    grad_normed = jnp.roll(grad_shifted, (LEV // 2, WIN_LAT // 2, WIN_LON // 2), axis=(0, 1, 2))
    grad_f32 = grad_normed.astype(jnp.float32)
    scaled = grad_f32 * norm_gain
    grad_field = cotangent.astype(jnp.float32) + inv_std * (scaled - lax.optimization_barrier(jnp.mean(scaled, axis=-1, keepdims=True)) - normalized * lax.optimization_barrier(jnp.mean(scaled * normalized, axis=-1, keepdims=True)))
    factor = 1.0 / math.sqrt(TOKENS)
    grad_gain = lax.optimization_barrier(jnp.sum(grad_f32 * normalized, axis=(0, 1, 2))) * factor
    return (grad_field.astype(jnp.bfloat16), (sums[0] * factor).astype(jnp.bfloat16), (sums[1] * factor).astype(jnp.bfloat16), grad_gain, grad_table)
```

```python
import functools
import math

import jax
import jax.numpy as jnp
from jax import lax
from jax.experimental import pallas as pl
from jax.experimental.pallas import tpu as pltpu
from jax.sharding import PartitionSpec as P

HEADS = 12
LEV = 2
WIN_LAT = 6
WIN_LON = 12
PLANE = LEV * WIN_LAT
CELLS = PLANE * WIN_LON
SPAN = (2 * WIN_LON - 1) * PLANE
WIDE = 384
LANES = 128
QUARTER = LEV * (WIN_LAT // 2) * (WIN_LON // 2)

norm_eps = 1e-05
masked_score = -1000000000.0
f32 = jnp.float32
bf16 = jnp.bfloat16

QUARTERS = ((0, 0), (0, 1), (1, 0), (1, 1))


def segments():
    reach = SPAN // PLANE
    first = 0
    for level_i in range(LEV):
        for level_j in range(LEV):
            for row_i in range(WIN_LAT):
                for row_j in range(WIN_LAT):
                    yield first, level_i * WIN_LAT + row_i, level_j * WIN_LAT + row_j
                    first += reach


def rounded_up(value, step):
    return -(-value // step) * step


class Packet:
    def __init__(self, lon_count, features):
        self.lon_count = lon_count
        self.weight_rows = features // lon_count
        self.weight_used = 6 * self.weight_rows
        self.weight_size = rounded_up(self.weight_used, 16)
        self.table_tiles = -(-PLANE * SPAN // LANES)
        self.table_rows = HEADS * self.table_tiles
        self.table_size = rounded_up(self.table_rows, 4 * 16)
        self.quarter = self.table_size // 4


def nt_dot(left, right):
    return lax.dot_general(left, right, (((1,), (1,)), ((), ())), preferred_element_type=f32)


def nn_dot(left, right):
    return jnp.dot(left, right, preferred_element_type=f32)


def fetch(sources, targets, sems):
    copies = [pltpu.make_async_copy(src, dst, sems.at[at]) for at, (src, dst) in enumerate(zip(sources, targets))]
    for copy in copies:
        copy.start()
    return copies


def load_kernel(field_src, cot_src, *refs):
    out_refs, (field_ref, cot_ref, sems) = refs[:4], refs[4:]
    for copy in fetch((field_src, cot_src), (field_ref, cot_ref), sems):
        copy.wait()
    half_rows, half_cols = WIN_LAT // 2, WIN_LON // 2
    for (lat_half, lon_half), out_ref in zip(QUARTERS, out_refs):
        first_row, first_col = (1 - lat_half) * half_rows, (1 - lon_half) * half_cols
        pieces = []
        for ref in (field_ref, cot_ref):
            for row in range(half_rows):
                for col in range(half_cols):
                    pieces.append(ref[first_row + row, first_col + col].astype(f32))
        out_ref[...] = jnp.concatenate(pieces, axis=0).astype(bf16)


def one_hot(flags):
    return flags.astype(f32).astype(bf16)


def counted(shape, axis):
    return lax.broadcasted_iota(jnp.int32, shape, axis)


def cell_source(cell, stride):
    col, level, row = lax.div(cell, PLANE), lax.rem(lax.div(cell, WIN_LAT), LEV), lax.rem(cell, WIN_LAT)
    half_rows, half_cols = WIN_LAT // 2, WIN_LON // 2
    quarter = 2 * lax.div(row, half_rows) + lax.div(col, half_cols)
    place = lax.rem(row, half_rows) * half_cols + lax.rem(col, half_cols)
    return quarter * stride + place * LEV + lax.rem(level + LEV // 2, LEV)


def unpack_kernel(own_ref, lon_ref, lat_ref, diag_ref, out_ref):
    half_rows, half_cols = WIN_LAT // 2, WIN_LON // 2
    sources = ((own_ref, 0), (lon_ref, 0), (lat_ref, 0), (diag_ref, QUARTER))
    for (lat_half, lon_half), (ref, start) in zip(QUARTERS, sources):
        first_row, first_col = (1 - lat_half) * half_rows, (1 - lon_half) * half_cols
        cells = ref[...].astype(f32)[start : start + QUARTER]
        for row in range(half_rows):
            for col in range(half_cols):
                first = (row * half_cols + col) * LEV
                out_ref[first_row + row, first_col + col] = cells[first : first + LEV].astype(bf16)


def bias_kernel(
    table_src,
    regions_src,
    win_src,
    wout_src,
    gain_src,
    out_ref,
    win_t_ref,
    lanes_ref,
    rows_ref,
    eye_ref,
    place_ref,
    place_t_ref,
    win_ref,
    wout_ref,
    gain_ref,
    stage,
    full,
    table_ref,
    regions_ref,
    sems,
):
    sources = (table_src, regions_src, win_src, wout_src, gain_src)
    copies = fetch(sources, (table_ref, regions_ref, win_ref, wout_ref, gain_ref), sems)
    features = win_ref.shape[0]
    square = (features, features)
    eye = one_hot(counted(square, 0) == counted(square, 1))
    eye_ref[...] = eye
    source, lane = cell_source(counted((CELLS, 1), 0), 2 * QUARTER), counted((CELLS, 2 * CELLS), 1)
    place_ref[:CELLS] = one_hot(source == lane)
    place_ref[CELLS:] = one_hot(source + QUARTER == lane)
    place_t_ref[...] = one_hot(cell_source(counted((1, CELLS), 1), QUARTER) == counted((CELLS, CELLS), 0))
    lane = counted((1, WIDE), 1)
    target = jnp.where(lane < SPAN, lax.rem(lane, PLANE) * (SPAN // PLANE) + lax.div(lane, PLANE), -1)
    lanes_ref[...] = one_hot(target == counted((WIDE, WIDE), 0))
    sixteens = HEADS * 16
    row = counted((sixteens, 1), 0)
    target = jnp.where(lax.rem(row, 16) < PLANE, lax.rem(row, 16) * 16 + lax.div(row, 16), -1)
    rows_ref[...] = one_hot(target == counted((sixteens, sixteens), 1))

    stage[...] = jnp.zeros(stage.shape, f32)
    reach = SPAN // PLANE
    for copy in copies:
        copy.wait()
    for block in range(3):
        cols = slice(block * features, (block + 1) * features)
        win_t_ref[cols] = nt_dot(eye, win_ref[:, cols]).astype(bf16)
    table = table_ref[...].astype(f32)
    for first, plane_i, plane_j in segments():
        stage[16 * plane_j : 16 * plane_j + HEADS, reach * plane_i : reach * (plane_i + 1)] = table[
            :, first : first + reach
        ]
    moved = nn_dot(stage[...].astype(bf16), lanes_ref[...]).astype(bf16)
    rows = nn_dot(rows_ref[...], moved)

    region_rows = [regions_ref[row, level : level + 1, :] for level in range(LEV) for row in range(WIN_LAT)]
    region_grid = jnp.concatenate(region_rows, axis=0).astype(f32).astype(bf16)
    cell, lane = counted((CELLS, PLANE), 0), counted((CELLS, PLANE), 1)
    by_plane = nn_dot(one_hot(lax.rem(cell, PLANE) == lane), region_grid)
    region_col = jnp.sum(jnp.where(lax.div(cell, PLANE) == lane, by_plane, 0.0), axis=1, keepdims=True)
    across = counted((CELLS, CELLS), 0) == counted((CELLS, CELLS), 1)
    region_row = jnp.sum(jnp.where(across, region_col, 0.0), axis=0, keepdims=True)
    same = region_col == region_row

    for col in range(WIN_LON):
        shift = PLANE * (WIN_LON - 1 - col)
        moved = rows if shift == 0 else pltpu.roll(rows, WIDE - shift, 1)
        for head in range(HEADS):
            full[head, PLANE * col : PLANE * (col + 1), :] = moved[16 * head : 16 * head + PLANE, :CELLS]
    for head in range(HEADS):
        out_ref[head] = jnp.where(same, full[head], masked_score).astype(bf16)


def window_kernel(
    packet,
    place_id,
    own_ref,
    lon_ref,
    lat_ref,
    diag_ref,
    gain_ref,
    win_ref,
    win_t_ref,
    wout_ref,
    bias_ref,
    place_ref,
    eye_ref,
    keep_ref,
    send_ref,
    scores_ref,
    right,
    normalized_ref,
    inv_std_ref,
    cot_ref,
    left,
):
    features = win_ref.shape[0]
    head_dim = features // HEADS
    group_heads = LANES // head_dim
    score_scale = head_dim ** (-0.5)
    quarters = (own_ref, lon_ref, lat_ref, diag_ref)
    eye = eye_ref[...]
    stacked = jnp.concatenate([ref[...].astype(f32) for ref in quarters], axis=0).astype(bf16)
    placed = nn_dot(place_ref[...], stacked)
    field = placed[:CELLS]
    cot = placed[CELLS:].astype(bf16)
    cot_ref[...] = cot
    gain = gain_ref[...].reshape(1, features)

    centred = field - jnp.mean(field, axis=-1, keepdims=True)
    inv_std = lax.rsqrt(jnp.mean(centred * centred, axis=-1, keepdims=True) + norm_eps)
    normalized = centred * inv_std
    normalized_ref[...] = normalized
    inv_std_ref[...] = inv_std
    normed = (normalized * gain).astype(bf16)

    projected_t = nt_dot(win_t_ref[...], normed).astype(bf16)
    keys_values = nn_dot(normed, win_ref[:, features:]).astype(bf16)
    grad_att_t = nt_dot(wout_ref[...], cot).astype(bf16)
    left[0] = nt_dot(eye, normed).astype(bf16)
    right[3] = nt_dot(eye, cot).astype(bf16)

    def spread(head_rows, slot):
        parts = []
        if slot:
            parts.append(jnp.zeros((slot * head_dim, CELLS), bf16))
        parts.append(head_rows)
        if slot < group_heads - 1:
            parts.append(jnp.zeros(((group_heads - 1 - slot) * head_dim, CELLS), bf16))
        return jnp.concatenate(parts, axis=0)

    def rows_of(head):
        return slice(head * head_dim, (head + 1) * head_dim)

    def part(head, index):
        return projected_t[index * features + head * head_dim : index * features + (head + 1) * head_dim]

    def scores_of(head):
        group, slot = divmod(head, group_heads)
        keys = keys_values[:, group * LANES : (group + 1) * LANES]
        values = keys_values[:, features + group * LANES : features + (group + 1) * LANES]
        scores = nn_dot(keys, spread(part(head, 0), slot))
        return scores, nn_dot(values, spread(grad_att_t[rows_of(head)], slot))

    def softmax_of(head, scores, grad_probs):
        scores = scores * score_scale + bias_ref[head].astype(f32)
        grown = jnp.exp(scores - jnp.max(scores, axis=0, keepdims=True))
        probs = grown * (1.0 / jnp.sum(grown, axis=0, keepdims=True))
        weighted = probs * grad_probs
        grad_scores = weighted - probs * jnp.sum(weighted, axis=0, keepdims=True)
        return probs.astype(bf16), (grad_scores * score_scale).astype(bf16)

    def products_of(head, probs_low, scores_low):
        rows = rows_of(head)
        scores_ref[head] = scores_low
        left[1, rows] = nn_dot(part(head, 2), probs_low).astype(bf16)
        right[0, rows] = nn_dot(part(head, 1), scores_low).astype(bf16)
        right[1, rows] = nt_dot(part(head, 0), scores_low).astype(bf16)
        right[2, rows] = nt_dot(grad_att_t[rows], probs_low).astype(bf16)

    raw, soft = {}, {}
    for turn in range(HEADS + 2):
        if turn < HEADS:
            raw[turn] = scores_of(turn)
        if turn >= 2:
            products_of(turn - 2, *soft.pop(turn - 2))
        if 1 <= turn <= HEADS:
            soft[turn - 1] = softmax_of(turn - 1, *raw.pop(turn - 1))

    odd = lax.rem(place_id[1], 2)

    for out_ref, half in ((send_ref, 1 - odd), (keep_ref, odd)):
        low = nt_dot(left[0], right[2 * half])
        high = nt_dot(left[half], right[2 * half + 1])
        for owner in range(packet.lon_count):
            rows = slice(owner * packet.weight_rows, (owner + 1) * packet.weight_rows)
            pieces = [
                block[rows, tile * LANES : (tile + 1) * LANES] for block in (low, high) for tile in range(3)
            ]
            if packet.weight_size > packet.weight_used:
                pieces.append(jnp.zeros((packet.weight_size - packet.weight_used, LANES), f32))
            first = owner * packet.weight_size
            out_ref[first : first + packet.weight_size] = jnp.concatenate(pieces, axis=0).astype(bf16)


def field_kernel(
    win_ref,
    grad_projected_ref,
    normalized_ref,
    inv_std_ref,
    cot_ref,
    gain_ref,
    place_t_ref,
    eye_ref,
    back_own_ref,
    back_lon_ref,
    back_lat_ref,
    gain_out_ref,
):
    features = win_ref.shape[0]
    grad_shifted_t = sum(
        nn_dot(win_ref[:, block * features : (block + 1) * features], grad_projected_ref[block]) for block in range(3)
    ).astype(bf16)
    grad_normed = nt_dot(eye_ref[:CELLS, :CELLS], grad_shifted_t)
    normalized = normalized_ref[...]
    scaled = grad_normed * gain_ref[...].reshape(1, features)
    grad_field = cot_ref[...].astype(f32) + inv_std_ref[...] * (
        scaled
        - jnp.mean(scaled, axis=-1, keepdims=True)
        - normalized * jnp.mean(scaled * normalized, axis=-1, keepdims=True)
    )
    back = nn_dot(place_t_ref[...], grad_field.astype(bf16))
    quarters = [back[quarter * QUARTER : (quarter + 1) * QUARTER] for quarter in range(4)]
    back_own_ref[...] = quarters[0].astype(bf16)
    back_lon_ref[...] = jnp.concatenate([quarters[1], quarters[3]], axis=0).astype(bf16)
    back_lat_ref[...] = quarters[2].astype(bf16)
    gain_sum = jnp.sum(grad_normed * normalized, axis=0, keepdims=True)
    gain_rows = [gain_sum[:, tile * LANES : (tile + 1) * LANES] for tile in range(3)]
    gain_out_ref[...] = jnp.concatenate(gain_rows + [jnp.zeros((13, LANES), f32)], axis=0).astype(bf16)


def fold_kernel(packet, scores_ref, lanes_ref, rows_ref, out_ref, wide, table, flat):
    wide[...] = jnp.zeros(wide.shape, f32)
    table[...] = jnp.zeros(table.shape, f32)
    flat[...] = jnp.zeros(flat.shape, f32)
    for head in range(HEADS):
        wide[head % 2, :, :CELLS] = scores_ref[head].astype(f32)
        total = wide[head % 2, :PLANE, :]
        for col in range(1, WIN_LON):
            total = pltpu.roll(total, PLANE, 1) + wide[head % 2, PLANE * col : PLANE * (col + 1), :]
        table[16 * head : 16 * head + PLANE, :] = total
    moved = nn_dot(rows_ref[...], table[...].astype(bf16)).astype(bf16)
    moved = nt_dot(moved, lanes_ref[...])
    reach = SPAN // PLANE
    for first, plane_i, plane_j in segments():
        flat[:HEADS, first : first + reach] = moved[
            16 * plane_j : 16 * plane_j + HEADS, reach * plane_i : reach * (plane_i + 1)
        ]
    tiles = [flat[:HEADS, tile * LANES : (tile + 1) * LANES] for tile in range(packet.table_tiles)]
    tiles.append(jnp.zeros((packet.table_size - packet.table_rows, LANES), f32))
    out_ref[...] = jnp.concatenate(tiles, axis=0).astype(bf16)


def first_exchange_kernel(packet, place_id, keep_ref, recv_ref, table_ref, *out_refs):
    low = lax.rem(place_id[0], 4)
    size, quarter = packet.weight_size, packet.quarter
    for step, out_ref in enumerate(out_refs):
        digit = lax.bitwise_xor(low, step)
        for upper in range(packet.lon_count // 4):
            rows = pl.ds(pl.multiple_of((upper * 4 + digit) * size, 16), size)
            out_ref[upper * size : (upper + 1) * size] = keep_ref[rows] + recv_ref[rows]
        first = packet.lon_count // 4 * size
        out_ref[first:] = table_ref[pl.ds(pl.multiple_of(digit * quarter, 16), quarter)]


def summed(refs, rows):
    terms = [ref[rows] for ref in refs]
    while len(terms) > 1:
        terms = [left + right for left, right in zip(terms[::2], terms[1::2])]
    return terms[0]


def next_exchange_kernel(packet, shift, gains, place_id, *refs):
    gain_refs, held, out_refs = refs[:gains], refs[gains:-4], refs[-4:]
    size, quarter = packet.weight_size, packet.quarter
    digit = lax.rem(lax.shift_right_logical(place_id[0], shift), 4)
    groups = (out_refs[0].shape[0] - quarter - 16) // size
    rest = 4 * groups * size
    table = summed(held, slice(rest, rest + quarter))
    gain = summed(gain_refs, slice(0, 16)) if gains else summed(held, slice(rest + quarter, rest + quarter + 16))
    for step, out_ref in enumerate(out_refs):
        for upper in range(groups):
            owner = upper * 4 + lax.bitwise_xor(digit, step)
            out_ref[upper * size : (upper + 1) * size] = summed(held, pl.ds(pl.multiple_of(owner * size, 16), size))
        out_ref[groups * size : groups * size + quarter] = table
        out_ref[groups * size + quarter :] = gain


def last_sum_kernel(packet, a_ref, b_ref, c_ref, d_ref, weight_ref, table_ref):
    refs = (a_ref, b_ref, c_ref, d_ref)
    weight_ref[...] = summed(refs, slice(0, packet.weight_size))
    table_ref[...] = summed(refs, slice(packet.weight_size, packet.weight_size + packet.quarter + 16))


def finish_kernel(
    packet,
    table_scale,
    factor,
    place_id,
    weights_ref,
    other_weights_ref,
    a_ref,
    b_ref,
    c_ref,
    d_ref,
    grad_in_ref,
    grad_out_ref,
    grad_table_ref,
    grad_gain_ref,
    quarters,
):
    odd = lax.rem(place_id[1], 2) == 1
    own, other = weights_ref[...].astype(f32) * factor, other_weights_ref[...].astype(f32) * factor
    halves = (jnp.where(odd, other, own), jnp.where(odd, own, other))
    size = packet.weight_rows
    tiles = [half[tile * size : (tile + 1) * size] for half in halves for tile in range(6)]
    grad_in_ref[...] = jnp.concatenate(tiles[:9], axis=1).astype(bf16)
    grad_out_ref[...] = jnp.concatenate(tiles[9:], axis=1).astype(bf16)

    low = lax.rem(place_id[0], 4)
    parts = (a_ref, b_ref, c_ref, d_ref)
    for step, ref in enumerate(parts):
        quarters[lax.bitwise_xor(low, step)] = ref[: packet.quarter].astype(f32)
    total = quarters[...].reshape(packet.table_size, LANES)
    for tile in range(packet.table_tiles):
        first = tile * LANES
        width = min(LANES, grad_table_ref.shape[2] - first)
        block = total[HEADS * tile : HEADS * (tile + 1), :width] * table_scale
        for head in range(HEADS):
            grad_table_ref[head, :, first : first + width] = block[head : head + 1]
    gain = sum(ref[packet.quarter :].astype(f32) for ref in parts) * factor
    grad_gain_ref[...] = jnp.concatenate([gain[tile : tile + 1] for tile in range(3)], axis=1).reshape(
        grad_gain_ref.shape
    )


def whole(count):
    return [pl.BlockSpec(memory_space=pltpu.VMEM)] * count


scalars = pl.BlockSpec(memory_space=pltpu.SMEM)


def call(kernel, name, in_specs, outs, scratch=(), flops=0, moved=0):
    return pl.pallas_call(
        kernel,
        name=name,
        out_shape=outs,
        in_specs=in_specs,
        out_specs=jax.tree.map(lambda _: pl.BlockSpec(memory_space=pltpu.VMEM), outs),
        scratch_shapes=list(scratch),
        compiler_params=pltpu.CompilerParams(vmem_limit_bytes=20 * 1024 * 1024),
        cost_estimate=pl.CostEstimate(flops=flops, bytes_accessed=moved, transcendentals=0),
    )


def on_device(lon_count, lat_count, latent_field, cotangent, norm_gain, input_weight, output_weight, bias_table, regions):
    features = latent_field.shape[3]
    head_dim = features // HEADS
    packet = Packet(lon_count, features)
    place_id = jnp.stack([lax.axis_index("lon"), lax.axis_index("lat")]).astype(jnp.int32)

    def move(value, lon_step, lat_step):
        pairs = []
        for lon in range(lon_count):
            for lat in range(lat_count):
                target = ((lon + lon_step) % lon_count) * lat_count + (lat + lat_step) % lat_count
                pairs.append((lon * lat_count + lat, target))
        return lax.ppermute(value, ("lon", "lat"), pairs)

    def swap(value, axis, mask):
        count = lon_count if axis == "lon" else lat_count
        return lax.ppermute(value, axis, [(source, source ^ mask) for source in range(count)])

    struct = jax.ShapeDtypeStruct
    def in_hbm(*arrays):
        return [pltpu.with_memory_space_constraint(array, pltpu.HBM) for array in arrays]

    def space_for(array):
        return pltpu.VMEM(array.shape, array.dtype)

    hbm = pl.BlockSpec(memory_space=pltpu.HBM)
    field, cot = jnp.transpose(latent_field, (1, 2, 0, 3)), jnp.transpose(cotangent, (1, 2, 0, 3))
    own, to_lon, to_lat, to_diag = call(
        load_kernel,
        "load",
        [hbm] * 2,
        [struct((2 * QUARTER, features), bf16)] * 4,
        [space_for(field), space_for(cot), pltpu.SemaphoreType.DMA((2,))],
        moved=1 << 20,
    )(*in_hbm(field, cot))
    from_lon = move(to_lon, -1, 0)
    from_diag = move(to_diag, -1, -1)
    from_lat = move(to_lat, 0, -1)

    table, region_grid = bias_table[0], jnp.transpose(regions, (1, 0, 2))
    bias_full, input_weight_t, lane_moves, row_moves, eye, place, place_t, weight_in, weight_out, gain = call(
        bias_kernel,
        "expand_bias",
        [hbm] * 5,
        [
            struct((HEADS, CELLS, CELLS), bf16),
            struct((3 * features, features), bf16),
            struct((WIDE, WIDE), bf16),
            struct((HEADS * 16, HEADS * 16), bf16),
            struct((features, features), bf16),
            struct((2 * CELLS, 2 * CELLS), bf16),
            struct((CELLS, CELLS), bf16),
            struct(input_weight.shape, bf16),
            struct(output_weight.shape, bf16),
            struct(norm_gain.shape, f32),
        ],
        [
            pltpu.VMEM((HEADS * 16, WIDE), f32),
            pltpu.VMEM((HEADS, CELLS, CELLS), f32),
            space_for(table),
            space_for(region_grid),
            pltpu.SemaphoreType.DMA((5,)),
        ],
        moved=1 << 21,
    )(*in_hbm(table, region_grid, input_weight, output_weight, norm_gain))

    half_sum = struct((lon_count * packet.weight_size, LANES), bf16)
    results = call(
        functools.partial(window_kernel, packet),
        "window",
        [scalars] + whole(11),
        [
            half_sum,
            half_sum,
            struct((HEADS, CELLS, CELLS), bf16),
            struct((4, features, CELLS), bf16),
            struct((CELLS, features), f32),
            struct((CELLS, 1), f32),
            struct((CELLS, features), bf16),
        ],
        [pltpu.VMEM((2, features, CELLS), bf16)],
        flops=10**9,
        moved=5 << 20,
    )(
        place_id,
        own,
        from_lon,
        from_lat,
        from_diag,
        gain,
        weight_in,
        input_weight_t,
        weight_out,
        bias_full,
        place,
        eye,
    )
    keep, send, scores_low, *saved = results

    received = swap(send, "lat", 1)
    table_part = call(
        functools.partial(fold_kernel, packet),
        "fold_table",
        whole(3),
        struct((packet.table_size, LANES), bf16),
        [
            pltpu.VMEM((2, CELLS, WIDE), f32),
            pltpu.VMEM((HEADS * 16, WIDE), f32),
            pltpu.VMEM((16, packet.table_tiles * LANES), f32),
        ],
        moved=1 << 21,
    )(scores_low, lane_moves, row_moves)

    groups = lon_count // 4
    parts = call(
        functools.partial(first_exchange_kernel, packet),
        "add_lat",
        [scalars] + whole(3),
        [struct((groups * packet.weight_size + packet.quarter, LANES), bf16)] * 4,
        moved=2 << 20,
    )(place_id, keep, received, table_part)
    parts, saved = lax.optimization_barrier((parts, saved))

    def trade(parts, shift):
        return [swap(parts[step], "lon", step << shift) for step in (3, 2, 1)] + [parts[0]]

    held = trade(parts, 0)
    piece = struct((QUARTER, features), bf16)
    back_own, back_lon, back_lat, gain_part = call(
        field_kernel,
        "grad_field",
        whole(8),
        [piece, struct((2 * QUARTER, features), bf16), piece, struct((16, LANES), bf16)],
        flops=10**8,
        moved=5 << 20,
    )(weight_in, *saved, gain, place_t, eye)
    home_lat = move(back_lat, 0, 1)
    gain_other = swap(gain_part, "lat", 1)
    held, home_lat, gain_other = lax.optimization_barrier((held, home_lat, gain_other))
    gains = [gain_part, gain_other]
    home_lon = move(back_lon, 1, 0)
    home_diag = move(home_lon, 0, 1)
    for shift in range(2, lon_count.bit_length() - 1, 2):
        groups //= 4
        parts = call(
            functools.partial(next_exchange_kernel, packet, shift, len(gains)),
            "add_lon",
            [scalars] + whole(len(gains) + 4),
            [struct((groups * packet.weight_size + packet.quarter + 16, LANES), bf16)] * 4,
            moved=1 << 20,
        )(place_id, *gains, *held)
        gains = []
        held = trade(parts, shift)
    weight_sum, table_sum = call(
        functools.partial(last_sum_kernel, packet),
        "add_last",
        whole(4),
        [struct((packet.weight_size, LANES), bf16), struct((packet.quarter + 16, LANES), bf16)],
        moved=1 << 18,
    )(*held)
    table_parts = trade([table_sum] * 4, 0)[::-1]
    for bit in range(1, lat_count.bit_length() - 1):
        weight_sum = weight_sum + swap(weight_sum, "lat", 1 << bit)
    weight_other = swap(weight_sum, "lat", 1)

    cells_in_all = latent_field.shape[0] * latent_field.shape[1] * latent_field.shape[2]
    factor = 1.0 / math.sqrt(cells_in_all * lon_count * lat_count)
    grad_input_weight, grad_output_weight, grad_table, gain_sum = call(
        functools.partial(finish_kernel, packet, math.sqrt(head_dim), factor),
        "finish",
        [scalars] + whole(6),
        [
            struct((packet.weight_rows, 3 * features), bf16),
            struct((packet.weight_rows, features), bf16),
            struct((HEADS, 1, PLANE * SPAN), f32),
            struct((features,), f32),
        ],
        [pltpu.VMEM((4, packet.quarter, LANES), f32)],
        moved=1 << 19,
    )(place_id, weight_sum, weight_other, *table_parts)
    for bit in range(1, lat_count.bit_length() - 1):
        gain_sum = gain_sum + swap(gain_sum, "lat", 1 << bit)

    grad_field = call(
        unpack_kernel, "unpack_quarters", whole(4), struct((WIN_LAT, WIN_LON, LEV, features), bf16), moved=4 << 20
    )(back_own, home_lon, home_lat, home_diag)
    return (
        jnp.transpose(grad_field, (2, 0, 1, 3)),
        grad_input_weight,
        grad_output_weight,
        gain_sum,
        jnp.transpose(grad_table, (1, 0, 2)),
    )


def solution(mesh):
    in_specs = (
        P(None, "lat", "lon", None),
        P(None, "lat", "lon", None),
        P(),
        P(),
        P(),
        P("lat", None, None),
        P(None, "lat", "lon"),
    )
    out_specs = (
        P(None, "lat", "lon", None),
        P("lon", None),
        P("lon", None),
        P(),
        P("lat", None, None),
    )
    return jax.shard_map(
        functools.partial(on_device, mesh.shape["lon"], mesh.shape["lat"]),
        mesh=mesh,
        in_specs=in_specs,
        out_specs=out_specs,
        check_vma=False,
    )
```

```python
import functools
import math

import jax
import jax.numpy as jnp
from jax import lax
from jax.experimental import pallas as pl
from jax.experimental.pallas import tpu as pltpu
from jax.sharding import PartitionSpec as P

HEADS = 12
LEV = 2
WIN_LAT = 6
WIN_LON = 12
PLANE = LEV * WIN_LAT
CELLS = PLANE * WIN_LON
SPAN = (2 * WIN_LON - 1) * PLANE
WIDE = 384
LANES = 128
QUARTER = LEV * (WIN_LAT // 2) * (WIN_LON // 2)

norm_eps = 1e-05
masked_score = -1000000000.0
f32 = jnp.float32
bf16 = jnp.bfloat16

QUARTERS = ((0, 0), (0, 1), (1, 0), (1, 1))


def segments():
    reach = SPAN // PLANE
    first = 0
    for level_i in range(LEV):
        for level_j in range(LEV):
            for row_i in range(WIN_LAT):
                for row_j in range(WIN_LAT):
                    yield first, level_i * WIN_LAT + row_i, level_j * WIN_LAT + row_j
                    first += reach


def rounded_up(value, step):
    return -(-value // step) * step


class Packet:
    def __init__(self, lon_count, features):
        self.lon_count = lon_count
        self.weight_rows = features // lon_count
        self.weight_used = 6 * self.weight_rows
        self.weight_size = rounded_up(self.weight_used, 16)
        self.table_tiles = -(-PLANE * SPAN // LANES)
        self.table_rows = HEADS * self.table_tiles
        self.table_size = rounded_up(self.table_rows, 4 * 16)
        self.quarter = self.table_size // 4


def nt_dot(left, right):
    return lax.dot_general(left, right, (((1,), (1,)), ((), ())), preferred_element_type=f32)


def nn_dot(left, right):
    return jnp.dot(left, right, preferred_element_type=f32)


def fetch(sources, targets, sems):
    copies = [pltpu.make_async_copy(src, dst, sems.at[at]) for at, (src, dst) in enumerate(zip(sources, targets))]
    for copy in copies:
        copy.start()
    return copies


def load_kernel(field_src, cot_src, *refs):
    sources, out_refs, targets, (field_ref, cot_ref, sems) = refs[:3], refs[3:7], refs[7:10], refs[10:]
    copies = fetch((field_src, cot_src) + sources, (field_ref, cot_ref) + targets, sems)
    for copy in copies[:2]:
        copy.wait()
    half_rows, half_cols = WIN_LAT // 2, WIN_LON // 2
    for (lat_half, lon_half), out_ref in zip(QUARTERS, out_refs):
        first_row, first_col = (1 - lat_half) * half_rows, (1 - lon_half) * half_cols
        pieces = []
        for ref in (field_ref, cot_ref):
            for row in range(half_rows):
                for col in range(half_cols):
                    pieces.append(ref[first_row + row, first_col + col].astype(f32))
        out_ref[...] = jnp.concatenate(pieces, axis=0).astype(bf16)
    for copy in copies[2:]:
        copy.wait()


def one_hot(flags):
    return flags.astype(f32).astype(bf16)


def counted(shape, axis):
    return lax.broadcasted_iota(jnp.int32, shape, axis)


def cell_source(cell, stride):
    col, level, row = lax.div(cell, PLANE), lax.rem(lax.div(cell, WIN_LAT), LEV), lax.rem(cell, WIN_LAT)
    half_rows, half_cols = WIN_LAT // 2, WIN_LON // 2
    quarter = 2 * lax.div(row, half_rows) + lax.div(col, half_cols)
    place = lax.rem(row, half_rows) * half_cols + lax.rem(col, half_cols)
    return quarter * stride + place * LEV + lax.rem(level + LEV // 2, LEV)


def unpack_kernel(own_ref, lon_ref, lat_ref, diag_ref, out_ref):
    half_rows, half_cols = WIN_LAT // 2, WIN_LON // 2
    sources = ((own_ref, 0), (lon_ref, 0), (lat_ref, 0), (diag_ref, QUARTER))
    for (lat_half, lon_half), (ref, start) in zip(QUARTERS, sources):
        first_row, first_col = (1 - lat_half) * half_rows, (1 - lon_half) * half_cols
        cells = ref[...].astype(f32)[start : start + QUARTER]
        for row in range(half_rows):
            for col in range(half_cols):
                first = (row * half_cols + col) * LEV
                out_ref[first_row + row, first_col + col] = cells[first : first + LEV].astype(bf16)


def bias_kernel(
    table_ref,
    regions_ref,
    win_src,
    wout_src,
    out_ref,
    win_t_ref,
    lanes_ref,
    rows_ref,
    eye_ref,
    place_ref,
    place_t_ref,
    win_ref,
    wout_ref,
    stage,
    full,
    sems,
):
    copies = fetch((win_src, wout_src), (win_ref, wout_ref), sems)
    features = win_ref.shape[0]
    square = (features, features)
    eye = one_hot(counted(square, 0) == counted(square, 1))
    eye_ref[...] = eye
    source, lane = cell_source(counted((CELLS, 1), 0), 2 * QUARTER), counted((CELLS, 2 * CELLS), 1)
    place_ref[:CELLS] = one_hot(source == lane)
    place_ref[CELLS:] = one_hot(source + QUARTER == lane)
    place_t_ref[...] = one_hot(cell_source(counted((1, CELLS), 1), QUARTER) == counted((CELLS, CELLS), 0))
    lane = counted((1, WIDE), 1)
    target = jnp.where(lane < SPAN, lax.rem(lane, PLANE) * (SPAN // PLANE) + lax.div(lane, PLANE), -1)
    lanes_ref[...] = one_hot(target == counted((WIDE, WIDE), 0))
    sixteens = HEADS * 16
    row = counted((sixteens, 1), 0)
    target = jnp.where(lax.rem(row, 16) < PLANE, lax.rem(row, 16) * 16 + lax.div(row, 16), -1)
    rows_ref[...] = one_hot(target == counted((sixteens, sixteens), 1))

    stage[...] = jnp.zeros(stage.shape, f32)
    reach = SPAN // PLANE
    table = table_ref[...].astype(f32)
    for first, plane_i, plane_j in segments():
        stage[16 * plane_j : 16 * plane_j + HEADS, reach * plane_i : reach * (plane_i + 1)] = table[
            :, first : first + reach
        ]
    moved = nn_dot(stage[...].astype(bf16), lanes_ref[...]).astype(bf16)
    rows = nn_dot(rows_ref[...], moved)

    region_rows = [regions_ref[row, level : level + 1, :] for level in range(LEV) for row in range(WIN_LAT)]
    region_grid = jnp.concatenate(region_rows, axis=0).astype(f32).astype(bf16)
    cell, lane = counted((CELLS, PLANE), 0), counted((CELLS, PLANE), 1)
    by_plane = nn_dot(one_hot(lax.rem(cell, PLANE) == lane), region_grid)
    region_col = jnp.sum(jnp.where(lax.div(cell, PLANE) == lane, by_plane, 0.0), axis=1, keepdims=True)
    across = counted((CELLS, CELLS), 0) == counted((CELLS, CELLS), 1)
    region_row = jnp.sum(jnp.where(across, region_col, 0.0), axis=0, keepdims=True)
    same = region_col == region_row

    for col in range(WIN_LON):
        shift = PLANE * (WIN_LON - 1 - col)
        moved = rows if shift == 0 else pltpu.roll(rows, WIDE - shift, 1)
        for head in range(HEADS):
            full[head, PLANE * col : PLANE * (col + 1), :] = moved[16 * head : 16 * head + PLANE, :CELLS]
    for head in range(HEADS):
        out_ref[head] = jnp.where(same, full[head], masked_score).astype(bf16)
    for copy in copies:
        copy.wait()
    for block in range(3):
        cols = slice(block * features, (block + 1) * features)
        win_t_ref[cols] = nt_dot(eye, win_ref[:, cols]).astype(bf16)


def window_kernel(
    packet,
    own_ref,
    lon_ref,
    lat_ref,
    diag_ref,
    gain_ref,
    win_ref,
    win_t_ref,
    wout_ref,
    bias_ref,
    place_ref,
    eye_ref,
    keep_ref,
    send_ref,
    scores_ref,
    right,
    normalized_ref,
    inv_std_ref,
    cot_ref,
    left,
):
    features = win_ref.shape[0]
    head_dim = features // HEADS
    group_heads = LANES // head_dim
    score_scale = head_dim ** (-0.5)
    quarters = (own_ref, lon_ref, lat_ref, diag_ref)
    eye = eye_ref[...]
    stacked = jnp.concatenate([ref[...].astype(f32) for ref in quarters], axis=0).astype(bf16)
    placed = nn_dot(place_ref[...], stacked)
    field = placed[:CELLS]
    cot = placed[CELLS:].astype(bf16)
    cot_ref[...] = cot
    gain = gain_ref[...].reshape(1, features)

    centred = field - jnp.mean(field, axis=-1, keepdims=True)
    inv_std = lax.rsqrt(jnp.mean(centred * centred, axis=-1, keepdims=True) + norm_eps)
    normalized = centred * inv_std
    normalized_ref[...] = normalized
    inv_std_ref[...] = inv_std
    normed = (normalized * gain).astype(bf16)

    projected_t = nt_dot(win_t_ref[...], normed).astype(bf16)
    keys_values = nn_dot(normed, win_ref[:, features:]).astype(bf16)
    grad_att_t = nt_dot(wout_ref[...], cot).astype(bf16)
    left[0] = nt_dot(eye, normed).astype(bf16)
    right[3] = nt_dot(eye, cot).astype(bf16)

    def spread(head_rows, slot):
        parts = []
        if slot:
            parts.append(jnp.zeros((slot * head_dim, CELLS), bf16))
        parts.append(head_rows)
        if slot < group_heads - 1:
            parts.append(jnp.zeros(((group_heads - 1 - slot) * head_dim, CELLS), bf16))
        return jnp.concatenate(parts, axis=0)

    def rows_of(head):
        return slice(head * head_dim, (head + 1) * head_dim)

    def part(head, index):
        return projected_t[index * features + head * head_dim : index * features + (head + 1) * head_dim]

    def scores_of(head):
        group, slot = divmod(head, group_heads)
        keys = keys_values[:, group * LANES : (group + 1) * LANES]
        values = keys_values[:, features + group * LANES : features + (group + 1) * LANES]
        scores = nn_dot(keys, spread(part(head, 0), slot))
        return scores, nn_dot(values, spread(grad_att_t[rows_of(head)], slot))

    def softmax_of(head, scores, grad_probs):
        scores = scores * score_scale + bias_ref[head].astype(f32)
        grown = jnp.exp(scores - jnp.max(scores, axis=0, keepdims=True))
        probs = grown * (1.0 / jnp.sum(grown, axis=0, keepdims=True))
        weighted = probs * grad_probs
        grad_scores = weighted - probs * jnp.sum(weighted, axis=0, keepdims=True)
        return probs.astype(bf16), (grad_scores * score_scale).astype(bf16)

    def products_of(head, probs_low, scores_low):
        rows = rows_of(head)
        scores_ref[head] = scores_low
        left[1, rows] = nn_dot(part(head, 2), probs_low).astype(bf16)
        right[0, rows] = nn_dot(part(head, 1), scores_low).astype(bf16)
        right[1, rows] = nt_dot(part(head, 0), scores_low).astype(bf16)
        right[2, rows] = nt_dot(grad_att_t[rows], probs_low).astype(bf16)

    raw, soft = {}, {}
    for turn in range(HEADS + 2):
        if turn < HEADS:
            raw[turn] = scores_of(turn)
        if turn >= 2:
            products_of(turn - 2, *soft.pop(turn - 2))
        if 1 <= turn <= HEADS:
            soft[turn - 1] = softmax_of(turn - 1, *raw.pop(turn - 1))

    odd = lax.rem(lax.axis_index("lat"), 2)

    for out_ref, half in ((send_ref, 1 - odd), (keep_ref, odd)):
        low = nt_dot(left[0], right[2 * half])
        high = nt_dot(left[half], right[2 * half + 1])
        for owner in range(packet.lon_count):
            rows = slice(owner * packet.weight_rows, (owner + 1) * packet.weight_rows)
            pieces = [
                block[rows, tile * LANES : (tile + 1) * LANES] for block in (low, high) for tile in range(3)
            ]
            if packet.weight_size > packet.weight_used:
                pieces.append(jnp.zeros((packet.weight_size - packet.weight_used, LANES), f32))
            first = owner * packet.weight_size
            out_ref[first : first + packet.weight_size] = jnp.concatenate(pieces, axis=0).astype(bf16)


def field_kernel(
    win_ref,
    grad_projected_ref,
    normalized_ref,
    inv_std_ref,
    cot_ref,
    gain_ref,
    place_t_ref,
    eye_ref,
    back_own_ref,
    back_lon_ref,
    back_lat_ref,
    gain_out_ref,
):
    features = win_ref.shape[0]
    grad_shifted_t = sum(
        nn_dot(win_ref[:, block * features : (block + 1) * features], grad_projected_ref[block]) for block in range(3)
    ).astype(bf16)
    grad_normed = nt_dot(eye_ref[:CELLS, :CELLS], grad_shifted_t)
    normalized = normalized_ref[...]
    scaled = grad_normed * gain_ref[...].reshape(1, features)
    grad_field = cot_ref[...].astype(f32) + inv_std_ref[...] * (
        scaled
        - jnp.mean(scaled, axis=-1, keepdims=True)
        - normalized * jnp.mean(scaled * normalized, axis=-1, keepdims=True)
    )
    back = nn_dot(place_t_ref[...], grad_field.astype(bf16))
    quarters = [back[quarter * QUARTER : (quarter + 1) * QUARTER] for quarter in range(4)]
    back_own_ref[...] = quarters[0].astype(bf16)
    back_lon_ref[...] = jnp.concatenate([quarters[1], quarters[3]], axis=0).astype(bf16)
    back_lat_ref[...] = quarters[2].astype(bf16)
    gain_sum = jnp.sum(grad_normed * normalized, axis=0, keepdims=True)
    gain_rows = [gain_sum[:, tile * LANES : (tile + 1) * LANES] for tile in range(3)]
    gain_out_ref[...] = jnp.concatenate(gain_rows + [jnp.zeros((13, LANES), f32)], axis=0).astype(bf16)


def fold_kernel(packet, scores_ref, lanes_ref, rows_ref, out_ref, wide, table, flat):
    wide[...] = jnp.zeros(wide.shape, f32)
    table[...] = jnp.zeros(table.shape, f32)
    flat[...] = jnp.zeros(flat.shape, f32)
    for head in range(HEADS):
        wide[head % 2, :, :CELLS] = scores_ref[head].astype(f32)
        total = wide[head % 2, :PLANE, :]
        for col in range(1, WIN_LON):
            total = pltpu.roll(total, PLANE, 1) + wide[head % 2, PLANE * col : PLANE * (col + 1), :]
        table[16 * head : 16 * head + PLANE, :] = total
    moved = nn_dot(rows_ref[...], table[...].astype(bf16)).astype(bf16)
    moved = nt_dot(moved, lanes_ref[...])
    reach = SPAN // PLANE
    for first, plane_i, plane_j in segments():
        flat[:HEADS, first : first + reach] = moved[
            16 * plane_j : 16 * plane_j + HEADS, reach * plane_i : reach * (plane_i + 1)
        ]
    tiles = [flat[:HEADS, tile * LANES : (tile + 1) * LANES] for tile in range(packet.table_tiles)]
    tiles.append(jnp.zeros((packet.table_size - packet.table_rows, LANES), f32))
    out_ref[...] = jnp.concatenate(tiles, axis=0).astype(bf16)


def first_exchange_kernel(packet, keep_ref, recv_ref, table_ref, *out_refs):
    low = lax.rem(lax.axis_index("lon"), 4)
    size, quarter = packet.weight_size, packet.quarter
    for step, out_ref in enumerate(out_refs):
        digit = lax.bitwise_xor(low, step)
        for upper in range(packet.lon_count // 4):
            rows = pl.ds(pl.multiple_of((upper * 4 + digit) * size, 16), size)
            out_ref[upper * size : (upper + 1) * size] = keep_ref[rows] + recv_ref[rows]
        first = packet.lon_count // 4 * size
        out_ref[first:] = table_ref[pl.ds(pl.multiple_of(digit * quarter, 16), quarter)]


def summed(refs, rows):
    terms = [ref[rows] for ref in refs]
    while len(terms) > 1:
        terms = [left + right for left, right in zip(terms[::2], terms[1::2])]
    return terms[0]


def next_exchange_kernel(packet, shift, gains, *refs):
    gain_refs, held, out_refs = refs[:gains], refs[gains:-4], refs[-4:]
    size, quarter = packet.weight_size, packet.quarter
    digit = lax.rem(lax.shift_right_logical(lax.axis_index("lon"), shift), 4)
    groups = (out_refs[0].shape[0] - quarter - 16) // size
    rest = 4 * groups * size
    table = summed(held, slice(rest, rest + quarter))
    gain = summed(gain_refs, slice(0, 16)) if gains else summed(held, slice(rest + quarter, rest + quarter + 16))
    for step, out_ref in enumerate(out_refs):
        for upper in range(groups):
            owner = upper * 4 + lax.bitwise_xor(digit, step)
            out_ref[upper * size : (upper + 1) * size] = summed(held, pl.ds(pl.multiple_of(owner * size, 16), size))
        out_ref[groups * size : groups * size + quarter] = table
        out_ref[groups * size + quarter :] = gain


def last_sum_kernel(packet, a_ref, b_ref, c_ref, d_ref, weight_ref, table_ref):
    refs = (a_ref, b_ref, c_ref, d_ref)
    weight_ref[...] = summed(refs, slice(0, packet.weight_size))
    table_ref[...] = summed(refs, slice(packet.weight_size, packet.weight_size + packet.quarter + 16))


def finish_kernel(
    packet,
    table_scale,
    factor,
    weights_ref,
    other_weights_ref,
    a_ref,
    b_ref,
    c_ref,
    d_ref,
    grad_in_ref,
    grad_out_ref,
    grad_table_ref,
    grad_gain_ref,
    quarters,
):
    odd = lax.rem(lax.axis_index("lat"), 2) == 1
    own, other = weights_ref[...].astype(f32) * factor, other_weights_ref[...].astype(f32) * factor
    halves = (jnp.where(odd, other, own), jnp.where(odd, own, other))
    size = packet.weight_rows
    tiles = [half[tile * size : (tile + 1) * size] for half in halves for tile in range(6)]
    grad_in_ref[...] = jnp.concatenate(tiles[:9], axis=1).astype(bf16)
    grad_out_ref[...] = jnp.concatenate(tiles[9:], axis=1).astype(bf16)

    low = lax.rem(lax.axis_index("lon"), 4)
    parts = (a_ref, b_ref, c_ref, d_ref)
    for step, ref in enumerate(parts):
        quarters[lax.bitwise_xor(low, step)] = ref[: packet.quarter].astype(f32)
    total = quarters[...].reshape(packet.table_size, LANES)
    for tile in range(packet.table_tiles):
        first = tile * LANES
        width = min(LANES, grad_table_ref.shape[2] - first)
        block = total[HEADS * tile : HEADS * (tile + 1), :width] * table_scale
        for head in range(HEADS):
            grad_table_ref[head, :, first : first + width] = block[head : head + 1]
    gain = sum(ref[packet.quarter :].astype(f32) for ref in parts) * factor
    grad_gain_ref[...] = jnp.concatenate([gain[tile : tile + 1] for tile in range(3)], axis=1).reshape(
        grad_gain_ref.shape
    )


def whole(count):
    return [pl.BlockSpec(memory_space=pltpu.VMEM)] * count


def call(kernel, name, in_specs, outs, scratch=(), flops=0, moved=0):
    return pl.pallas_call(
        kernel,
        name=name,
        out_shape=outs,
        in_specs=in_specs,
        out_specs=jax.tree.map(lambda _: pl.BlockSpec(memory_space=pltpu.VMEM), outs),
        scratch_shapes=list(scratch),
        compiler_params=pltpu.CompilerParams(vmem_limit_bytes=20 * 1024 * 1024),
        cost_estimate=pl.CostEstimate(flops=flops, bytes_accessed=moved, transcendentals=0),
    )


def on_device(lon_count, lat_count, latent_field, cotangent, norm_gain, input_weight, output_weight, bias_table, regions):
    features = latent_field.shape[3]
    head_dim = features // HEADS
    packet = Packet(lon_count, features)

    def move(value, lon_step, lat_step):
        pairs = []
        for lon in range(lon_count):
            for lat in range(lat_count):
                target = ((lon + lon_step) % lon_count) * lat_count + (lat + lat_step) % lat_count
                pairs.append((lon * lat_count + lat, target))
        return lax.ppermute(value, ("lon", "lat"), pairs)

    def swap(value, axis, mask):
        count = lon_count if axis == "lon" else lat_count
        return lax.ppermute(value, axis, [(source, source ^ mask) for source in range(count)])

    struct = jax.ShapeDtypeStruct
    def in_hbm(*arrays):
        return [pltpu.with_memory_space_constraint(array, pltpu.HBM) for array in arrays]

    def space_for(array):
        return pltpu.VMEM(array.shape, array.dtype)

    hbm = pl.BlockSpec(memory_space=pltpu.HBM)
    field, cot = jnp.transpose(latent_field, (1, 2, 0, 3)), jnp.transpose(cotangent, (1, 2, 0, 3))
    small = (bias_table[0], jnp.transpose(regions, (1, 0, 2)), norm_gain)
    own, to_lon, to_lat, to_diag, table, region_grid, gain = call(
        load_kernel,
        "load",
        [hbm] * 5,
        [struct((2 * QUARTER, features), bf16)] * 4 + [struct(array.shape, array.dtype) for array in small],
        [space_for(field), space_for(cot), pltpu.SemaphoreType.DMA((5,))],
        moved=1 << 20,
    )(*in_hbm(field, cot, *small))
    from_lon = move(to_lon, -1, 0)
    from_diag = move(to_diag, -1, -1)
    from_lat = move(to_lat, 0, -1)

    bias_full, input_weight_t, lane_moves, row_moves, eye, place, place_t, weight_in, weight_out = call(
        bias_kernel,
        "expand_bias",
        whole(2) + [hbm] * 2,
        [
            struct((HEADS, CELLS, CELLS), bf16),
            struct((3 * features, features), bf16),
            struct((WIDE, WIDE), bf16),
            struct((HEADS * 16, HEADS * 16), bf16),
            struct((features, features), bf16),
            struct((2 * CELLS, 2 * CELLS), bf16),
            struct((CELLS, CELLS), bf16),
            struct(input_weight.shape, bf16),
            struct(output_weight.shape, bf16),
        ],
        [
            pltpu.VMEM((HEADS * 16, WIDE), f32),
            pltpu.VMEM((HEADS, CELLS, CELLS), f32),
            pltpu.SemaphoreType.DMA((2,)),
        ],
        moved=1 << 21,
    )(table, region_grid, *in_hbm(input_weight, output_weight))

    half_sum = struct((lon_count * packet.weight_size, LANES), bf16)
    results = call(
        functools.partial(window_kernel, packet),
        "window",
        whole(11),
        [
            half_sum,
            half_sum,
            struct((HEADS, CELLS, CELLS), bf16),
            struct((4, features, CELLS), bf16),
            struct((CELLS, features), f32),
            struct((CELLS, 1), f32),
            struct((CELLS, features), bf16),
        ],
        [pltpu.VMEM((2, features, CELLS), bf16)],
        flops=10**9,
        moved=5 << 20,
    )(
            own,
        from_lon,
        from_lat,
        from_diag,
        gain,
        weight_in,
        input_weight_t,
        weight_out,
        bias_full,
        place,
        eye,
    )
    keep, send, scores_low, *saved = results

    received = swap(send, "lat", 1)
    table_part = call(
        functools.partial(fold_kernel, packet),
        "fold_table",
        whole(3),
        struct((packet.table_size, LANES), bf16),
        [
            pltpu.VMEM((2, CELLS, WIDE), f32),
            pltpu.VMEM((HEADS * 16, WIDE), f32),
            pltpu.VMEM((16, packet.table_tiles * LANES), f32),
        ],
        moved=1 << 21,
    )(scores_low, lane_moves, row_moves)

    groups = lon_count // 4
    parts = call(
        functools.partial(first_exchange_kernel, packet),
        "add_lat",
        whole(3),
        [struct((groups * packet.weight_size + packet.quarter, LANES), bf16)] * 4,
        moved=2 << 20,
    )(keep, received, table_part)
    parts, saved = lax.optimization_barrier((parts, saved))

    def trade(parts, shift):
        return [swap(parts[step], "lon", step << shift) for step in (3, 2, 1)] + [parts[0]]

    held = trade(parts, 0)
    piece = struct((QUARTER, features), bf16)
    back_own, back_lon, back_lat, gain_part = call(
        field_kernel,
        "grad_field",
        whole(8),
        [piece, struct((2 * QUARTER, features), bf16), piece, struct((16, LANES), bf16)],
        flops=10**8,
        moved=5 << 20,
    )(weight_in, *saved, gain, place_t, eye)
    home_lat = move(back_lat, 0, 1)
    gain_other = swap(gain_part, "lat", 1)
    held, home_lat, gain_other = lax.optimization_barrier((held, home_lat, gain_other))
    gains = [gain_part, gain_other]
    home_lon = move(back_lon, 1, 0)
    home_diag = move(home_lon, 0, 1)
    for shift in range(2, lon_count.bit_length() - 1, 2):
        groups //= 4
        parts = call(
            functools.partial(next_exchange_kernel, packet, shift, len(gains)),
            "add_lon",
            whole(len(gains) + 4),
            [struct((groups * packet.weight_size + packet.quarter + 16, LANES), bf16)] * 4,
            moved=1 << 20,
        )(*gains, *held)
        gains = []
        held = trade(parts, shift)
    weight_sum, table_sum = call(
        functools.partial(last_sum_kernel, packet),
        "add_last",
        whole(4),
        [struct((packet.weight_size, LANES), bf16), struct((packet.quarter + 16, LANES), bf16)],
        moved=1 << 18,
    )(*held)
    table_parts = trade([table_sum] * 4, 0)[::-1]
    for bit in range(1, lat_count.bit_length() - 1):
        weight_sum = weight_sum + swap(weight_sum, "lat", 1 << bit)
    weight_other = swap(weight_sum, "lat", 1)

    cells_in_all = latent_field.shape[0] * latent_field.shape[1] * latent_field.shape[2]
    factor = 1.0 / math.sqrt(cells_in_all * lon_count * lat_count)
    grad_input_weight, grad_output_weight, grad_table, gain_sum = call(
        functools.partial(finish_kernel, packet, math.sqrt(head_dim), factor),
        "finish",
        whole(6),
        [
            struct((packet.weight_rows, 3 * features), bf16),
            struct((packet.weight_rows, features), bf16),
            struct((HEADS, 1, PLANE * SPAN), f32),
            struct((features,), f32),
        ],
        [pltpu.VMEM((4, packet.quarter, LANES), f32)],
        moved=1 << 19,
    )(weight_sum, weight_other, *table_parts)
    for bit in range(1, lat_count.bit_length() - 1):
        gain_sum = gain_sum + swap(gain_sum, "lat", 1 << bit)

    grad_field = call(
        unpack_kernel, "unpack_quarters", whole(4), struct((WIN_LAT, WIN_LON, LEV, features), bf16), moved=4 << 20
    )(back_own, home_lon, home_lat, home_diag)
    return (
        jnp.transpose(grad_field, (2, 0, 1, 3)),
        grad_input_weight,
        grad_output_weight,
        gain_sum,
        jnp.transpose(grad_table, (1, 0, 2)),
    )


def solution(mesh):
    in_specs = (
        P(None, "lat", "lon", None),
        P(None, "lat", "lon", None),
        P(),
        P(),
        P(),
        P("lat", None, None),
        P(None, "lat", "lon"),
    )
    out_specs = (
        P(None, "lat", "lon", None),
        P("lon", None),
        P("lon", None),
        P(),
        P("lat", None, None),
    )
    return jax.shard_map(
        functools.partial(on_device, mesh.shape["lon"], mesh.shape["lat"]),
        mesh=mesh,
        in_specs=in_specs,
        out_specs=out_specs,
        check_vma=False,
    )
```

```python
import functools
import math

import jax
import jax.numpy as jnp
from jax import lax
from jax.experimental import pallas as pl
from jax.experimental.pallas import tpu as pltpu
from jax.sharding import PartitionSpec as P

HEADS = 12
LEV = 2
WIN_LAT = 6
WIN_LON = 12
PLANE = LEV * WIN_LAT
CELLS = PLANE * WIN_LON
SPAN = (2 * WIN_LON - 1) * PLANE
WIDE = 384
LANES = 128
QUARTER = LEV * (WIN_LAT // 2) * (WIN_LON // 2)

norm_eps = 1e-05
masked_score = -1000000000.0
f32 = jnp.float32
bf16 = jnp.bfloat16

QUARTERS = ((0, 0), (0, 1), (1, 0), (1, 1))


def segments():
    reach = SPAN // PLANE
    first = 0
    for level_i in range(LEV):
        for level_j in range(LEV):
            for row_i in range(WIN_LAT):
                for row_j in range(WIN_LAT):
                    yield first, level_i * WIN_LAT + row_i, level_j * WIN_LAT + row_j
                    first += reach


def rounded_up(value, step):
    return -(-value // step) * step


class Packet:
    def __init__(self, lon_count, features):
        self.lon_count = lon_count
        self.weight_rows = features // lon_count
        self.weight_used = 6 * self.weight_rows
        self.weight_size = rounded_up(self.weight_used, 16)
        self.table_tiles = -(-PLANE * SPAN // LANES)
        self.table_rows = HEADS * self.table_tiles
        self.table_size = rounded_up(self.table_rows, 4 * 16)
        self.quarter = self.table_size // 4


def nt_dot(left, right):
    return lax.dot_general(left, right, (((1,), (1,)), ((), ())), preferred_element_type=f32)


def nn_dot(left, right):
    return jnp.dot(left, right, preferred_element_type=f32)


def fetch(sources, targets, sems):
    copies = [pltpu.make_async_copy(src, dst, sems.at[at]) for at, (src, dst) in enumerate(zip(sources, targets))]
    for copy in copies:
        copy.start()
    return copies


class Route:
    def __init__(self, lon_count, lat_count):
        self.lon_count, self.lat_count = lon_count, lat_count
        self.middle = lon_count // 2
        middle, last = self.middle, lon_count - 1
        self.near = [(lon + 1, lon) for lon in range(middle)] + [(0, middle)]
        self.near += [(lon - 1, lon) for lon in range(middle + 2, lon_count)]
        self.joint = [(middle, middle + 1), (last, middle)]

    def move(self, value, pairs, lat_step):
        count = self.lat_count
        pairs = [(src * count + lat, dst * count + (lat + lat_step) % count) for src, dst in pairs for lat in range(count)]
        return lax.ppermute(value, ("lon", "lat"), pairs)

    def west(self, own, near, joint, joint_at):
        lon = lax.axis_index("lon")
        by_joint = (lon == self.middle) | (lon == joint_at)
        return jnp.where(lon < self.middle, own, jnp.where(by_joint, joint, near))

    def east(self, own, near):
        return jnp.where(lax.axis_index("lon") <= self.middle, near, own)


SAME = 80


def load_kernel(route, field_src, cot_src, *refs):
    sources, out_refs, (table_ref, gain_ref) = refs[:3], refs[3:9], refs[9:11]
    field_ref, cot_ref, regions_ref, sems = refs[11:]
    copies = fetch((field_src, cot_src) + sources, (field_ref, cot_ref, regions_ref, table_ref, gain_ref), sems)
    for copy in copies[:3]:
        copy.wait()
    half_rows, half_cols = WIN_LAT // 2, WIN_LON // 2
    features = field_ref.shape[3]
    lon = lax.axis_index("lon")
    own_col = jnp.where(lon < route.middle, half_cols, 0)
    far_col = jnp.where(lon <= route.middle, 0, half_cols)
    ids = [regions_ref[row, level : level + 1, :].astype(f32) for level in range(LEV) for row in range(WIN_LAT)]
    ids.append(jnp.zeros((1, features - CELLS), f32))
    tail = jnp.concatenate([jnp.concatenate(ids, axis=1), jnp.zeros((SAME - 2 * QUARTER - 1, features), f32)], axis=0)
    wanted = (
        (half_rows, own_col),
        (half_rows, far_col),
        (0, far_col),
        (0, own_col),
        (half_rows, half_cols),
        (0, half_cols),
    )
    for (first_row, first_col), out_ref in zip(wanted, out_refs):
        pieces = [
            ref[first_row + row, first_col + col].astype(f32)
            for ref in (field_ref, cot_ref)
            for row in range(half_rows)
            for col in range(half_cols)
        ]
        if out_ref.shape[0] == SAME:
            pieces.append(tail)
        out_ref[...] = jnp.concatenate(pieces, axis=0).astype(bf16)
    for copy in copies[3:]:
        copy.wait()


def one_hot(flags):
    return flags.astype(f32).astype(bf16)


def counted(shape, axis):
    return lax.broadcasted_iota(jnp.int32, shape, axis)


def cell_source(cell, stride):
    col, level, row = lax.div(cell, PLANE), lax.rem(lax.div(cell, WIN_LAT), LEV), lax.rem(cell, WIN_LAT)
    half_rows, half_cols = WIN_LAT // 2, WIN_LON // 2
    quarter = 2 * lax.div(row, half_rows) + lax.div(col, half_cols)
    place = lax.rem(row, half_rows) * half_cols + lax.rem(col, half_cols)
    return quarter * stride + place * LEV + lax.rem(level + LEV // 2, LEV)


def unpack_kernel(route, own_ref, near_ref, joint_ref, lat_ref, near_diag_ref, joint_diag_ref, out_ref):
    half_rows, half_cols = WIN_LAT // 2, WIN_LON // 2
    last = route.lon_count - 1
    own, lat = own_ref[...].astype(f32), lat_ref[...].astype(f32)
    near, joint = near_ref[...].astype(f32)[:QUARTER], joint_ref[...].astype(f32)[:QUARTER]
    near_diag = near_diag_ref[...].astype(f32)[QUARTER:]
    joint_diag = joint_diag_ref[...].astype(f32)[QUARTER:]
    quarters = (
        route.west(own, near, joint, last),
        route.east(own, near),
        route.west(lat, near_diag, joint_diag, last),
        route.east(lat, near_diag),
    )
    for (lat_half, lon_half), cells in zip(QUARTERS, quarters):
        first_row, first_col = (1 - lat_half) * half_rows, (1 - lon_half) * half_cols
        for row in range(half_rows):
            for col in range(half_cols):
                first = (row * half_cols + col) * LEV
                out_ref[first_row + row, first_col + col] = cells[first : first + LEV].astype(bf16)


def bias_kernel(
    table_ref,
    win_src,
    wout_src,
    out_ref,
    win_t_ref,
    lanes_ref,
    rows_ref,
    eye_ref,
    place_ref,
    place_t_ref,
    win_ref,
    wout_ref,
    stage,
    full,
    sems,
):
    copies = fetch((win_src, wout_src), (win_ref, wout_ref), sems)
    features = win_ref.shape[0]
    square = (features, features)
    eye = one_hot(counted(square, 0) == counted(square, 1))
    eye_ref[...] = eye
    source, lane = cell_source(counted((CELLS, 1), 0), 2 * QUARTER), counted((CELLS, 2 * CELLS), 1)
    place_ref[:CELLS] = one_hot(source == lane)
    place_ref[CELLS:] = one_hot(source + QUARTER == lane)
    place_t_ref[...] = one_hot(cell_source(counted((1, CELLS), 1), QUARTER) == counted((CELLS, CELLS), 0))
    lane = counted((1, WIDE), 1)
    target = jnp.where(lane < SPAN, lax.rem(lane, PLANE) * (SPAN // PLANE) + lax.div(lane, PLANE), -1)
    lanes_ref[...] = one_hot(target == counted((WIDE, WIDE), 0))
    sixteens = HEADS * 16
    row = counted((sixteens, 1), 0)
    target = jnp.where(lax.rem(row, 16) < PLANE, lax.rem(row, 16) * 16 + lax.div(row, 16), -1)
    rows_ref[...] = one_hot(target == counted((sixteens, sixteens), 1))

    stage[...] = jnp.zeros(stage.shape, f32)
    reach = SPAN // PLANE
    table = table_ref[...].astype(f32)
    for first, plane_i, plane_j in segments():
        stage[16 * plane_j : 16 * plane_j + HEADS, reach * plane_i : reach * (plane_i + 1)] = table[
            :, first : first + reach
        ]
    moved = nn_dot(stage[...].astype(bf16), lanes_ref[...]).astype(bf16)
    rows = nn_dot(rows_ref[...], moved)

    for col in range(WIN_LON):
        shift = PLANE * (WIN_LON - 1 - col)
        moved = rows if shift == 0 else pltpu.roll(rows, WIDE - shift, 1)
        for head in range(HEADS):
            full[head, PLANE * col : PLANE * (col + 1), :] = moved[16 * head : 16 * head + PLANE, :CELLS]
    for head in range(HEADS):
        out_ref[head] = full[head].astype(bf16)
    for copy in copies:
        copy.wait()
    for block in range(3):
        cols = slice(block * features, (block + 1) * features)
        win_t_ref[cols] = nt_dot(eye, win_ref[:, cols]).astype(bf16)


def window_kernel(
    route,
    packet,
    own_ref,
    near_ref,
    near_diag_ref,
    lat_ref,
    joint_ref,
    joint_diag_ref,
    gain_ref,
    win_ref,
    win_t_ref,
    wout_ref,
    bias_ref,
    place_ref,
    eye_ref,
    keep_ref,
    send_ref,
    scores_ref,
    right,
    normalized_ref,
    inv_std_ref,
    cot_ref,
    left,
):
    features = win_ref.shape[0]
    head_dim = features // HEADS
    group_heads = LANES // head_dim
    score_scale = head_dim ** (-0.5)
    eye = eye_ref[...]
    messages = (own_ref, near_ref, near_diag_ref, lat_ref, joint_ref, joint_diag_ref)
    own, near, near_diag, lat, joint, joint_diag = [ref[...].astype(f32) for ref in messages]
    west = route.west(own, near, joint, route.middle + 1)
    quarters = [
        west[: 2 * QUARTER],
        route.east(own, near)[: 2 * QUARTER],
        route.west(lat, near_diag, joint_diag, route.middle + 1),
        route.east(lat, near_diag),
    ]
    stacked = jnp.concatenate(quarters, axis=0).astype(bf16)
    cell, lane = counted((CELLS, CELLS), 0), counted((CELLS, CELLS), 1)
    source = lax.rem(cell, PLANE) * WIN_LON + lax.div(cell, PLANE)
    ids = west[2 * QUARTER : 2 * QUARTER + 1, :CELLS]
    region_col = jnp.sum(jnp.where(source == lane, ids, 0.0), axis=1, keepdims=True)
    region_row = jnp.sum(jnp.where(cell == lane, region_col, 0.0), axis=0, keepdims=True)
    same = region_col == region_row
    placed = nn_dot(place_ref[...], stacked)
    field = placed[:CELLS]
    cot = placed[CELLS:].astype(bf16)
    cot_ref[...] = cot
    gain = gain_ref[...].reshape(1, features)

    centred = field - jnp.mean(field, axis=-1, keepdims=True)
    inv_std = lax.rsqrt(jnp.mean(centred * centred, axis=-1, keepdims=True) + norm_eps)
    normalized = centred * inv_std
    normalized_ref[...] = normalized
    inv_std_ref[...] = inv_std
    normed = (normalized * gain).astype(bf16)

    projected_t = nt_dot(win_t_ref[...], normed).astype(bf16)
    keys_values = nn_dot(normed, win_ref[:, features:]).astype(bf16)
    grad_att_t = nt_dot(wout_ref[...], cot).astype(bf16)
    left[0] = nt_dot(eye, normed).astype(bf16)
    right[3] = nt_dot(eye, cot).astype(bf16)

    def spread(head_rows, slot):
        parts = []
        if slot:
            parts.append(jnp.zeros((slot * head_dim, CELLS), bf16))
        parts.append(head_rows)
        if slot < group_heads - 1:
            parts.append(jnp.zeros(((group_heads - 1 - slot) * head_dim, CELLS), bf16))
        return jnp.concatenate(parts, axis=0)

    def rows_of(head):
        return slice(head * head_dim, (head + 1) * head_dim)

    def part(head, index):
        return projected_t[index * features + head * head_dim : index * features + (head + 1) * head_dim]

    def scores_of(head):
        group, slot = divmod(head, group_heads)
        keys = keys_values[:, group * LANES : (group + 1) * LANES]
        values = keys_values[:, features + group * LANES : features + (group + 1) * LANES]
        scores = nn_dot(keys, spread(part(head, 0), slot))
        return scores, nn_dot(values, spread(grad_att_t[rows_of(head)], slot))

    def softmax_of(head, scores, grad_probs):
        scores = jnp.where(same, scores * score_scale + bias_ref[head].astype(f32), masked_score)
        grown = jnp.exp(scores - jnp.max(scores, axis=0, keepdims=True))
        probs = grown * (1.0 / jnp.sum(grown, axis=0, keepdims=True))
        weighted = probs * grad_probs
        grad_scores = weighted - probs * jnp.sum(weighted, axis=0, keepdims=True)
        return probs.astype(bf16), (grad_scores * score_scale).astype(bf16)

    def products_of(head, probs_low, scores_low):
        rows = rows_of(head)
        scores_ref[head] = scores_low
        left[1, rows] = nn_dot(part(head, 2), probs_low).astype(bf16)
        right[0, rows] = nn_dot(part(head, 1), scores_low).astype(bf16)
        right[1, rows] = nt_dot(part(head, 0), scores_low).astype(bf16)
        right[2, rows] = nt_dot(grad_att_t[rows], probs_low).astype(bf16)

    raw, soft = {}, {}
    for turn in range(HEADS + 2):
        if turn < HEADS:
            raw[turn] = scores_of(turn)
        if turn >= 2:
            products_of(turn - 2, *soft.pop(turn - 2))
        if 1 <= turn <= HEADS:
            soft[turn - 1] = softmax_of(turn - 1, *raw.pop(turn - 1))

    odd = lax.rem(lax.axis_index("lat"), 2)

    for out_ref, half in ((send_ref, 1 - odd), (keep_ref, odd)):
        low = nt_dot(left[0], right[2 * half])
        high = nt_dot(left[half], right[2 * half + 1])
        for owner in range(packet.lon_count):
            rows = slice(owner * packet.weight_rows, (owner + 1) * packet.weight_rows)
            pieces = [
                block[rows, tile * LANES : (tile + 1) * LANES] for block in (low, high) for tile in range(3)
            ]
            if packet.weight_size > packet.weight_used:
                pieces.append(jnp.zeros((packet.weight_size - packet.weight_used, LANES), f32))
            first = owner * packet.weight_size
            out_ref[first : first + packet.weight_size] = jnp.concatenate(pieces, axis=0).astype(bf16)


def field_kernel(
    route,
    win_ref,
    grad_projected_ref,
    normalized_ref,
    inv_std_ref,
    cot_ref,
    gain_ref,
    place_t_ref,
    eye_ref,
    back_own_ref,
    back_near_ref,
    back_joint_ref,
    back_lat_ref,
    gain_out_ref,
):
    features = win_ref.shape[0]
    grad_shifted_t = sum(
        nn_dot(win_ref[:, block * features : (block + 1) * features], grad_projected_ref[block]) for block in range(3)
    ).astype(bf16)
    grad_normed = nt_dot(eye_ref[:CELLS, :CELLS], grad_shifted_t)
    normalized = normalized_ref[...]
    scaled = grad_normed * gain_ref[...].reshape(1, features)
    grad_field = cot_ref[...].astype(f32) + inv_std_ref[...] * (
        scaled
        - jnp.mean(scaled, axis=-1, keepdims=True)
        - normalized * jnp.mean(scaled * normalized, axis=-1, keepdims=True)
    )
    back = nn_dot(place_t_ref[...], grad_field.astype(bf16))
    quarters = [back[quarter * QUARTER : (quarter + 1) * QUARTER] for quarter in range(4)]
    west, east = jnp.concatenate(quarters[::2], axis=0), jnp.concatenate(quarters[1::2], axis=0)
    lon = lax.axis_index("lon")
    kept = jnp.where(lon < route.middle, west, east)
    back_own_ref[...] = kept[:QUARTER].astype(bf16)
    back_near_ref[...] = jnp.where(lon <= route.middle, east, west).astype(bf16)
    back_joint_ref[...] = west.astype(bf16)
    back_lat_ref[...] = kept[QUARTER:].astype(bf16)
    gain_sum = jnp.sum(grad_normed * normalized, axis=0, keepdims=True)
    gain_rows = [gain_sum[:, tile * LANES : (tile + 1) * LANES] for tile in range(3)]
    gain_out_ref[...] = jnp.concatenate(gain_rows + [jnp.zeros((13, LANES), f32)], axis=0).astype(bf16)


def fold_kernel(packet, scores_ref, lanes_ref, rows_ref, out_ref, wide, table, flat):
    wide[...] = jnp.zeros(wide.shape, f32)
    table[...] = jnp.zeros(table.shape, f32)
    flat[...] = jnp.zeros(flat.shape, f32)
    for head in range(HEADS):
        wide[head % 2, :, :CELLS] = scores_ref[head].astype(f32)
        total = wide[head % 2, :PLANE, :]
        for col in range(1, WIN_LON):
            total = pltpu.roll(total, PLANE, 1) + wide[head % 2, PLANE * col : PLANE * (col + 1), :]
        table[16 * head : 16 * head + PLANE, :] = total
    moved = nn_dot(rows_ref[...], table[...].astype(bf16)).astype(bf16)
    moved = nt_dot(moved, lanes_ref[...])
    reach = SPAN // PLANE
    for first, plane_i, plane_j in segments():
        flat[:HEADS, first : first + reach] = moved[
            16 * plane_j : 16 * plane_j + HEADS, reach * plane_i : reach * (plane_i + 1)
        ]
    tiles = [flat[:HEADS, tile * LANES : (tile + 1) * LANES] for tile in range(packet.table_tiles)]
    tiles.append(jnp.zeros((packet.table_size - packet.table_rows, LANES), f32))
    out_ref[...] = jnp.concatenate(tiles, axis=0).astype(bf16)


def first_exchange_kernel(packet, keep_ref, recv_ref, table_ref, *out_refs):
    low = lax.rem(lax.axis_index("lon"), 4)
    size, quarter = packet.weight_size, packet.quarter
    for step, out_ref in enumerate(out_refs):
        digit = lax.bitwise_xor(low, step)
        for upper in range(packet.lon_count // 4):
            rows = pl.ds(pl.multiple_of((upper * 4 + digit) * size, 16), size)
            out_ref[upper * size : (upper + 1) * size] = keep_ref[rows] + recv_ref[rows]
        first = packet.lon_count // 4 * size
        out_ref[first:] = table_ref[pl.ds(pl.multiple_of(digit * quarter, 16), quarter)]


def summed(refs, rows):
    terms = [ref[rows] for ref in refs]
    while len(terms) > 1:
        terms = [left + right for left, right in zip(terms[::2], terms[1::2])]
    return terms[0]


def next_exchange_kernel(packet, shift, gains, *refs):
    gain_refs, held, out_refs = refs[:gains], refs[gains:-4], refs[-4:]
    size, quarter = packet.weight_size, packet.quarter
    digit = lax.rem(lax.shift_right_logical(lax.axis_index("lon"), shift), 4)
    groups = (out_refs[0].shape[0] - quarter - 16) // size
    rest = 4 * groups * size
    table = summed(held, slice(rest, rest + quarter))
    gain = summed(gain_refs, slice(0, 16)) if gains else summed(held, slice(rest + quarter, rest + quarter + 16))
    for step, out_ref in enumerate(out_refs):
        for upper in range(groups):
            owner = upper * 4 + lax.bitwise_xor(digit, step)
            out_ref[upper * size : (upper + 1) * size] = summed(held, pl.ds(pl.multiple_of(owner * size, 16), size))
        out_ref[groups * size : groups * size + quarter] = table
        out_ref[groups * size + quarter :] = gain


def last_sum_kernel(packet, a_ref, b_ref, c_ref, d_ref, weight_ref, table_ref):
    refs = (a_ref, b_ref, c_ref, d_ref)
    weight_ref[...] = summed(refs, slice(0, packet.weight_size))
    table_ref[...] = summed(refs, slice(packet.weight_size, packet.weight_size + packet.quarter + 16))


def finish_kernel(
    packet,
    table_scale,
    factor,
    weights_ref,
    other_weights_ref,
    a_ref,
    b_ref,
    c_ref,
    d_ref,
    grad_in_ref,
    grad_out_ref,
    grad_table_ref,
    grad_gain_ref,
    quarters,
):
    odd = lax.rem(lax.axis_index("lat"), 2) == 1
    own, other = weights_ref[...].astype(f32) * factor, other_weights_ref[...].astype(f32) * factor
    halves = (jnp.where(odd, other, own), jnp.where(odd, own, other))
    size = packet.weight_rows
    tiles = [half[tile * size : (tile + 1) * size] for half in halves for tile in range(6)]
    grad_in_ref[...] = jnp.concatenate(tiles[:9], axis=1).astype(bf16)
    grad_out_ref[...] = jnp.concatenate(tiles[9:], axis=1).astype(bf16)

    low = lax.rem(lax.axis_index("lon"), 4)
    parts = (a_ref, b_ref, c_ref, d_ref)
    for step, ref in enumerate(parts):
        quarters[lax.bitwise_xor(low, step)] = ref[: packet.quarter].astype(f32)
    total = quarters[...].reshape(packet.table_size, LANES)
    for tile in range(packet.table_tiles):
        first = tile * LANES
        width = min(LANES, grad_table_ref.shape[2] - first)
        block = total[HEADS * tile : HEADS * (tile + 1), :width] * table_scale
        for head in range(HEADS):
            grad_table_ref[head, :, first : first + width] = block[head : head + 1]
    gain = sum(ref[packet.quarter :].astype(f32) for ref in parts) * factor
    grad_gain_ref[...] = jnp.concatenate([gain[tile : tile + 1] for tile in range(3)], axis=1).reshape(
        grad_gain_ref.shape
    )


def whole(count):
    return [pl.BlockSpec(memory_space=pltpu.VMEM)] * count


def call(kernel, name, in_specs, outs, scratch=(), flops=0, moved=0):
    return pl.pallas_call(
        kernel,
        name=name,
        out_shape=outs,
        in_specs=in_specs,
        out_specs=jax.tree.map(lambda _: pl.BlockSpec(memory_space=pltpu.VMEM), outs),
        scratch_shapes=list(scratch),
        compiler_params=pltpu.CompilerParams(vmem_limit_bytes=20 * 1024 * 1024),
        cost_estimate=pl.CostEstimate(flops=flops, bytes_accessed=moved, transcendentals=0),
    )


def on_device(lon_count, lat_count, latent_field, cotangent, norm_gain, input_weight, output_weight, bias_table, regions):
    features = latent_field.shape[3]
    head_dim = features // HEADS
    packet = Packet(lon_count, features)

    route = Route(lon_count, lat_count)
    everyone = [(lon, lon) for lon in range(lon_count)]
    backward, joint_backward = [[(dst, src) for src, dst in pairs] for pairs in (route.near, route.joint)]

    def swap(value, axis, mask):
        count = lon_count if axis == "lon" else lat_count
        return lax.ppermute(value, axis, [(source, source ^ mask) for source in range(count)])

    struct = jax.ShapeDtypeStruct
    def in_hbm(*arrays):
        return [pltpu.with_memory_space_constraint(array, pltpu.HBM) for array in arrays]

    def space_for(array):
        return pltpu.VMEM(array.shape, array.dtype)

    hbm = pl.BlockSpec(memory_space=pltpu.HBM)
    field, cot = jnp.transpose(latent_field, (1, 2, 0, 3)), jnp.transpose(cotangent, (1, 2, 0, 3))
    small = (jnp.transpose(regions, (1, 0, 2)), bias_table[0], norm_gain)
    same, others = struct((SAME, features), bf16), struct((2 * QUARTER, features), bf16)
    own, far, far_others, to_lat, west, west_others, table, gain = call(
        functools.partial(load_kernel, route),
        "load",
        [hbm] * 5,
        [same, same, others, others, same, others] + [struct(array.shape, array.dtype) for array in small[1:]],
        [space_for(field), space_for(cot), space_for(small[0]), pltpu.SemaphoreType.DMA((5,))],
        moved=1 << 20,
    )(*in_hbm(field, cot, *small))
    from_near = route.move(far, route.near, 0)
    from_near_diag = route.move(far_others, route.near, -1)
    from_joint = route.move(west, route.joint, 0)
    from_joint_diag = route.move(west_others, route.joint, -1)
    from_lat = route.move(to_lat, everyone, -1)

    bias_full, input_weight_t, lane_moves, row_moves, eye, place, place_t, weight_in, weight_out = call(
        bias_kernel,
        "expand_bias",
        whole(1) + [hbm] * 2,
        [
            struct((HEADS, CELLS, CELLS), bf16),
            struct((3 * features, features), bf16),
            struct((WIDE, WIDE), bf16),
            struct((HEADS * 16, HEADS * 16), bf16),
            struct((features, features), bf16),
            struct((2 * CELLS, 2 * CELLS), bf16),
            struct((CELLS, CELLS), bf16),
            struct(input_weight.shape, bf16),
            struct(output_weight.shape, bf16),
        ],
        [
            pltpu.VMEM((HEADS * 16, WIDE), f32),
            pltpu.VMEM((HEADS, CELLS, CELLS), f32),
            pltpu.SemaphoreType.DMA((2,)),
        ],
        moved=1 << 21,
    )(table, *in_hbm(input_weight, output_weight))

    half_sum = struct((lon_count * packet.weight_size, LANES), bf16)
    results = call(
        functools.partial(window_kernel, route, packet),
        "window",
        whole(13),
        [
            half_sum,
            half_sum,
            struct((HEADS, CELLS, CELLS), bf16),
            struct((4, features, CELLS), bf16),
            struct((CELLS, features), f32),
            struct((CELLS, 1), f32),
            struct((CELLS, features), bf16),
        ],
        [pltpu.VMEM((2, features, CELLS), bf16)],
        flops=10**9,
        moved=5 << 20,
    )(
            own,
        from_near,
        from_near_diag,
        from_lat,
        from_joint,
        from_joint_diag,
        gain,
        weight_in,
        input_weight_t,
        weight_out,
        bias_full,
        place,
        eye,
    )
    keep, send, scores_low, *saved = results

    received = swap(send, "lat", 1)
    table_part = call(
        functools.partial(fold_kernel, packet),
        "fold_table",
        whole(3),
        struct((packet.table_size, LANES), bf16),
        [
            pltpu.VMEM((2, CELLS, WIDE), f32),
            pltpu.VMEM((HEADS * 16, WIDE), f32),
            pltpu.VMEM((16, packet.table_tiles * LANES), f32),
        ],
        moved=1 << 21,
    )(scores_low, lane_moves, row_moves)

    groups = lon_count // 4
    parts = call(
        functools.partial(first_exchange_kernel, packet),
        "add_lat",
        whole(3),
        [struct((groups * packet.weight_size + packet.quarter, LANES), bf16)] * 4,
        moved=2 << 20,
    )(keep, received, table_part)
    parts, saved = lax.optimization_barrier((parts, saved))

    def trade(parts, shift):
        return [swap(parts[step], "lon", step << shift) for step in (3, 2, 1)] + [parts[0]]

    held = trade(parts, 0)
    piece = struct((QUARTER, features), bf16)
    back_own, back_near, back_joint, back_lat, gain_part = call(
        functools.partial(field_kernel, route),
        "grad_field",
        whole(8),
        [piece, others, others, piece, struct((16, LANES), bf16)],
        flops=10**8,
        moved=5 << 20,
    )(weight_in, *saved, gain, place_t, eye)
    home_lat = route.move(back_lat, everyone, 1)
    gain_other = swap(gain_part, "lat", 1)
    held, home_lat, gain_other = lax.optimization_barrier((held, home_lat, gain_other))
    gains = [gain_part, gain_other]
    home_near = route.move(back_near, backward, 0)
    home_joint = route.move(back_joint, joint_backward, 0)
    home_near_diag = route.move(home_near, everyone, 1)
    home_joint_diag = route.move(home_joint, everyone, 1)
    for shift in range(2, lon_count.bit_length() - 1, 2):
        groups //= 4
        parts = call(
            functools.partial(next_exchange_kernel, packet, shift, len(gains)),
            "add_lon",
            whole(len(gains) + 4),
            [struct((groups * packet.weight_size + packet.quarter + 16, LANES), bf16)] * 4,
            moved=1 << 20,
        )(*gains, *held)
        gains = []
        held = trade(parts, shift)
    weight_sum, table_sum = call(
        functools.partial(last_sum_kernel, packet),
        "add_last",
        whole(4),
        [struct((packet.weight_size, LANES), bf16), struct((packet.quarter + 16, LANES), bf16)],
        moved=1 << 18,
    )(*held)
    table_parts = trade([table_sum] * 4, 0)[::-1]
    for bit in range(1, lat_count.bit_length() - 1):
        weight_sum = weight_sum + swap(weight_sum, "lat", 1 << bit)
    weight_other = swap(weight_sum, "lat", 1)

    cells_in_all = latent_field.shape[0] * latent_field.shape[1] * latent_field.shape[2]
    factor = 1.0 / math.sqrt(cells_in_all * lon_count * lat_count)
    grad_input_weight, grad_output_weight, grad_table, gain_sum = call(
        functools.partial(finish_kernel, packet, math.sqrt(head_dim), factor),
        "finish",
        whole(6),
        [
            struct((packet.weight_rows, 3 * features), bf16),
            struct((packet.weight_rows, features), bf16),
            struct((HEADS, 1, PLANE * SPAN), f32),
            struct((features,), f32),
        ],
        [pltpu.VMEM((4, packet.quarter, LANES), f32)],
        moved=1 << 19,
    )(weight_sum, weight_other, *table_parts)
    for bit in range(1, lat_count.bit_length() - 1):
        gain_sum = gain_sum + swap(gain_sum, "lat", 1 << bit)

    grad_field = call(
        functools.partial(unpack_kernel, route),
        "unpack_quarters",
        whole(6),
        struct((WIN_LAT, WIN_LON, LEV, features), bf16),
        moved=4 << 20,
    )(back_own, home_near, home_joint, home_lat, home_near_diag, home_joint_diag)
    return (
        jnp.transpose(grad_field, (2, 0, 1, 3)),
        grad_input_weight,
        grad_output_weight,
        gain_sum,
        jnp.transpose(grad_table, (1, 0, 2)),
    )


def solution(mesh):
    in_specs = (
        P(None, "lat", "lon", None),
        P(None, "lat", "lon", None),
        P(),
        P(),
        P(),
        P("lat", None, None),
        P(None, "lat", "lon"),
    )
    out_specs = (
        P(None, "lat", "lon", None),
        P("lon", None),
        P("lon", None),
        P(),
        P("lat", None, None),
    )
    return jax.shard_map(
        functools.partial(on_device, mesh.shape["lon"], mesh.shape["lat"]),
        mesh=mesh,
        in_specs=in_specs,
        out_specs=out_specs,
        check_vma=False,
    )
```

```python
import functools
import math

import jax
import jax.numpy as jnp
from jax import lax
from jax.experimental import pallas as pl
from jax.experimental.pallas import tpu as pltpu
from jax.sharding import PartitionSpec as P

HEADS = 12
LEV = 2
WIN_LAT = 6
WIN_LON = 12
PLANE = LEV * WIN_LAT
CELLS = PLANE * WIN_LON
SPAN = (2 * WIN_LON - 1) * PLANE
WIDE = 384
LANES = 128
QUARTER = LEV * (WIN_LAT // 2) * (WIN_LON // 2)

norm_eps = 1e-05
masked_score = -1000000000.0
f32 = jnp.float32
bf16 = jnp.bfloat16

QUARTERS = ((0, 0), (0, 1), (1, 0), (1, 1))


def segments():
    reach = SPAN // PLANE
    first = 0
    for level_i in range(LEV):
        for level_j in range(LEV):
            for row_i in range(WIN_LAT):
                for row_j in range(WIN_LAT):
                    yield first, level_i * WIN_LAT + row_i, level_j * WIN_LAT + row_j
                    first += reach


def rounded_up(value, step):
    return -(-value // step) * step


class Packet:
    def __init__(self, lon_count, features):
        self.lon_count = lon_count
        self.weight_rows = features // lon_count
        self.weight_used = 6 * self.weight_rows
        self.weight_size = rounded_up(self.weight_used, 16)
        self.table_tiles = -(-PLANE * SPAN // LANES)
        self.table_rows = HEADS * self.table_tiles
        self.table_size = rounded_up(self.table_rows, 4 * 16)
        self.quarter = self.table_size // 4


def nt_dot(left, right):
    return lax.dot_general(left, right, (((1,), (1,)), ((), ())), preferred_element_type=f32)


def nn_dot(left, right):
    return jnp.dot(left, right, preferred_element_type=f32)


def fetch(sources, targets, sems):
    copies = [pltpu.make_async_copy(src, dst, sems.at[at]) for at, (src, dst) in enumerate(zip(sources, targets))]
    for copy in copies:
        copy.start()
    return copies


SAME = 80


def load_kernel(field_src, cot_src, *refs):
    sources, out_refs, (table_ref, gain_ref) = refs[:3], refs[3:7], refs[7:9]
    field_ref, cot_ref, regions_ref, sems = refs[9:]
    copies = fetch((field_src, cot_src) + sources, (field_ref, cot_ref, regions_ref, table_ref, gain_ref), sems)
    for copy in copies[:3]:
        copy.wait()
    half_rows, half_cols = WIN_LAT // 2, WIN_LON // 2
    features = field_ref.shape[3]
    ids = [regions_ref[row, level : level + 1, :].astype(f32) for level in range(LEV) for row in range(WIN_LAT)]
    ids.append(jnp.zeros((1, features - CELLS), f32))
    tail = jnp.concatenate([jnp.concatenate(ids, axis=1), jnp.zeros((SAME - 2 * QUARTER - 1, features), f32)], axis=0)
    wanted = ((half_rows, 0), (half_rows, half_cols), (0, half_cols), (0, 0))
    for (first_row, first_col), out_ref in zip(wanted, out_refs):
        pieces = [
            ref[first_row + row, first_col + col].astype(f32)
            for ref in (field_ref, cot_ref)
            for row in range(half_rows)
            for col in range(half_cols)
        ]
        if out_ref.shape[0] == SAME:
            pieces.append(tail)
        out_ref[...] = jnp.concatenate(pieces, axis=0).astype(bf16)
    for copy in copies[3:]:
        copy.wait()


def one_hot(flags):
    return flags.astype(f32).astype(bf16)


def counted(shape, axis):
    return lax.broadcasted_iota(jnp.int32, shape, axis)


def cell_source(cell, stride):
    col, level, row = lax.div(cell, PLANE), lax.rem(lax.div(cell, WIN_LAT), LEV), lax.rem(cell, WIN_LAT)
    half_rows, half_cols = WIN_LAT // 2, WIN_LON // 2
    quarter = 2 * lax.div(row, half_rows) + lax.div(col, half_cols)
    place = lax.rem(row, half_rows) * half_cols + lax.rem(col, half_cols)
    return quarter * stride + place * LEV + lax.rem(level + LEV // 2, LEV)


def unpack_kernel(own_ref, near_ref, lat_ref, near_diag_ref, out_ref):
    half_rows, half_cols = WIN_LAT // 2, WIN_LON // 2
    quarters = (
        near_ref[...].astype(f32)[:QUARTER],
        own_ref[...].astype(f32),
        near_diag_ref[...].astype(f32)[QUARTER:],
        lat_ref[...].astype(f32),
    )
    for (lat_half, lon_half), cells in zip(QUARTERS, quarters):
        first_row, first_col = (1 - lat_half) * half_rows, (1 - lon_half) * half_cols
        for row in range(half_rows):
            for col in range(half_cols):
                first = (row * half_cols + col) * LEV
                out_ref[first_row + row, first_col + col] = cells[first : first + LEV].astype(bf16)


def bias_kernel(
    table_ref,
    win_src,
    wout_src,
    out_ref,
    win_t_ref,
    lanes_ref,
    rows_ref,
    eye_ref,
    place_ref,
    place_t_ref,
    win_ref,
    wout_ref,
    stage,
    full,
    sems,
):
    copies = fetch((win_src, wout_src), (win_ref, wout_ref), sems)
    features = win_ref.shape[0]
    square = (features, features)
    eye = one_hot(counted(square, 0) == counted(square, 1))
    eye_ref[...] = eye
    source, lane = cell_source(counted((CELLS, 1), 0), 2 * QUARTER), counted((CELLS, 2 * CELLS), 1)
    place_ref[:CELLS] = one_hot(source == lane)
    place_ref[CELLS:] = one_hot(source + QUARTER == lane)
    place_t_ref[...] = one_hot(cell_source(counted((1, CELLS), 1), QUARTER) == counted((CELLS, CELLS), 0))
    lane = counted((1, WIDE), 1)
    target = jnp.where(lane < SPAN, lax.rem(lane, PLANE) * (SPAN // PLANE) + lax.div(lane, PLANE), -1)
    lanes_ref[...] = one_hot(target == counted((WIDE, WIDE), 0))
    sixteens = HEADS * 16
    row = counted((sixteens, 1), 0)
    target = jnp.where(lax.rem(row, 16) < PLANE, lax.rem(row, 16) * 16 + lax.div(row, 16), -1)
    rows_ref[...] = one_hot(target == counted((sixteens, sixteens), 1))

    stage[...] = jnp.zeros(stage.shape, f32)
    reach = SPAN // PLANE
    table = table_ref[...].astype(f32)
    for first, plane_i, plane_j in segments():
        stage[16 * plane_j : 16 * plane_j + HEADS, reach * plane_i : reach * (plane_i + 1)] = table[
            :, first : first + reach
        ]
    moved = nn_dot(stage[...].astype(bf16), lanes_ref[...]).astype(bf16)
    rows = nn_dot(rows_ref[...], moved)

    for col in range(WIN_LON):
        shift = PLANE * (WIN_LON - 1 - col)
        moved = rows if shift == 0 else pltpu.roll(rows, WIDE - shift, 1)
        for head in range(HEADS):
            full[head, PLANE * col : PLANE * (col + 1), :] = moved[16 * head : 16 * head + PLANE, :CELLS]
    for head in range(HEADS):
        out_ref[head] = full[head].astype(bf16)
    for copy in copies:
        copy.wait()
    win_t_ref[...] = nt_dot(eye, win_ref[:, :features]).astype(bf16)


def window_kernel(
    packet,
    own_ref,
    near_ref,
    near_diag_ref,
    lat_ref,
    gain_ref,
    win_ref,
    win_t_ref,
    wout_ref,
    bias_ref,
    place_ref,
    keep_ref,
    send_ref,
    scores_ref,
    right,
    normalized_ref,
    inv_std_ref,
    cot_ref,
    left,
):
    features = win_ref.shape[0]
    head_dim = features // HEADS
    group_heads = LANES // head_dim
    score_scale = head_dim ** (-0.5)
    near = near_ref[...].astype(f32)
    west, east = [near[: 2 * QUARTER], near_diag_ref[...].astype(f32)], [own_ref[...].astype(f32), lat_ref[...].astype(f32)]
    stacked = jnp.concatenate([west[0], east[0], west[1], east[1]], axis=0).astype(bf16)
    cell, lane = counted((CELLS, CELLS), 0), counted((CELLS, CELLS), 1)
    source = lax.rem(cell, PLANE) * WIN_LON + lax.div(cell, PLANE)
    ids = near[2 * QUARTER : 2 * QUARTER + 1, :CELLS]
    region_col = jnp.sum(jnp.where(source == lane, ids, 0.0), axis=1, keepdims=True)
    region_row = jnp.sum(jnp.where(cell == lane, region_col, 0.0), axis=0, keepdims=True)
    same = region_col == region_row
    placed = nn_dot(place_ref[...], stacked)
    field = placed[:CELLS]
    cot = placed[CELLS:].astype(bf16)
    cot_ref[...] = cot
    gain = gain_ref[...].reshape(1, features)

    centred = field - jnp.mean(field, axis=-1, keepdims=True)
    inv_std = lax.rsqrt(jnp.mean(centred * centred, axis=-1, keepdims=True) + norm_eps)
    normalized = centred * inv_std
    normalized_ref[...] = normalized
    inv_std_ref[...] = inv_std
    normed = (normalized * gain).astype(bf16)

    query_t = nt_dot(win_t_ref[...], normed).astype(bf16)
    wide_keys_values = nn_dot(normed, win_ref[:, features:])
    keys_values = wide_keys_values.astype(bf16)
    grad_att_t = nt_dot(wout_ref[...], cot).astype(bf16)
    key_value_t = jnp.transpose(wide_keys_values).astype(bf16)
    left[0] = jnp.transpose(normed.astype(f32)).astype(bf16)
    right[3] = jnp.transpose(placed[CELLS:]).astype(bf16)

    def spread(head_rows, slot):
        parts = []
        if slot:
            parts.append(jnp.zeros((slot * head_dim, CELLS), bf16))
        parts.append(head_rows)
        if slot < group_heads - 1:
            parts.append(jnp.zeros(((group_heads - 1 - slot) * head_dim, CELLS), bf16))
        return jnp.concatenate(parts, axis=0)

    def rows_of(head):
        return slice(head * head_dim, (head + 1) * head_dim)

    def part(head, index):
        if index == 0:
            return query_t[rows_of(head)]
        first = (index - 1) * features + head * head_dim
        return key_value_t[first : first + head_dim]

    def scores_of(head):
        group, slot = divmod(head, group_heads)
        keys = keys_values[:, group * LANES : (group + 1) * LANES]
        values = keys_values[:, features + group * LANES : features + (group + 1) * LANES]
        scores = nn_dot(keys, spread(part(head, 0), slot))
        return scores, nn_dot(values, spread(grad_att_t[rows_of(head)], slot))

    def softmax_of(head, scores, grad_probs):
        scores = jnp.where(same, scores * score_scale + bias_ref[head].astype(f32), masked_score)
        grown = jnp.exp(scores - jnp.max(scores, axis=0, keepdims=True))
        probs = grown * (1.0 / jnp.sum(grown, axis=0, keepdims=True))
        weighted = probs * grad_probs
        grad_scores = weighted - probs * jnp.sum(weighted, axis=0, keepdims=True)
        return probs.astype(bf16), (grad_scores * score_scale).astype(bf16)

    def products_of(head, probs_low, scores_low):
        rows = rows_of(head)
        scores_ref[head] = scores_low
        left[1, rows] = nn_dot(part(head, 2), probs_low).astype(bf16)
        right[0, rows] = nn_dot(part(head, 1), scores_low).astype(bf16)
        right[1, rows] = nt_dot(part(head, 0), scores_low).astype(bf16)
        right[2, rows] = nt_dot(grad_att_t[rows], probs_low).astype(bf16)

    raw, soft = {}, {}
    for turn in range(HEADS + 2):
        if turn < HEADS:
            raw[turn] = scores_of(turn)
        if turn >= 2:
            products_of(turn - 2, *soft.pop(turn - 2))
        if 1 <= turn <= HEADS:
            soft[turn - 1] = softmax_of(turn - 1, *raw.pop(turn - 1))

    odd = lax.rem(lax.axis_index("lat"), 2)

    for out_ref, half in ((send_ref, 1 - odd), (keep_ref, odd)):
        low = nt_dot(left[0], right[2 * half])
        high = nt_dot(left[half], right[2 * half + 1])
        for owner in range(packet.lon_count):
            rows = slice(owner * packet.weight_rows, (owner + 1) * packet.weight_rows)
            pieces = [
                block[rows, tile * LANES : (tile + 1) * LANES] for block in (low, high) for tile in range(3)
            ]
            if packet.weight_size > packet.weight_used:
                pieces.append(jnp.zeros((packet.weight_size - packet.weight_used, LANES), f32))
            first = owner * packet.weight_size
            out_ref[first : first + packet.weight_size] = jnp.concatenate(pieces, axis=0).astype(bf16)


def field_kernel(
    win_ref,
    grad_projected_ref,
    normalized_ref,
    inv_std_ref,
    cot_ref,
    gain_ref,
    place_t_ref,
    eye_ref,
    back_own_ref,
    back_near_ref,
    back_lat_ref,
    gain_out_ref,
):
    features = win_ref.shape[0]
    grad_shifted_t = sum(
        nn_dot(win_ref[:, block * features : (block + 1) * features], grad_projected_ref[block]) for block in range(3)
    ).astype(bf16)
    grad_normed = nt_dot(eye_ref[:CELLS, :CELLS], grad_shifted_t)
    normalized = normalized_ref[...]
    scaled = grad_normed * gain_ref[...].reshape(1, features)
    grad_field = cot_ref[...].astype(f32) + inv_std_ref[...] * (
        scaled
        - jnp.mean(scaled, axis=-1, keepdims=True)
        - normalized * jnp.mean(scaled * normalized, axis=-1, keepdims=True)
    )
    back = nn_dot(place_t_ref[...], grad_field.astype(bf16))
    quarters = [back[quarter * QUARTER : (quarter + 1) * QUARTER] for quarter in range(4)]
    back_own_ref[...] = quarters[1].astype(bf16)
    back_near_ref[...] = jnp.concatenate(quarters[::2], axis=0).astype(bf16)
    back_lat_ref[...] = quarters[3].astype(bf16)
    gain_sum = jnp.sum(grad_normed * normalized, axis=0, keepdims=True)
    gain_rows = [gain_sum[:, tile * LANES : (tile + 1) * LANES] for tile in range(3)]
    gain_out_ref[...] = jnp.concatenate(gain_rows + [jnp.zeros((13, LANES), f32)], axis=0).astype(bf16)


def fold_kernel(packet, scores_ref, lanes_ref, rows_ref, out_ref, wide, table, flat):
    wide[...] = jnp.zeros(wide.shape, f32)
    table[...] = jnp.zeros(table.shape, f32)
    flat[...] = jnp.zeros(flat.shape, f32)
    for head in range(HEADS):
        wide[head % 2, :, :CELLS] = scores_ref[head].astype(f32)
        total = wide[head % 2, :PLANE, :]
        for col in range(1, WIN_LON):
            total = pltpu.roll(total, PLANE, 1) + wide[head % 2, PLANE * col : PLANE * (col + 1), :]
        table[16 * head : 16 * head + PLANE, :] = total
    moved = nn_dot(rows_ref[...], table[...].astype(bf16)).astype(bf16)
    moved = nt_dot(moved, lanes_ref[...])
    reach = SPAN // PLANE
    for first, plane_i, plane_j in segments():
        flat[:HEADS, first : first + reach] = moved[
            16 * plane_j : 16 * plane_j + HEADS, reach * plane_i : reach * (plane_i + 1)
        ]
    tiles = [flat[:HEADS, tile * LANES : (tile + 1) * LANES] for tile in range(packet.table_tiles)]
    tiles.append(jnp.zeros((packet.table_size - packet.table_rows, LANES), f32))
    out_ref[...] = jnp.concatenate(tiles, axis=0).astype(bf16)


def first_exchange_kernel(packet, keep_ref, recv_ref, table_ref, *out_refs):
    low = lax.rem(lax.axis_index("lon"), 4)
    size, quarter = packet.weight_size, packet.quarter
    for step, out_ref in enumerate(out_refs):
        digit = lax.bitwise_xor(low, step)
        for upper in range(packet.lon_count // 4):
            rows = pl.ds(pl.multiple_of((upper * 4 + digit) * size, 16), size)
            out_ref[upper * size : (upper + 1) * size] = keep_ref[rows] + recv_ref[rows]
        first = packet.lon_count // 4 * size
        out_ref[first:] = table_ref[pl.ds(pl.multiple_of(digit * quarter, 16), quarter)]


def summed(refs, rows):
    terms = [ref[rows] for ref in refs]
    while len(terms) > 1:
        terms = [left + right for left, right in zip(terms[::2], terms[1::2])]
    return terms[0]


def next_exchange_kernel(packet, shift, gains, *refs):
    gain_refs, held, out_refs = refs[:gains], refs[gains:-4], refs[-4:]
    size, quarter = packet.weight_size, packet.quarter
    digit = lax.rem(lax.shift_right_logical(lax.axis_index("lon"), shift), 4)
    groups = (out_refs[0].shape[0] - quarter - 16) // size
    rest = 4 * groups * size
    table = summed(held, slice(rest, rest + quarter))
    gain = summed(gain_refs, slice(0, 16)) if gains else summed(held, slice(rest + quarter, rest + quarter + 16))
    for step, out_ref in enumerate(out_refs):
        for upper in range(groups):
            owner = upper * 4 + lax.bitwise_xor(digit, step)
            out_ref[upper * size : (upper + 1) * size] = summed(held, pl.ds(pl.multiple_of(owner * size, 16), size))
        out_ref[groups * size : groups * size + quarter] = table
        out_ref[groups * size + quarter :] = gain


def last_sum_kernel(packet, a_ref, b_ref, c_ref, d_ref, weight_ref, table_ref):
    refs = (a_ref, b_ref, c_ref, d_ref)
    weight_ref[...] = summed(refs, slice(0, packet.weight_size))
    table_ref[...] = summed(refs, slice(packet.weight_size, packet.weight_size + packet.quarter + 16))


def finish_kernel(
    packet,
    table_scale,
    factor,
    weights_ref,
    other_weights_ref,
    a_ref,
    b_ref,
    c_ref,
    d_ref,
    grad_in_ref,
    grad_out_ref,
    grad_table_ref,
    grad_gain_ref,
    quarters,
):
    odd = lax.rem(lax.axis_index("lat"), 2) == 1
    own, other = weights_ref[...].astype(f32) * factor, other_weights_ref[...].astype(f32) * factor
    halves = (jnp.where(odd, other, own), jnp.where(odd, own, other))
    size = packet.weight_rows
    tiles = [half[tile * size : (tile + 1) * size] for half in halves for tile in range(6)]
    grad_in_ref[...] = jnp.concatenate(tiles[:9], axis=1).astype(bf16)
    grad_out_ref[...] = jnp.concatenate(tiles[9:], axis=1).astype(bf16)

    low = lax.rem(lax.axis_index("lon"), 4)
    parts = (a_ref, b_ref, c_ref, d_ref)
    for step, ref in enumerate(parts):
        quarters[lax.bitwise_xor(low, step)] = ref[: packet.quarter].astype(f32)
    total = quarters[...].reshape(packet.table_size, LANES)
    for tile in range(packet.table_tiles):
        first = tile * LANES
        width = min(LANES, grad_table_ref.shape[2] - first)
        block = total[HEADS * tile : HEADS * (tile + 1), :width] * table_scale
        for head in range(HEADS):
            grad_table_ref[head, :, first : first + width] = block[head : head + 1]
    gain = sum(ref[packet.quarter :].astype(f32) for ref in parts) * factor
    grad_gain_ref[...] = jnp.concatenate([gain[tile : tile + 1] for tile in range(3)], axis=1).reshape(
        grad_gain_ref.shape
    )


def whole(count):
    return [pl.BlockSpec(memory_space=pltpu.VMEM)] * count


def call(kernel, name, in_specs, outs, scratch=(), flops=0, moved=0):
    return pl.pallas_call(
        kernel,
        name=name,
        out_shape=outs,
        in_specs=in_specs,
        out_specs=jax.tree.map(lambda _: pl.BlockSpec(memory_space=pltpu.VMEM), outs),
        scratch_shapes=list(scratch),
        compiler_params=pltpu.CompilerParams(vmem_limit_bytes=20 * 1024 * 1024),
        cost_estimate=pl.CostEstimate(flops=flops, bytes_accessed=moved, transcendentals=0),
    )


def on_device(lon_count, lat_count, latent_field, cotangent, norm_gain, input_weight, output_weight, bias_table, regions):
    features = latent_field.shape[3]
    head_dim = features // HEADS
    packet = Packet(lon_count, features)

    def move(value, lon_step, lat_step):
        pairs = []
        for lon in range(lon_count):
            for lat in range(lat_count):
                target = ((lon + lon_step) % lon_count) * lat_count + (lat + lat_step) % lat_count
                pairs.append((lon * lat_count + lat, target))
        return lax.ppermute(value, ("lon", "lat"), pairs)

    def swap(value, axis, mask):
        count = lon_count if axis == "lon" else lat_count
        return lax.ppermute(value, axis, [(source, source ^ mask) for source in range(count)])

    struct = jax.ShapeDtypeStruct
    def in_hbm(*arrays):
        return [pltpu.with_memory_space_constraint(array, pltpu.HBM) for array in arrays]

    def space_for(array):
        return pltpu.VMEM(array.shape, array.dtype)

    hbm = pl.BlockSpec(memory_space=pltpu.HBM)
    field, cot = jnp.transpose(latent_field, (1, 2, 0, 3)), jnp.transpose(cotangent, (1, 2, 0, 3))
    small = (jnp.transpose(regions, (1, 0, 2)), bias_table[0], norm_gain)
    same, others = struct((SAME, features), bf16), struct((2 * QUARTER, features), bf16)
    own, far, far_others, to_lat, table, gain = call(
        load_kernel,
        "load",
        [hbm] * 5,
        [others, same, others, others] + [struct(array.shape, array.dtype) for array in small[1:]],
        [space_for(field), space_for(cot), space_for(small[0]), pltpu.SemaphoreType.DMA((5,))],
        moved=1 << 20,
    )(*in_hbm(field, cot, *small))
    from_near = move(far, 1, 0)
    from_near_diag = move(far_others, 1, -1)
    from_lat = move(to_lat, 0, -1)

    bias_full, input_weight_t, lane_moves, row_moves, eye, place, place_t, weight_in, weight_out = call(
        bias_kernel,
        "expand_bias",
        whole(1) + [hbm] * 2,
        [
            struct((HEADS, CELLS, CELLS), bf16),
            struct((features, features), bf16),
            struct((WIDE, WIDE), bf16),
            struct((HEADS * 16, HEADS * 16), bf16),
            struct((features, features), bf16),
            struct((2 * CELLS, 2 * CELLS), bf16),
            struct((CELLS, CELLS), bf16),
            struct(input_weight.shape, bf16),
            struct(output_weight.shape, bf16),
        ],
        [
            pltpu.VMEM((HEADS * 16, WIDE), f32),
            pltpu.VMEM((HEADS, CELLS, CELLS), f32),
            pltpu.SemaphoreType.DMA((2,)),
        ],
        moved=1 << 21,
    )(table, *in_hbm(input_weight, output_weight))

    half_sum = struct((lon_count * packet.weight_size, LANES), bf16)
    results = call(
        functools.partial(window_kernel, packet),
        "window",
        whole(10),
        [
            half_sum,
            half_sum,
            struct((HEADS, CELLS, CELLS), bf16),
            struct((4, features, CELLS), bf16),
            struct((CELLS, features), f32),
            struct((CELLS, 1), f32),
            struct((CELLS, features), bf16),
        ],
        [pltpu.VMEM((2, features, CELLS), bf16)],
        flops=10**9,
        moved=5 << 20,
    )(
            own,
        from_near,
        from_near_diag,
        from_lat,
        gain,
        weight_in,
        input_weight_t,
        weight_out,
        bias_full,
        place,
    )
    keep, send, scores_low, *saved = results

    received = swap(send, "lat", 1)
    table_part = call(
        functools.partial(fold_kernel, packet),
        "fold_table",
        whole(3),
        struct((packet.table_size, LANES), bf16),
        [
            pltpu.VMEM((2, CELLS, WIDE), f32),
            pltpu.VMEM((HEADS * 16, WIDE), f32),
            pltpu.VMEM((16, packet.table_tiles * LANES), f32),
        ],
        moved=1 << 21,
    )(scores_low, lane_moves, row_moves)

    groups = lon_count // 4
    parts = call(
        functools.partial(first_exchange_kernel, packet),
        "add_lat",
        whole(3),
        [struct((groups * packet.weight_size + packet.quarter, LANES), bf16)] * 4,
        moved=2 << 20,
    )(keep, received, table_part)
    parts, saved = lax.optimization_barrier((parts, saved))

    def trade(parts, shift):
        return [swap(parts[step], "lon", step << shift) for step in (3, 2, 1)] + [parts[0]]

    held = trade(parts, 0)
    piece = struct((QUARTER, features), bf16)
    back_own, back_near, back_lat, gain_part = call(
        field_kernel,
        "grad_field",
        whole(8),
        [piece, others, piece, struct((16, LANES), bf16)],
        flops=10**8,
        moved=5 << 20,
    )(weight_in, *saved, gain, place_t, eye)
    home_lat = move(back_lat, 0, 1)
    gain_other = swap(gain_part, "lat", 1)
    held, home_lat, gain_other = lax.optimization_barrier((held, home_lat, gain_other))
    gains = [gain_part, gain_other]
    home_near = move(back_near, -1, 0)
    home_diag = move(home_near, 0, 1)
    for shift in range(2, lon_count.bit_length() - 1, 2):
        groups //= 4
        parts = call(
            functools.partial(next_exchange_kernel, packet, shift, len(gains)),
            "add_lon",
            whole(len(gains) + 4),
            [struct((groups * packet.weight_size + packet.quarter + 16, LANES), bf16)] * 4,
            moved=1 << 20,
        )(*gains, *held)
        gains = []
        held = trade(parts, shift)
    weight_sum, table_sum = call(
        functools.partial(last_sum_kernel, packet),
        "add_last",
        whole(4),
        [struct((packet.weight_size, LANES), bf16), struct((packet.quarter + 16, LANES), bf16)],
        moved=1 << 18,
    )(*held)
    table_parts = trade([table_sum] * 4, 0)[::-1]
    for bit in range(1, lat_count.bit_length() - 1):
        weight_sum = weight_sum + swap(weight_sum, "lat", 1 << bit)
    weight_other = swap(weight_sum, "lat", 1)

    cells_in_all = latent_field.shape[0] * latent_field.shape[1] * latent_field.shape[2]
    factor = 1.0 / math.sqrt(cells_in_all * lon_count * lat_count)
    grad_input_weight, grad_output_weight, grad_table, gain_sum = call(
        functools.partial(finish_kernel, packet, math.sqrt(head_dim), factor),
        "finish",
        whole(6),
        [
            struct((packet.weight_rows, 3 * features), bf16),
            struct((packet.weight_rows, features), bf16),
            struct((HEADS, 1, PLANE * SPAN), f32),
            struct((features,), f32),
        ],
        [pltpu.VMEM((4, packet.quarter, LANES), f32)],
        moved=1 << 19,
    )(weight_sum, weight_other, *table_parts)
    for bit in range(1, lat_count.bit_length() - 1):
        gain_sum = gain_sum + swap(gain_sum, "lat", 1 << bit)

    grad_field = call(
        unpack_kernel,
        "unpack_quarters",
        whole(4),
        struct((WIN_LAT, WIN_LON, LEV, features), bf16),
        moved=4 << 20,
    )(back_own, home_near, home_lat, home_diag)
    return (
        jnp.transpose(grad_field, (2, 0, 1, 3)),
        grad_input_weight,
        grad_output_weight,
        gain_sum,
        jnp.transpose(grad_table, (1, 0, 2)),
    )


def solution(mesh):
    in_specs = (
        P(None, "lat", "lon", None),
        P(None, "lat", "lon", None),
        P(),
        P(),
        P(),
        P("lat", None, None),
        P(None, "lat", "lon"),
    )
    out_specs = (
        P(None, "lat", "lon", None),
        P("lon", None),
        P("lon", None),
        P(),
        P("lat", None, None),
    )
    return jax.shard_map(
        functools.partial(on_device, mesh.shape["lon"], mesh.shape["lat"]),
        mesh=mesh,
        in_specs=in_specs,
        out_specs=out_specs,
        check_vma=False,
    )
```

```python
import functools
import math

import jax
import jax.numpy as jnp
from jax import lax
from jax.experimental import pallas as pl
from jax.experimental.pallas import tpu as pltpu
from jax.sharding import PartitionSpec as P

HEADS = 12
LEV = 2
WIN_LAT = 6
WIN_LON = 12
PLANE = LEV * WIN_LAT
CELLS = PLANE * WIN_LON
SPAN = (2 * WIN_LON - 1) * PLANE
WIDE = 384
LANES = 128
QUARTER = LEV * (WIN_LAT // 2) * (WIN_LON // 2)

norm_eps = 1e-05
masked_score = -1000000000.0
f32 = jnp.float32
bf16 = jnp.bfloat16

QUARTERS = ((0, 0), (0, 1), (1, 0), (1, 1))


def segments():
    reach = SPAN // PLANE
    first = 0
    for level_i in range(LEV):
        for level_j in range(LEV):
            for row_i in range(WIN_LAT):
                for row_j in range(WIN_LAT):
                    yield first, level_i * WIN_LAT + row_i, level_j * WIN_LAT + row_j
                    first += reach


def rounded_up(value, step):
    return -(-value // step) * step


class Packet:
    def __init__(self, lon_count, features):
        self.lon_count = lon_count
        self.weight_rows = features // lon_count
        self.weight_used = 6 * self.weight_rows
        self.weight_size = rounded_up(self.weight_used, 16)
        self.table_tiles = -(-PLANE * SPAN // LANES)
        self.table_rows = HEADS * self.table_tiles
        self.table_size = rounded_up(self.table_rows, 4 * 16)
        self.quarter = self.table_size // 4


def nt_dot(left, right):
    return lax.dot_general(left, right, (((1,), (1,)), ((), ())), preferred_element_type=f32)


def nn_dot(left, right):
    return jnp.dot(left, right, preferred_element_type=f32)


def fetch(sources, targets, sems):
    copies = [pltpu.make_async_copy(src, dst, sems.at[at]) for at, (src, dst) in enumerate(zip(sources, targets))]
    for copy in copies:
        copy.start()
    return copies


SAME = 80


def load_kernel(field_src, cot_src, *refs):
    sources, out_refs, (table_ref, gain_ref) = refs[:3], refs[3:7], refs[7:9]
    field_ref, cot_ref, regions_ref, sems = refs[9:]
    copies = fetch((field_src, cot_src) + sources, (field_ref, cot_ref, regions_ref, table_ref, gain_ref), sems)
    for copy in copies[:3]:
        copy.wait()
    half_rows, half_cols = WIN_LAT // 2, WIN_LON // 2
    features = field_ref.shape[3]
    ids = [regions_ref[row, level : level + 1, :].astype(f32) for level in range(LEV) for row in range(WIN_LAT)]
    ids.append(jnp.zeros((1, features - CELLS), f32))
    tail = jnp.concatenate([jnp.concatenate(ids, axis=1), jnp.zeros((SAME - 2 * QUARTER - 1, features), f32)], axis=0)
    wanted = ((half_rows, 0), (half_rows, half_cols), (0, half_cols), (0, 0))
    for (first_row, first_col), out_ref in zip(wanted, out_refs):
        pieces = [
            ref[first_row + row, first_col + col].astype(f32)
            for ref in (field_ref, cot_ref)
            for row in range(half_rows)
            for col in range(half_cols)
        ]
        if out_ref.shape[0] == SAME:
            pieces.append(tail)
        out_ref[...] = jnp.concatenate(pieces, axis=0).astype(bf16)
    for copy in copies[3:]:
        copy.wait()


def one_hot(flags):
    return flags.astype(f32).astype(bf16)


def counted(shape, axis):
    return lax.broadcasted_iota(jnp.int32, shape, axis)


def cell_source(cell, stride):
    col, level, row = lax.div(cell, PLANE), lax.rem(lax.div(cell, WIN_LAT), LEV), lax.rem(cell, WIN_LAT)
    half_rows, half_cols = WIN_LAT // 2, WIN_LON // 2
    quarter = 2 * lax.div(row, half_rows) + lax.div(col, half_cols)
    place = lax.rem(row, half_rows) * half_cols + lax.rem(col, half_cols)
    return quarter * stride + place * LEV + lax.rem(level + LEV // 2, LEV)


def unpack_kernel(own_ref, near_ref, lat_ref, near_diag_ref, out_ref):
    half_rows, half_cols = WIN_LAT // 2, WIN_LON // 2
    quarters = (
        near_ref[...].astype(f32)[:QUARTER],
        own_ref[...].astype(f32),
        near_diag_ref[...].astype(f32)[QUARTER:],
        lat_ref[...].astype(f32),
    )
    for (lat_half, lon_half), cells in zip(QUARTERS, quarters):
        first_row, first_col = (1 - lat_half) * half_rows, (1 - lon_half) * half_cols
        for row in range(half_rows):
            for col in range(half_cols):
                first = (row * half_cols + col) * LEV
                out_ref[first_row + row, first_col + col] = cells[first : first + LEV].astype(bf16)


def bias_kernel(
    table_ref,
    win_src,
    wout_src,
    out_ref,
    win_t_ref,
    lanes_ref,
    rows_ref,
    eye_ref,
    place_ref,
    place_t_ref,
    win_ref,
    wout_ref,
    stage,
    full,
    sems,
):
    copies = fetch((win_src, wout_src), (win_ref, wout_ref), sems)
    features = win_ref.shape[0]
    square = (features, features)
    eye = one_hot(counted(square, 0) == counted(square, 1))
    eye_ref[...] = eye
    source, lane = cell_source(counted((CELLS, 1), 0), 2 * QUARTER), counted((CELLS, 2 * CELLS), 1)
    place_ref[:CELLS] = one_hot(source == lane)
    place_ref[CELLS:] = one_hot(source + QUARTER == lane)
    place_t_ref[...] = one_hot(cell_source(counted((1, CELLS), 1), QUARTER) == counted((CELLS, CELLS), 0))
    lane = counted((1, WIDE), 1)
    target = jnp.where(lane < SPAN, lax.rem(lane, PLANE) * (SPAN // PLANE) + lax.div(lane, PLANE), -1)
    lanes_ref[...] = one_hot(target == counted((WIDE, WIDE), 0))
    sixteens = HEADS * 16
    row = counted((sixteens, 1), 0)
    target = jnp.where(lax.rem(row, 16) < PLANE, lax.rem(row, 16) * 16 + lax.div(row, 16), -1)
    rows_ref[...] = one_hot(target == counted((sixteens, sixteens), 1))

    stage[...] = jnp.zeros(stage.shape, f32)
    reach = SPAN // PLANE
    table = table_ref[...].astype(f32)
    for first, plane_i, plane_j in segments():
        stage[16 * plane_j : 16 * plane_j + HEADS, reach * plane_i : reach * (plane_i + 1)] = table[
            :, first : first + reach
        ]
    moved = nn_dot(stage[...].astype(bf16), lanes_ref[...]).astype(bf16)
    rows = nn_dot(rows_ref[...], moved)

    for col in range(WIN_LON):
        shift = PLANE * (WIN_LON - 1 - col)
        moved = rows if shift == 0 else pltpu.roll(rows, WIDE - shift, 1)
        for head in range(HEADS):
            full[head, PLANE * col : PLANE * (col + 1), :] = moved[16 * head : 16 * head + PLANE, :CELLS]
    for head in range(HEADS):
        out_ref[head] = full[head].astype(bf16)
    for copy in copies:
        copy.wait()
    win_t_ref[...] = nt_dot(eye, win_ref[:, :features]).astype(bf16)


def window_kernel(
    packet,
    own_ref,
    near_ref,
    near_diag_ref,
    lat_ref,
    gain_ref,
    win_ref,
    win_t_ref,
    wout_ref,
    bias_ref,
    place_ref,
    keep_ref,
    send_ref,
    scores_ref,
    right,
    normalized_ref,
    inv_std_ref,
    cot_ref,
    left,
):
    features = win_ref.shape[0]
    head_dim = features // HEADS
    group_heads = LANES // head_dim
    score_scale = head_dim ** (-0.5)
    near = near_ref[...].astype(f32)
    west, east = [near[: 2 * QUARTER], near_diag_ref[...].astype(f32)], [own_ref[...].astype(f32), lat_ref[...].astype(f32)]
    stacked = jnp.concatenate([west[0], east[0], west[1], east[1]], axis=0).astype(bf16)
    cell, lane = counted((CELLS, CELLS), 0), counted((CELLS, CELLS), 1)
    source = lax.rem(cell, PLANE) * WIN_LON + lax.div(cell, PLANE)
    ids = near[2 * QUARTER : 2 * QUARTER + 1, :CELLS]
    region_col = jnp.sum(jnp.where(source == lane, ids, 0.0), axis=1, keepdims=True)
    region_row = jnp.sum(jnp.where(cell == lane, region_col, 0.0), axis=0, keepdims=True)
    same = region_col == region_row
    placed = nn_dot(place_ref[...], stacked)
    field = placed[:CELLS]
    cot = placed[CELLS:].astype(bf16)
    cot_ref[...] = cot
    gain = gain_ref[...].reshape(1, features)

    centred = field - jnp.mean(field, axis=-1, keepdims=True)
    inv_std = lax.rsqrt(jnp.mean(centred * centred, axis=-1, keepdims=True) + norm_eps)
    normalized = centred * inv_std
    normalized_ref[...] = normalized
    inv_std_ref[...] = inv_std
    normed = (normalized * gain).astype(bf16)

    query_t = nt_dot(win_t_ref[...], normed).astype(bf16)
    wide_keys_values = nn_dot(normed, win_ref[:, features:])
    keys_values = wide_keys_values.astype(bf16)
    grad_att_t = nt_dot(wout_ref[...], cot).astype(bf16)
    key_value_t = jnp.transpose(wide_keys_values).astype(bf16)
    left[0] = jnp.transpose(normed.astype(f32)).astype(bf16)
    right[3] = jnp.transpose(placed[CELLS:]).astype(bf16)

    def spread(head_rows, slot):
        parts = []
        if slot:
            parts.append(jnp.zeros((slot * head_dim, CELLS), bf16))
        parts.append(head_rows)
        if slot < group_heads - 1:
            parts.append(jnp.zeros(((group_heads - 1 - slot) * head_dim, CELLS), bf16))
        return jnp.concatenate(parts, axis=0)

    def rows_of(head):
        return slice(head * head_dim, (head + 1) * head_dim)

    def part(head, index):
        if index == 0:
            return query_t[rows_of(head)]
        first = (index - 1) * features + head * head_dim
        return key_value_t[first : first + head_dim]

    def scores_of(head):
        group, slot = divmod(head, group_heads)
        keys = keys_values[:, group * LANES : (group + 1) * LANES]
        values = keys_values[:, features + group * LANES : features + (group + 1) * LANES]
        scores = nn_dot(keys, spread(part(head, 0), slot))
        return scores, nn_dot(values, spread(grad_att_t[rows_of(head)], slot))

    def softmax_of(head, scores, grad_probs):
        scores = jnp.where(same, scores * score_scale + bias_ref[head].astype(f32), masked_score)
        grown = jnp.exp(scores - jnp.max(scores, axis=0, keepdims=True))
        probs = grown * (1.0 / jnp.sum(grown, axis=0, keepdims=True))
        weighted = probs * grad_probs
        grad_scores = weighted - probs * jnp.sum(weighted, axis=0, keepdims=True)
        return probs.astype(bf16), (grad_scores * score_scale).astype(bf16)

    def products_of(head, probs_low, scores_low):
        rows = rows_of(head)
        scores_ref[head] = scores_low
        left[1, rows] = nn_dot(part(head, 2), probs_low).astype(bf16)
        right[0, rows] = nn_dot(part(head, 1), scores_low).astype(bf16)
        right[1, rows] = nt_dot(part(head, 0), scores_low).astype(bf16)
        right[2, rows] = nt_dot(grad_att_t[rows], probs_low).astype(bf16)

    raw, soft = {}, {}
    for turn in range(HEADS + 2):
        if turn < HEADS:
            raw[turn] = scores_of(turn)
        if turn >= 2:
            products_of(turn - 2, *soft.pop(turn - 2))
        if 1 <= turn <= HEADS:
            soft[turn - 1] = softmax_of(turn - 1, *raw.pop(turn - 1))

    odd = lax.rem(lax.axis_index("lat"), 2)

    for out_ref, half in ((send_ref, 1 - odd), (keep_ref, odd)):
        low = nt_dot(left[0], right[2 * half])
        high = nt_dot(left[half], right[2 * half + 1])
        for owner in range(packet.lon_count):
            rows = slice(owner * packet.weight_rows, (owner + 1) * packet.weight_rows)
            pieces = [
                block[rows, tile * LANES : (tile + 1) * LANES] for block in (low, high) for tile in range(3)
            ]
            if packet.weight_size > packet.weight_used:
                pieces.append(jnp.zeros((packet.weight_size - packet.weight_used, LANES), f32))
            first = owner * packet.weight_size
            out_ref[first : first + packet.weight_size] = jnp.concatenate(pieces, axis=0).astype(bf16)


def field_kernel(
    win_ref,
    grad_projected_ref,
    normalized_ref,
    inv_std_ref,
    cot_ref,
    gain_ref,
    place_t_ref,
    eye_ref,
    back_own_ref,
    back_near_ref,
    back_lat_ref,
    gain_out_ref,
):
    features = win_ref.shape[0]
    grad_shifted_t = sum(
        nn_dot(win_ref[:, block * features : (block + 1) * features], grad_projected_ref[block]) for block in range(3)
    ).astype(bf16)
    grad_normed = nt_dot(eye_ref[:CELLS, :CELLS], grad_shifted_t)
    normalized = normalized_ref[...]
    scaled = grad_normed * gain_ref[...].reshape(1, features)
    grad_field = cot_ref[...].astype(f32) + inv_std_ref[...] * (
        scaled
        - jnp.mean(scaled, axis=-1, keepdims=True)
        - normalized * jnp.mean(scaled * normalized, axis=-1, keepdims=True)
    )
    back = nn_dot(place_t_ref[...], grad_field.astype(bf16))
    quarters = [back[quarter * QUARTER : (quarter + 1) * QUARTER] for quarter in range(4)]
    back_own_ref[...] = quarters[1].astype(bf16)
    back_near_ref[...] = jnp.concatenate(quarters[::2], axis=0).astype(bf16)
    back_lat_ref[...] = quarters[3].astype(bf16)
    gain_sum = jnp.sum(grad_normed * normalized, axis=0, keepdims=True)
    gain_rows = [gain_sum[:, tile * LANES : (tile + 1) * LANES] for tile in range(3)]
    gain_out_ref[...] = jnp.concatenate(gain_rows + [jnp.zeros((13, LANES), f32)], axis=0).astype(bf16)


def fold_kernel(packet, scores_ref, lanes_ref, rows_ref, out_ref, wide, table, flat):
    wide[...] = jnp.zeros(wide.shape, f32)
    table[...] = jnp.zeros(table.shape, f32)
    flat[...] = jnp.zeros(flat.shape, bf16)
    for head in range(HEADS):
        wide[head % 2, :, :CELLS] = scores_ref[head].astype(f32)
        total = wide[head % 2, :PLANE, :]
        for col in range(1, WIN_LON):
            total = pltpu.roll(total, PLANE, 1) + wide[head % 2, PLANE * col : PLANE * (col + 1), :]
        table[16 * head : 16 * head + PLANE, :] = total
    moved = nn_dot(rows_ref[...], table[...].astype(bf16)).astype(bf16)
    moved = nt_dot(moved, lanes_ref[...]).astype(bf16)
    reach = SPAN // PLANE
    for first, plane_i, plane_j in segments():
        flat[:, first : first + reach] = moved[16 * plane_j : 16 * (plane_j + 1), reach * plane_i : reach * (plane_i + 1)]
    tiles = [
        flat[:, tile * LANES : (tile + 1) * LANES].astype(f32)[:HEADS] for tile in range(packet.table_tiles)
    ]
    tiles.append(jnp.zeros((packet.table_size - packet.table_rows, LANES), f32))
    out_ref[...] = jnp.concatenate(tiles, axis=0).astype(bf16)


def first_exchange_kernel(packet, keep_ref, recv_ref, table_ref, *out_refs):
    low = lax.rem(lax.axis_index("lon"), 4)
    size, quarter = packet.weight_size, packet.quarter
    for step, out_ref in enumerate(out_refs):
        digit = lax.bitwise_xor(low, step)
        for upper in range(packet.lon_count // 4):
            rows = pl.ds(pl.multiple_of((upper * 4 + digit) * size, 16), size)
            out_ref[upper * size : (upper + 1) * size] = keep_ref[rows] + recv_ref[rows]
        first = packet.lon_count // 4 * size
        out_ref[first:] = table_ref[pl.ds(pl.multiple_of(digit * quarter, 16), quarter)]


def summed(refs, rows):
    terms = [ref[rows] for ref in refs]
    while len(terms) > 1:
        terms = [left + right for left, right in zip(terms[::2], terms[1::2])]
    return terms[0]


def next_exchange_kernel(packet, shift, gains, *refs):
    gain_refs, held, out_refs = refs[:gains], refs[gains:-4], refs[-4:]
    size, quarter = packet.weight_size, packet.quarter
    digit = lax.rem(lax.shift_right_logical(lax.axis_index("lon"), shift), 4)
    groups = (out_refs[0].shape[0] - quarter - 16) // size
    rest = 4 * groups * size
    table = summed(held, slice(rest, rest + quarter))
    gain = summed(gain_refs, slice(0, 16)) if gains else summed(held, slice(rest + quarter, rest + quarter + 16))
    for step, out_ref in enumerate(out_refs):
        for upper in range(groups):
            owner = upper * 4 + lax.bitwise_xor(digit, step)
            out_ref[upper * size : (upper + 1) * size] = summed(held, pl.ds(pl.multiple_of(owner * size, 16), size))
        out_ref[groups * size : groups * size + quarter] = table
        out_ref[groups * size + quarter :] = gain


def last_sum_kernel(packet, a_ref, b_ref, c_ref, d_ref, weight_ref, table_ref):
    refs = (a_ref, b_ref, c_ref, d_ref)
    weight_ref[...] = summed(refs, slice(0, packet.weight_size))
    table_ref[...] = summed(refs, slice(packet.weight_size, packet.weight_size + packet.quarter + 16))


def weights_out_kernel(packet, factor, weights_ref, other_weights_ref, grad_in_ref, grad_out_ref):
    odd = lax.rem(lax.axis_index("lat"), 2) == 1
    own, other = weights_ref[...].astype(f32) * factor, other_weights_ref[...].astype(f32) * factor
    halves = (jnp.where(odd, other, own), jnp.where(odd, own, other))
    size = packet.weight_rows
    tiles = [half[tile * size : (tile + 1) * size] for half in halves for tile in range(6)]
    grad_in_ref[...] = jnp.concatenate(tiles[:9], axis=1).astype(bf16)
    grad_out_ref[...] = jnp.concatenate(tiles[9:], axis=1).astype(bf16)


def table_out_kernel(packet, table_scale, factor, a_ref, b_ref, c_ref, d_ref, grad_table_ref, grad_gain_ref, quarters):
    low = lax.rem(lax.axis_index("lon"), 4)
    parts = (a_ref, b_ref, c_ref, d_ref)
    for step, ref in enumerate(parts):
        quarters[lax.bitwise_xor(low, step)] = ref[: packet.quarter].astype(f32)
    total = quarters[...].reshape(packet.table_size, LANES)
    for tile in range(packet.table_tiles):
        first = tile * LANES
        width = min(LANES, grad_table_ref.shape[2] - first)
        block = total[HEADS * tile : HEADS * (tile + 1), :width] * table_scale
        for head in range(HEADS):
            grad_table_ref[head, :, first : first + width] = block[head : head + 1]
    gain = sum(ref[packet.quarter :].astype(f32) for ref in parts) * factor
    grad_gain_ref[...] = jnp.concatenate([gain[tile : tile + 1] for tile in range(3)], axis=1).reshape(
        grad_gain_ref.shape
    )


def whole(count):
    return [pl.BlockSpec(memory_space=pltpu.VMEM)] * count


def call(kernel, name, in_specs, outs, scratch=(), flops=0, moved=0):
    return pl.pallas_call(
        kernel,
        name=name,
        out_shape=outs,
        in_specs=in_specs,
        out_specs=jax.tree.map(lambda _: pl.BlockSpec(memory_space=pltpu.VMEM), outs),
        scratch_shapes=list(scratch),
        compiler_params=pltpu.CompilerParams(vmem_limit_bytes=20 * 1024 * 1024),
        cost_estimate=pl.CostEstimate(flops=flops, bytes_accessed=moved, transcendentals=0),
    )


def on_device(lon_count, lat_count, latent_field, cotangent, norm_gain, input_weight, output_weight, bias_table, regions):
    features = latent_field.shape[3]
    head_dim = features // HEADS
    packet = Packet(lon_count, features)

    def move(value, lon_step, lat_step):
        pairs = []
        for lon in range(lon_count):
            for lat in range(lat_count):
                target = ((lon + lon_step) % lon_count) * lat_count + (lat + lat_step) % lat_count
                pairs.append((lon * lat_count + lat, target))
        return lax.ppermute(value, ("lon", "lat"), pairs)

    def swap(value, axis, mask):
        count = lon_count if axis == "lon" else lat_count
        return lax.ppermute(value, axis, [(source, source ^ mask) for source in range(count)])

    struct = jax.ShapeDtypeStruct
    def in_hbm(*arrays):
        return [pltpu.with_memory_space_constraint(array, pltpu.HBM) for array in arrays]

    def space_for(array):
        return pltpu.VMEM(array.shape, array.dtype)

    hbm = pl.BlockSpec(memory_space=pltpu.HBM)
    field, cot = jnp.transpose(latent_field, (1, 2, 0, 3)), jnp.transpose(cotangent, (1, 2, 0, 3))
    small = (jnp.transpose(regions, (1, 0, 2)), bias_table[0], norm_gain)
    same, others = struct((SAME, features), bf16), struct((2 * QUARTER, features), bf16)
    own, far, far_others, to_lat, table, gain = call(
        load_kernel,
        "load",
        [hbm] * 5,
        [others, same, others, others] + [struct(array.shape, array.dtype) for array in small[1:]],
        [space_for(field), space_for(cot), space_for(small[0]), pltpu.SemaphoreType.DMA((5,))],
        moved=1 << 20,
    )(*in_hbm(field, cot, *small))
    from_near = move(far, 1, 0)
    from_near_diag = move(far_others, 1, -1)
    from_lat = move(to_lat, 0, -1)

    bias_full, input_weight_t, lane_moves, row_moves, eye, place, place_t, weight_in, weight_out = call(
        bias_kernel,
        "expand_bias",
        whole(1) + [hbm] * 2,
        [
            struct((HEADS, CELLS, CELLS), bf16),
            struct((features, features), bf16),
            struct((WIDE, WIDE), bf16),
            struct((HEADS * 16, HEADS * 16), bf16),
            struct((features, features), bf16),
            struct((2 * CELLS, 2 * CELLS), bf16),
            struct((CELLS, CELLS), bf16),
            struct(input_weight.shape, bf16),
            struct(output_weight.shape, bf16),
        ],
        [
            pltpu.VMEM((HEADS * 16, WIDE), f32),
            pltpu.VMEM((HEADS, CELLS, CELLS), f32),
            pltpu.SemaphoreType.DMA((2,)),
        ],
        moved=1 << 21,
    )(table, *in_hbm(input_weight, output_weight))

    half_sum = struct((lon_count * packet.weight_size, LANES), bf16)
    results = call(
        functools.partial(window_kernel, packet),
        "window",
        whole(10),
        [
            half_sum,
            half_sum,
            struct((HEADS, CELLS, CELLS), bf16),
            struct((4, features, CELLS), bf16),
            struct((CELLS, features), f32),
            struct((CELLS, 1), f32),
            struct((CELLS, features), bf16),
        ],
        [pltpu.VMEM((2, features, CELLS), bf16)],
        flops=10**9,
        moved=5 << 20,
    )(
            own,
        from_near,
        from_near_diag,
        from_lat,
        gain,
        weight_in,
        input_weight_t,
        weight_out,
        bias_full,
        place,
    )
    keep, send, scores_low, *saved = results

    received = swap(send, "lat", 1)
    table_part = call(
        functools.partial(fold_kernel, packet),
        "fold_table",
        whole(3),
        struct((packet.table_size, LANES), bf16),
        [
            pltpu.VMEM((2, CELLS, WIDE), f32),
            pltpu.VMEM((HEADS * 16, WIDE), f32),
            pltpu.VMEM((16, packet.table_tiles * LANES), bf16),
        ],
        moved=1 << 21,
    )(scores_low, lane_moves, row_moves)

    groups = lon_count // 4
    parts = call(
        functools.partial(first_exchange_kernel, packet),
        "add_lat",
        whole(3),
        [struct((groups * packet.weight_size + packet.quarter, LANES), bf16)] * 4,
        moved=2 << 20,
    )(keep, received, table_part)
    parts, saved = lax.optimization_barrier((parts, saved))

    def trade(parts, shift):
        return [swap(parts[step], "lon", step << shift) for step in (3, 2, 1)] + [parts[0]]

    held = trade(parts, 0)
    piece = struct((QUARTER, features), bf16)
    back_own, back_near, back_lat, gain_part = call(
        field_kernel,
        "grad_field",
        whole(8),
        [piece, others, piece, struct((16, LANES), bf16)],
        flops=10**8,
        moved=5 << 20,
    )(weight_in, *saved, gain, place_t, eye)
    home_lat = move(back_lat, 0, 1)
    gain_other = swap(gain_part, "lat", 1)
    held, home_lat, gain_other = lax.optimization_barrier((held, home_lat, gain_other))
    gains = [gain_part, gain_other]
    home_near = move(back_near, -1, 0)
    home_diag = move(home_near, 0, 1)
    for shift in range(2, lon_count.bit_length() - 1, 2):
        groups //= 4
        parts = call(
            functools.partial(next_exchange_kernel, packet, shift, len(gains)),
            "add_lon",
            whole(len(gains) + 4),
            [struct((groups * packet.weight_size + packet.quarter + 16, LANES), bf16)] * 4,
            moved=1 << 20,
        )(*gains, *held)
        gains = []
        held = trade(parts, shift)
    weight_sum, table_sum = call(
        functools.partial(last_sum_kernel, packet),
        "add_last",
        whole(4),
        [struct((packet.weight_size, LANES), bf16), struct((packet.quarter + 16, LANES), bf16)],
        moved=1 << 18,
    )(*held)
    table_parts = trade([table_sum] * 4, 0)[::-1]
    for bit in range(1, lat_count.bit_length() - 1):
        weight_sum = weight_sum + swap(weight_sum, "lat", 1 << bit)
    weight_other = swap(weight_sum, "lat", 1)

    cells_in_all = latent_field.shape[0] * latent_field.shape[1] * latent_field.shape[2]
    factor = 1.0 / math.sqrt(cells_in_all * lon_count * lat_count)
    grad_input_weight, grad_output_weight = call(
        functools.partial(weights_out_kernel, packet, factor),
        "weights_out",
        whole(2),
        [struct((packet.weight_rows, 3 * features), bf16), struct((packet.weight_rows, features), bf16)],
        moved=1 << 18,
    )(weight_sum, weight_other)
    table_parts, grad_input_weight = lax.optimization_barrier((table_parts, grad_input_weight))
    grad_table, gain_sum = call(
        functools.partial(table_out_kernel, packet, math.sqrt(head_dim), factor),
        "table_out",
        whole(4),
        [struct((HEADS, 1, PLANE * SPAN), f32), struct((features,), f32)],
        [pltpu.VMEM((4, packet.quarter, LANES), f32)],
        moved=1 << 19,
    )(*table_parts)
    for bit in range(1, lat_count.bit_length() - 1):
        gain_sum = gain_sum + swap(gain_sum, "lat", 1 << bit)

    grad_field = call(
        unpack_kernel,
        "unpack_quarters",
        whole(4),
        struct((WIN_LAT, WIN_LON, LEV, features), bf16),
        moved=4 << 20,
    )(back_own, home_near, home_lat, home_diag)
    return (
        jnp.transpose(grad_field, (2, 0, 1, 3)),
        grad_input_weight,
        grad_output_weight,
        gain_sum,
        jnp.transpose(grad_table, (1, 0, 2)),
    )


def solution(mesh):
    in_specs = (
        P(None, "lat", "lon", None),
        P(None, "lat", "lon", None),
        P(),
        P(),
        P(),
        P("lat", None, None),
        P(None, "lat", "lon"),
    )
    out_specs = (
        P(None, "lat", "lon", None),
        P("lon", None),
        P("lon", None),
        P(),
        P("lat", None, None),
    )
    return jax.shard_map(
        functools.partial(on_device, mesh.shape["lon"], mesh.shape["lat"]),
        mesh=mesh,
        in_specs=in_specs,
        out_specs=out_specs,
        check_vma=False,
    )
```

```python
import functools
import math

import jax
import jax.numpy as jnp
from jax import lax
from jax.experimental import pallas as pl
from jax.experimental.pallas import tpu as pltpu
from jax.sharding import PartitionSpec as P

HEADS = 12
LEV = 2
WIN_LAT = 6
WIN_LON = 12
PLANE = LEV * WIN_LAT
CELLS = PLANE * WIN_LON
SPAN = (2 * WIN_LON - 1) * PLANE
WIDE = 384
LANES = 128
QUARTER = LEV * (WIN_LAT // 2) * (WIN_LON // 2)

norm_eps = 1e-05
masked_score = -1000000000.0
f32 = jnp.float32
bf16 = jnp.bfloat16

QUARTERS = ((0, 0), (0, 1), (1, 0), (1, 1))


def segments():
    reach = SPAN // PLANE
    first = 0
    for level_i in range(LEV):
        for level_j in range(LEV):
            for row_i in range(WIN_LAT):
                for row_j in range(WIN_LAT):
                    yield first, level_i * WIN_LAT + row_i, level_j * WIN_LAT + row_j
                    first += reach


def rounded_up(value, step):
    return -(-value // step) * step


class Packet:
    def __init__(self, lon_count, features):
        self.lon_count = lon_count
        self.weight_rows = features // lon_count
        self.weight_used = 6 * self.weight_rows
        self.weight_size = rounded_up(self.weight_used, 16)
        self.table_tiles = -(-PLANE * SPAN // LANES)
        self.table_rows = HEADS * self.table_tiles
        self.table_size = rounded_up(self.table_rows, 4 * 16)
        self.quarter = self.table_size // 4


def nt_dot(left, right):
    return lax.dot_general(left, right, (((1,), (1,)), ((), ())), preferred_element_type=f32)


def nn_dot(left, right):
    return jnp.dot(left, right, preferred_element_type=f32)


def fetch(sources, targets, sems):
    copies = [pltpu.make_async_copy(src, dst, sems.at[at]) for at, (src, dst) in enumerate(zip(sources, targets))]
    for copy in copies:
        copy.start()
    return copies


SAME = 80


def load_kernel(field_src, cot_src, *refs):
    sources, out_refs, (table_ref, gain_ref) = refs[:3], refs[3:7], refs[7:9]
    field_ref, cot_ref, regions_ref, sems = refs[9:]
    copies = fetch((field_src, cot_src) + sources, (field_ref, cot_ref, regions_ref, table_ref, gain_ref), sems)
    for copy in copies[:3]:
        copy.wait()
    half_rows, half_cols = WIN_LAT // 2, WIN_LON // 2
    features = field_ref.shape[3]
    ids = [regions_ref[row, level : level + 1, :].astype(f32) for level in range(LEV) for row in range(WIN_LAT)]
    ids.append(jnp.zeros((1, features - CELLS), f32))
    tail = jnp.concatenate([jnp.concatenate(ids, axis=1), jnp.zeros((SAME - 2 * QUARTER - 1, features), f32)], axis=0)
    wanted = ((half_rows, 0), (half_rows, half_cols), (0, half_cols), (0, 0))
    for (first_row, first_col), out_ref in zip(wanted, out_refs):
        pieces = [
            ref[first_row + row, first_col + col].astype(f32)
            for ref in (field_ref, cot_ref)
            for row in range(half_rows)
            for col in range(half_cols)
        ]
        if out_ref.shape[0] == SAME:
            pieces.append(tail)
        out_ref[...] = jnp.concatenate(pieces, axis=0).astype(bf16)
    for copy in copies[3:]:
        copy.wait()


def one_hot(flags):
    return flags.astype(f32).astype(bf16)


def counted(shape, axis):
    return lax.broadcasted_iota(jnp.int32, shape, axis)


def cell_source(cell, stride):
    col, level, row = lax.div(cell, PLANE), lax.rem(lax.div(cell, WIN_LAT), LEV), lax.rem(cell, WIN_LAT)
    half_rows, half_cols = WIN_LAT // 2, WIN_LON // 2
    quarter = 2 * lax.div(row, half_rows) + lax.div(col, half_cols)
    place = lax.rem(row, half_rows) * half_cols + lax.rem(col, half_cols)
    return quarter * stride + place * LEV + lax.rem(level + LEV // 2, LEV)


def unpack_kernel(own_ref, near_ref, lat_ref, near_diag_ref, out_ref):
    half_rows, half_cols = WIN_LAT // 2, WIN_LON // 2
    quarters = (
        near_ref[...].astype(f32)[:QUARTER],
        own_ref[...].astype(f32),
        near_diag_ref[...].astype(f32)[QUARTER:],
        lat_ref[...].astype(f32),
    )
    for (lat_half, lon_half), cells in zip(QUARTERS, quarters):
        first_row, first_col = (1 - lat_half) * half_rows, (1 - lon_half) * half_cols
        for row in range(half_rows):
            for col in range(half_cols):
                first = (row * half_cols + col) * LEV
                out_ref[first_row + row, first_col + col] = cells[first : first + LEV].astype(bf16)


def bias_kernel(
    table_ref,
    win_src,
    wout_src,
    out_ref,
    win_t_ref,
    lanes_ref,
    rows_ref,
    eye_ref,
    place_ref,
    place_t_ref,
    win_ref,
    wout_ref,
    stage,
    full,
    sems,
):
    copies = fetch((win_src, wout_src), (win_ref, wout_ref), sems)
    features = win_ref.shape[0]
    square = (features, features)
    eye = one_hot(counted(square, 0) == counted(square, 1))
    eye_ref[...] = eye
    source, lane = cell_source(counted((CELLS, 1), 0), 2 * QUARTER), counted((CELLS, 2 * CELLS), 1)
    place_ref[:CELLS] = one_hot(source == lane)
    place_ref[CELLS:] = one_hot(source + QUARTER == lane)
    place_t_ref[...] = one_hot(cell_source(counted((1, CELLS), 1), QUARTER) == counted((CELLS, CELLS), 0))
    lane = counted((1, WIDE), 1)
    target = jnp.where(lane < SPAN, lax.rem(lane, PLANE) * (SPAN // PLANE) + lax.div(lane, PLANE), -1)
    lanes_ref[...] = one_hot(target == counted((WIDE, WIDE), 0))
    sixteens = HEADS * 16
    row = counted((sixteens, 1), 0)
    target = jnp.where(lax.rem(row, 16) < PLANE, lax.rem(row, 16) * 16 + lax.div(row, 16), -1)
    rows_ref[...] = one_hot(target == counted((sixteens, sixteens), 1))

    stage[...] = jnp.zeros(stage.shape, f32)
    reach = SPAN // PLANE
    table = table_ref[...].astype(f32)
    for first, plane_i, plane_j in segments():
        stage[16 * plane_j : 16 * plane_j + HEADS, reach * plane_i : reach * (plane_i + 1)] = table[
            :, first : first + reach
        ]
    moved = nn_dot(stage[...].astype(bf16), lanes_ref[...]).astype(bf16)
    rows = nn_dot(rows_ref[...], moved)

    for col in range(WIN_LON):
        shift = PLANE * (WIN_LON - 1 - col)
        moved = rows if shift == 0 else pltpu.roll(rows, WIDE - shift, 1)
        for head in range(HEADS):
            full[head, PLANE * col : PLANE * (col + 1), :] = moved[16 * head : 16 * head + PLANE, :CELLS]
    for head in range(HEADS):
        out_ref[head] = full[head].astype(bf16)
    for copy in copies:
        copy.wait()
    win_t_ref[...] = nt_dot(eye, win_ref[:, :features]).astype(bf16)


def window_kernel(
    packet,
    own_ref,
    near_ref,
    near_diag_ref,
    lat_ref,
    gain_ref,
    win_ref,
    win_t_ref,
    wout_ref,
    bias_ref,
    place_ref,
    keep_ref,
    send_ref,
    scores_ref,
    right,
    normalized_ref,
    inv_std_ref,
    cot_ref,
    left,
):
    features = win_ref.shape[0]
    head_dim = features // HEADS
    group_heads = LANES // head_dim
    score_scale = head_dim ** (-0.5)
    near = near_ref[...].astype(f32)
    west, east = [near[: 2 * QUARTER], near_diag_ref[...].astype(f32)], [own_ref[...].astype(f32), lat_ref[...].astype(f32)]
    stacked = jnp.concatenate([west[0], east[0], west[1], east[1]], axis=0).astype(bf16)
    cell, lane = counted((CELLS, CELLS), 0), counted((CELLS, CELLS), 1)
    source = lax.rem(cell, PLANE) * WIN_LON + lax.div(cell, PLANE)
    ids = near[2 * QUARTER : 2 * QUARTER + 1, :CELLS]
    region_col = jnp.sum(jnp.where(source == lane, ids, 0.0), axis=1, keepdims=True)
    region_row = jnp.sum(jnp.where(cell == lane, region_col, 0.0), axis=0, keepdims=True)
    same = region_col == region_row
    placed = nn_dot(place_ref[...], stacked)
    field = placed[:CELLS]
    cot = placed[CELLS:].astype(bf16)
    cot_ref[...] = cot
    gain = gain_ref[...].reshape(1, features)

    centred = field - jnp.mean(field, axis=-1, keepdims=True)
    inv_std = lax.rsqrt(jnp.mean(centred * centred, axis=-1, keepdims=True) + norm_eps)
    normalized = centred * inv_std
    normalized_ref[...] = normalized
    inv_std_ref[...] = inv_std
    normed = (normalized * gain).astype(bf16)

    query_t = nt_dot(win_t_ref[...], normed).astype(bf16)
    wide_keys_values = nn_dot(normed, win_ref[:, features:])
    keys_values = wide_keys_values.astype(bf16)
    grad_att_t = nt_dot(wout_ref[...], cot).astype(bf16)
    key_value_t = jnp.transpose(wide_keys_values).astype(bf16)
    left[0] = jnp.transpose(normed.astype(f32)).astype(bf16)
    right[3] = jnp.transpose(placed[CELLS:]).astype(bf16)

    def spread(head_rows, slot):
        parts = []
        if slot:
            parts.append(jnp.zeros((slot * head_dim, CELLS), bf16))
        parts.append(head_rows)
        if slot < group_heads - 1:
            parts.append(jnp.zeros(((group_heads - 1 - slot) * head_dim, CELLS), bf16))
        return jnp.concatenate(parts, axis=0)

    def rows_of(head):
        return slice(head * head_dim, (head + 1) * head_dim)

    def part(head, index):
        if index == 0:
            return query_t[rows_of(head)]
        first = (index - 1) * features + head * head_dim
        return key_value_t[first : first + head_dim]

    def scores_of(head):
        group, slot = divmod(head, group_heads)
        keys = keys_values[:, group * LANES : (group + 1) * LANES]
        values = keys_values[:, features + group * LANES : features + (group + 1) * LANES]
        scores = nn_dot(keys, spread(part(head, 0), slot))
        return scores, nn_dot(values, spread(grad_att_t[rows_of(head)], slot))

    def softmax_of(head, scores, grad_probs):
        scores = jnp.where(same, scores * score_scale + bias_ref[head].astype(f32), masked_score)
        grown = jnp.exp(scores - jnp.max(scores, axis=0, keepdims=True))
        probs = grown * (1.0 / jnp.sum(grown, axis=0, keepdims=True))
        weighted = probs * grad_probs
        grad_scores = weighted - probs * jnp.sum(weighted, axis=0, keepdims=True)
        return probs.astype(bf16), (grad_scores * score_scale).astype(bf16)

    def products_of(head, probs_low, scores_low):
        rows = rows_of(head)
        scores_ref[head] = scores_low
        left[1, rows] = nn_dot(part(head, 2), probs_low).astype(bf16)
        right[0, rows] = nn_dot(part(head, 1), scores_low).astype(bf16)
        right[1, rows] = nt_dot(part(head, 0), scores_low).astype(bf16)
        right[2, rows] = nt_dot(grad_att_t[rows], probs_low).astype(bf16)

    raw, soft = {}, {}
    for turn in range(HEADS + 2):
        if turn < HEADS:
            raw[turn] = scores_of(turn)
        if turn >= 2:
            products_of(turn - 2, *soft.pop(turn - 2))
        if 1 <= turn <= HEADS:
            soft[turn - 1] = softmax_of(turn - 1, *raw.pop(turn - 1))

    odd = lax.rem(lax.axis_index("lat"), 2)

    for out_ref, half in ((send_ref, 1 - odd), (keep_ref, odd)):
        low = nt_dot(left[0], right[2 * half])
        high = nt_dot(left[half], right[2 * half + 1])
        for owner in range(packet.lon_count):
            rows = slice(owner * packet.weight_rows, (owner + 1) * packet.weight_rows)
            pieces = [
                block[rows, tile * LANES : (tile + 1) * LANES] for block in (low, high) for tile in range(3)
            ]
            if packet.weight_size > packet.weight_used:
                pieces.append(jnp.zeros((packet.weight_size - packet.weight_used, LANES), f32))
            first = owner * packet.weight_size
            out_ref[first : first + packet.weight_size] = jnp.concatenate(pieces, axis=0).astype(bf16)


def field_kernel(
    win_ref,
    grad_projected_ref,
    normalized_ref,
    inv_std_ref,
    cot_ref,
    gain_ref,
    place_t_ref,
    eye_ref,
    back_own_ref,
    back_near_ref,
    back_lat_ref,
    gain_out_ref,
):
    features = win_ref.shape[0]
    grad_shifted_t = sum(
        nn_dot(win_ref[:, block * features : (block + 1) * features], grad_projected_ref[block]) for block in range(3)
    ).astype(bf16)
    grad_normed = nt_dot(eye_ref[:CELLS, :CELLS], grad_shifted_t)
    normalized = normalized_ref[...]
    scaled = grad_normed * gain_ref[...].reshape(1, features)
    grad_field = cot_ref[...].astype(f32) + inv_std_ref[...] * (
        scaled
        - jnp.mean(scaled, axis=-1, keepdims=True)
        - normalized * jnp.mean(scaled * normalized, axis=-1, keepdims=True)
    )
    back = nn_dot(place_t_ref[...], grad_field.astype(bf16))
    quarters = [back[quarter * QUARTER : (quarter + 1) * QUARTER] for quarter in range(4)]
    back_own_ref[...] = quarters[1].astype(bf16)
    back_near_ref[...] = jnp.concatenate(quarters[::2], axis=0).astype(bf16)
    back_lat_ref[...] = quarters[3].astype(bf16)
    gain_sum = jnp.sum(grad_normed * normalized, axis=0, keepdims=True)
    gain_rows = [gain_sum[:, tile * LANES : (tile + 1) * LANES] for tile in range(3)]
    gain_out_ref[...] = jnp.concatenate(gain_rows + [jnp.zeros((13, LANES), f32)], axis=0).astype(bf16)


def fold_kernel(packet, scores_ref, lanes_ref, rows_ref, out_ref, wide, table, flat):
    wide[...] = jnp.zeros(wide.shape, f32)
    table[...] = jnp.zeros(table.shape, f32)
    flat[...] = jnp.zeros(flat.shape, bf16)
    for head in range(HEADS):
        wide[head % 2, :, :CELLS] = scores_ref[head].astype(f32)
        total = wide[head % 2, :PLANE, :]
        for col in range(1, WIN_LON):
            total = pltpu.roll(total, PLANE, 1) + wide[head % 2, PLANE * col : PLANE * (col + 1), :]
        table[16 * head : 16 * head + PLANE, :] = total
    moved = nn_dot(rows_ref[...], table[...].astype(bf16)).astype(bf16)
    moved = nt_dot(moved, lanes_ref[...]).astype(bf16)
    reach = SPAN // PLANE
    for first, plane_i, plane_j in segments():
        flat[:, first : first + reach] = moved[16 * plane_j : 16 * (plane_j + 1), reach * plane_i : reach * (plane_i + 1)]
    tiles = [
        flat[:, tile * LANES : (tile + 1) * LANES].astype(f32)[:HEADS] for tile in range(packet.table_tiles)
    ]
    tiles.append(jnp.zeros((packet.table_size - packet.table_rows, LANES), f32))
    out_ref[...] = jnp.concatenate(tiles, axis=0).astype(bf16)


def first_exchange_kernel(packet, keep_ref, recv_ref, table_ref, *out_refs):
    low = lax.rem(lax.axis_index("lon"), 4)
    size, quarter = packet.weight_size, packet.quarter
    for step, out_ref in enumerate(out_refs):
        digit = lax.bitwise_xor(low, step)
        for upper in range(packet.lon_count // 4):
            rows = pl.ds(pl.multiple_of((upper * 4 + digit) * size, 16), size)
            out_ref[upper * size : (upper + 1) * size] = keep_ref[rows] + recv_ref[rows]
        first = packet.lon_count // 4 * size
        out_ref[first:] = table_ref[pl.ds(pl.multiple_of(digit * quarter, 16), quarter)]


def summed(refs, rows):
    terms = [ref[rows] for ref in refs]
    while len(terms) > 1:
        terms = [left + right for left, right in zip(terms[::2], terms[1::2])]
    return terms[0]


def next_exchange_kernel(packet, shift, gains, *refs):
    gain_refs, held, out_refs = refs[:gains], refs[gains:-4], refs[-4:]
    size, quarter = packet.weight_size, packet.quarter
    digit = lax.rem(lax.shift_right_logical(lax.axis_index("lon"), shift), 4)
    groups = (out_refs[0].shape[0] - quarter - 16) // size
    rest = 4 * groups * size
    table = summed(held, slice(rest, rest + quarter))
    gain = summed(gain_refs, slice(0, 16)) if gains else summed(held, slice(rest + quarter, rest + quarter + 16))
    for step, out_ref in enumerate(out_refs):
        for upper in range(groups):
            owner = upper * 4 + lax.bitwise_xor(digit, step)
            out_ref[upper * size : (upper + 1) * size] = summed(held, pl.ds(pl.multiple_of(owner * size, 16), size))
        out_ref[groups * size : groups * size + quarter] = table
        out_ref[groups * size + quarter :] = gain


def last_sum_kernel(packet, a_ref, b_ref, c_ref, d_ref, upper_ref, lower_ref, table_ref):
    refs, cut = (a_ref, b_ref, c_ref, d_ref), upper_ref.shape[0]
    upper_ref[...] = summed(refs, slice(0, cut))
    lower_ref[...] = summed(refs, slice(cut, packet.weight_size))
    table_ref[...] = summed(refs, slice(packet.weight_size, packet.weight_size + packet.quarter + 16))


def weights_out_kernel(packet, factor, upper_ref, lower_ref, other_upper_ref, other_lower_ref, grad_in_ref, grad_out_ref):
    odd = lax.rem(lax.axis_index("lat"), 2) == 1
    own = jnp.concatenate([upper_ref[...], lower_ref[...]], axis=0).astype(f32) * factor
    other = jnp.concatenate([other_upper_ref[...], other_lower_ref[...]], axis=0).astype(f32) * factor
    halves = (jnp.where(odd, other, own), jnp.where(odd, own, other))
    size = packet.weight_rows
    tiles = [half[tile * size : (tile + 1) * size] for half in halves for tile in range(6)]
    grad_in_ref[...] = jnp.concatenate(tiles[:9], axis=1).astype(bf16)
    grad_out_ref[...] = jnp.concatenate(tiles[9:], axis=1).astype(bf16)


def table_out_kernel(packet, table_scale, factor, a_ref, b_ref, c_ref, d_ref, grad_table_ref, grad_gain_ref, quarters):
    low = lax.rem(lax.axis_index("lon"), 4)
    parts = (a_ref, b_ref, c_ref, d_ref)
    for step, ref in enumerate(parts):
        quarters[lax.bitwise_xor(low, step)] = ref[: packet.quarter].astype(f32)
    total = quarters[...].reshape(packet.table_size, LANES)
    for tile in range(packet.table_tiles):
        first = tile * LANES
        width = min(LANES, grad_table_ref.shape[2] - first)
        block = total[HEADS * tile : HEADS * (tile + 1), :width] * table_scale
        for head in range(HEADS):
            grad_table_ref[head, :, first : first + width] = block[head : head + 1]
    gain = sum(ref[packet.quarter :].astype(f32) for ref in parts) * factor
    grad_gain_ref[...] = jnp.concatenate([gain[tile : tile + 1] for tile in range(3)], axis=1).reshape(
        grad_gain_ref.shape
    )


def whole(count):
    return [pl.BlockSpec(memory_space=pltpu.VMEM)] * count


def call(kernel, name, in_specs, outs, scratch=(), flops=0, moved=0):
    return pl.pallas_call(
        kernel,
        name=name,
        out_shape=outs,
        in_specs=in_specs,
        out_specs=jax.tree.map(lambda _: pl.BlockSpec(memory_space=pltpu.VMEM), outs),
        scratch_shapes=list(scratch),
        compiler_params=pltpu.CompilerParams(vmem_limit_bytes=20 * 1024 * 1024),
        cost_estimate=pl.CostEstimate(flops=flops, bytes_accessed=moved, transcendentals=0),
    )


def on_device(lon_count, lat_count, latent_field, cotangent, norm_gain, input_weight, output_weight, bias_table, regions):
    features = latent_field.shape[3]
    head_dim = features // HEADS
    packet = Packet(lon_count, features)

    def move(value, lon_step, lat_step):
        pairs = []
        for lon in range(lon_count):
            for lat in range(lat_count):
                target = ((lon + lon_step) % lon_count) * lat_count + (lat + lat_step) % lat_count
                pairs.append((lon * lat_count + lat, target))
        return lax.ppermute(value, ("lon", "lat"), pairs)

    def swap(value, axis, mask):
        count = lon_count if axis == "lon" else lat_count
        return lax.ppermute(value, axis, [(source, source ^ mask) for source in range(count)])

    struct = jax.ShapeDtypeStruct
    def in_hbm(*arrays):
        return [pltpu.with_memory_space_constraint(array, pltpu.HBM) for array in arrays]

    def space_for(array):
        return pltpu.VMEM(array.shape, array.dtype)

    hbm = pl.BlockSpec(memory_space=pltpu.HBM)
    field, cot = jnp.transpose(latent_field, (1, 2, 0, 3)), jnp.transpose(cotangent, (1, 2, 0, 3))
    small = (jnp.transpose(regions, (1, 0, 2)), bias_table[0], norm_gain)
    same, others = struct((SAME, features), bf16), struct((2 * QUARTER, features), bf16)
    own, far, far_others, to_lat, table, gain = call(
        load_kernel,
        "load",
        [hbm] * 5,
        [others, same, others, others] + [struct(array.shape, array.dtype) for array in small[1:]],
        [space_for(field), space_for(cot), space_for(small[0]), pltpu.SemaphoreType.DMA((5,))],
        moved=1 << 20,
    )(*in_hbm(field, cot, *small))
    from_near = move(far, 1, 0)
    from_near_diag = move(far_others, 1, -1)
    from_lat = move(to_lat, 0, -1)

    bias_full, input_weight_t, lane_moves, row_moves, eye, place, place_t, weight_in, weight_out = call(
        bias_kernel,
        "expand_bias",
        whole(1) + [hbm] * 2,
        [
            struct((HEADS, CELLS, CELLS), bf16),
            struct((features, features), bf16),
            struct((WIDE, WIDE), bf16),
            struct((HEADS * 16, HEADS * 16), bf16),
            struct((features, features), bf16),
            struct((2 * CELLS, 2 * CELLS), bf16),
            struct((CELLS, CELLS), bf16),
            struct(input_weight.shape, bf16),
            struct(output_weight.shape, bf16),
        ],
        [
            pltpu.VMEM((HEADS * 16, WIDE), f32),
            pltpu.VMEM((HEADS, CELLS, CELLS), f32),
            pltpu.SemaphoreType.DMA((2,)),
        ],
        moved=1 << 21,
    )(table, *in_hbm(input_weight, output_weight))

    half_sum = struct((lon_count * packet.weight_size, LANES), bf16)
    results = call(
        functools.partial(window_kernel, packet),
        "window",
        whole(10),
        [
            half_sum,
            half_sum,
            struct((HEADS, CELLS, CELLS), bf16),
            struct((4, features, CELLS), bf16),
            struct((CELLS, features), f32),
            struct((CELLS, 1), f32),
            struct((CELLS, features), bf16),
        ],
        [pltpu.VMEM((2, features, CELLS), bf16)],
        flops=10**9,
        moved=5 << 20,
    )(
            own,
        from_near,
        from_near_diag,
        from_lat,
        gain,
        weight_in,
        input_weight_t,
        weight_out,
        bias_full,
        place,
    )
    keep, send, scores_low, *saved = results

    received = swap(send, "lat", 1)
    table_part = call(
        functools.partial(fold_kernel, packet),
        "fold_table",
        whole(3),
        struct((packet.table_size, LANES), bf16),
        [
            pltpu.VMEM((2, CELLS, WIDE), f32),
            pltpu.VMEM((HEADS * 16, WIDE), f32),
            pltpu.VMEM((16, packet.table_tiles * LANES), bf16),
        ],
        moved=1 << 21,
    )(scores_low, lane_moves, row_moves)

    groups = lon_count // 4
    parts = call(
        functools.partial(first_exchange_kernel, packet),
        "add_lat",
        whole(3),
        [struct((groups * packet.weight_size + packet.quarter, LANES), bf16)] * 4,
        moved=2 << 20,
    )(keep, received, table_part)
    parts, saved = lax.optimization_barrier((parts, saved))

    def trade(parts, shift):
        return [swap(parts[step], "lon", step << shift) for step in (3, 2, 1)] + [parts[0]]

    held = trade(parts, 0)
    piece = struct((QUARTER, features), bf16)
    back_own, back_near, back_lat, gain_part = call(
        field_kernel,
        "grad_field",
        whole(8),
        [piece, others, piece, struct((16, LANES), bf16)],
        flops=10**8,
        moved=5 << 20,
    )(weight_in, *saved, gain, place_t, eye)
    home_lat = move(back_lat, 0, 1)
    gain_other = swap(gain_part, "lat", 1)
    held, home_lat, gain_other = lax.optimization_barrier((held, home_lat, gain_other))
    gains = [gain_part, gain_other]
    home_near = move(back_near, -1, 0)
    home_diag = move(home_near, 0, 1)
    for shift in range(2, lon_count.bit_length() - 1, 2):
        groups //= 4
        parts = call(
            functools.partial(next_exchange_kernel, packet, shift, len(gains)),
            "add_lon",
            whole(len(gains) + 4),
            [struct((groups * packet.weight_size + packet.quarter + 16, LANES), bf16)] * 4,
            moved=1 << 20,
        )(*gains, *held)
        gains = []
        held = trade(parts, shift)
    cut = rounded_up(packet.weight_size // 2, 16)
    *weight_sums, table_sum = call(
        functools.partial(last_sum_kernel, packet),
        "add_last",
        whole(4),
        [struct((rows, LANES), bf16) for rows in (cut, packet.weight_size - cut, packet.quarter + 16)],
        moved=1 << 18,
    )(*held)
    table_parts = trade([table_sum] * 4, 0)[::-1]
    for bit in range(1, lat_count.bit_length() - 1):
        weight_sums = [part + swap(part, "lat", 1 << bit) for part in weight_sums]
    weight_others = [swap(part, "lat", 1) for part in weight_sums]

    cells_in_all = latent_field.shape[0] * latent_field.shape[1] * latent_field.shape[2]
    factor = 1.0 / math.sqrt(cells_in_all * lon_count * lat_count)
    grad_input_weight, grad_output_weight = call(
        functools.partial(weights_out_kernel, packet, factor),
        "weights_out",
        whole(4),
        [struct((packet.weight_rows, 3 * features), bf16), struct((packet.weight_rows, features), bf16)],
        moved=1 << 18,
    )(*weight_sums, *weight_others)
    table_parts, grad_input_weight = lax.optimization_barrier((table_parts, grad_input_weight))
    grad_table, gain_sum = call(
        functools.partial(table_out_kernel, packet, math.sqrt(head_dim), factor),
        "table_out",
        whole(4),
        [struct((HEADS, 1, PLANE * SPAN), f32), struct((features,), f32)],
        [pltpu.VMEM((4, packet.quarter, LANES), f32)],
        moved=1 << 19,
    )(*table_parts)
    for bit in range(1, lat_count.bit_length() - 1):
        gain_sum = gain_sum + swap(gain_sum, "lat", 1 << bit)

    grad_field = call(
        unpack_kernel,
        "unpack_quarters",
        whole(4),
        struct((WIN_LAT, WIN_LON, LEV, features), bf16),
        moved=4 << 20,
    )(back_own, home_near, home_lat, home_diag)
    return (
        jnp.transpose(grad_field, (2, 0, 1, 3)),
        grad_input_weight,
        grad_output_weight,
        gain_sum,
        jnp.transpose(grad_table, (1, 0, 2)),
    )


def solution(mesh):
    in_specs = (
        P(None, "lat", "lon", None),
        P(None, "lat", "lon", None),
        P(),
        P(),
        P(),
        P("lat", None, None),
        P(None, "lat", "lon"),
    )
    out_specs = (
        P(None, "lat", "lon", None),
        P("lon", None),
        P("lon", None),
        P(),
        P("lat", None, None),
    )
    return jax.shard_map(
        functools.partial(on_device, mesh.shape["lon"], mesh.shape["lat"]),
        mesh=mesh,
        in_specs=in_specs,
        out_specs=out_specs,
        check_vma=False,
    )
```

```python
import functools
import math

import jax
import jax.numpy as jnp
from jax import lax
from jax.experimental import pallas as pl
from jax.experimental.pallas import tpu as pltpu
from jax.sharding import PartitionSpec as P

HEADS = 12
LEV = 2
WIN_LAT = 6
WIN_LON = 12
PLANE = LEV * WIN_LAT
CELLS = PLANE * WIN_LON
SPAN = (2 * WIN_LON - 1) * PLANE
WIDE = 384
LANES = 128
QUARTER = LEV * (WIN_LAT // 2) * (WIN_LON // 2)

norm_eps = 1e-05
masked_score = -1000000000.0
f32 = jnp.float32
bf16 = jnp.bfloat16

QUARTERS = ((0, 0), (0, 1), (1, 0), (1, 1))


def segments():
    reach = SPAN // PLANE
    first = 0
    for level_i in range(LEV):
        for level_j in range(LEV):
            for row_i in range(WIN_LAT):
                for row_j in range(WIN_LAT):
                    yield first, level_i * WIN_LAT + row_i, level_j * WIN_LAT + row_j
                    first += reach


def rounded_up(value, step):
    return -(-value // step) * step


class Packet:
    def __init__(self, lon_count, features):
        self.lon_count = lon_count
        self.weight_rows = features // lon_count
        self.weight_used = 6 * self.weight_rows
        self.weight_size = rounded_up(self.weight_used, 16)
        self.table_tiles = -(-PLANE * SPAN // LANES)
        self.table_rows = HEADS * self.table_tiles
        self.table_size = rounded_up(self.table_rows, 4 * 16)
        self.quarter = self.table_size // 4


def nt_dot(left, right):
    return lax.dot_general(left, right, (((1,), (1,)), ((), ())), preferred_element_type=f32)


def nn_dot(left, right):
    return jnp.dot(left, right, preferred_element_type=f32)


def fetch(sources, targets, sems):
    copies = [pltpu.make_async_copy(src, dst, sems.at[at]) for at, (src, dst) in enumerate(zip(sources, targets))]
    for copy in copies:
        copy.start()
    return copies


SAME = 80


def load_kernel(field_src, cot_src, *refs):
    sources, out_refs, (table_ref, gain_ref) = refs[:3], refs[3:7], refs[7:9]
    field_ref, cot_ref, regions_ref, sems = refs[9:]
    copies = fetch((field_src, cot_src) + sources, (field_ref, cot_ref, regions_ref, table_ref, gain_ref), sems)
    for copy in copies[:3]:
        copy.wait()
    half_rows, half_cols = WIN_LAT // 2, WIN_LON // 2
    features = field_ref.shape[3]
    ids = [regions_ref[row, level : level + 1, :].astype(f32) for level in range(LEV) for row in range(WIN_LAT)]
    ids.append(jnp.zeros((1, features - CELLS), f32))
    tail = jnp.concatenate([jnp.concatenate(ids, axis=1), jnp.zeros((SAME - 2 * QUARTER - 1, features), f32)], axis=0)
    wanted = ((half_rows, 0), (half_rows, half_cols), (0, half_cols), (0, 0))
    for (first_row, first_col), out_ref in zip(wanted, out_refs):
        pieces = [
            ref[first_row + row, first_col + col].astype(f32)
            for ref in (field_ref, cot_ref)
            for row in range(half_rows)
            for col in range(half_cols)
        ]
        if out_ref.shape[0] == SAME:
            pieces.append(tail)
        out_ref[...] = jnp.concatenate(pieces, axis=0).astype(bf16)
    for copy in copies[3:]:
        copy.wait()


def one_hot(flags):
    return flags.astype(f32).astype(bf16)


def counted(shape, axis):
    return lax.broadcasted_iota(jnp.int32, shape, axis)


def cell_source(cell, stride):
    col, level, row = lax.div(cell, PLANE), lax.rem(lax.div(cell, WIN_LAT), LEV), lax.rem(cell, WIN_LAT)
    half_rows, half_cols = WIN_LAT // 2, WIN_LON // 2
    quarter = 2 * lax.div(row, half_rows) + lax.div(col, half_cols)
    place = lax.rem(row, half_rows) * half_cols + lax.rem(col, half_cols)
    return quarter * stride + place * LEV + lax.rem(level + LEV // 2, LEV)


def unpack_kernel(own_ref, near_ref, lat_ref, near_diag_ref, out_ref):
    half_rows, half_cols = WIN_LAT // 2, WIN_LON // 2
    quarters = (
        near_ref[...].astype(f32)[:QUARTER],
        own_ref[...].astype(f32),
        near_diag_ref[...].astype(f32)[QUARTER:],
        lat_ref[...].astype(f32),
    )
    for (lat_half, lon_half), cells in zip(QUARTERS, quarters):
        first_row, first_col = (1 - lat_half) * half_rows, (1 - lon_half) * half_cols
        for row in range(half_rows):
            for col in range(half_cols):
                first = (row * half_cols + col) * LEV
                out_ref[first_row + row, first_col + col] = cells[first : first + LEV].astype(bf16)


def bias_kernel(
    table_ref,
    win_src,
    wout_src,
    out_ref,
    win_t_ref,
    lanes_ref,
    rows_ref,
    eye_ref,
    place_ref,
    place_t_ref,
    win_ref,
    wout_ref,
    stage,
    full,
    sems,
):
    copies = fetch((win_src, wout_src), (win_ref, wout_ref), sems)
    features = win_ref.shape[0]
    square = (features, features)
    eye = one_hot(counted(square, 0) == counted(square, 1))
    eye_ref[...] = eye
    place_ref[...] = one_hot(cell_source(counted((CELLS, 1), 0), QUARTER) == counted((CELLS, CELLS), 1))
    place_t_ref[...] = one_hot(cell_source(counted((1, CELLS), 1), QUARTER) == counted((CELLS, CELLS), 0))
    lane = counted((1, WIDE), 1)
    target = jnp.where(lane < SPAN, lax.rem(lane, PLANE) * (SPAN // PLANE) + lax.div(lane, PLANE), -1)
    lanes_ref[...] = one_hot(target == counted((WIDE, WIDE), 0))
    sixteens = HEADS * 16
    row = counted((sixteens, 1), 0)
    target = jnp.where(lax.rem(row, 16) < PLANE, lax.rem(row, 16) * 16 + lax.div(row, 16), -1)
    rows_ref[...] = one_hot(target == counted((sixteens, sixteens), 1))

    stage[...] = jnp.zeros(stage.shape, f32)
    reach = SPAN // PLANE
    table = table_ref[...].astype(f32)
    for first, plane_i, plane_j in segments():
        stage[16 * plane_j : 16 * plane_j + HEADS, reach * plane_i : reach * (plane_i + 1)] = table[
            :, first : first + reach
        ]
    moved = nn_dot(stage[...].astype(bf16), lanes_ref[...]).astype(bf16)
    rows = nn_dot(rows_ref[...], moved)

    for col in range(WIN_LON):
        shift = PLANE * (WIN_LON - 1 - col)
        moved = rows if shift == 0 else pltpu.roll(rows, WIDE - shift, 1)
        for head in range(HEADS):
            full[head, PLANE * col : PLANE * (col + 1), :] = moved[16 * head : 16 * head + PLANE, :CELLS]
    for head in range(HEADS):
        out_ref[head] = full[head].astype(bf16)
    for copy in copies:
        copy.wait()
    win_t_ref[...] = nt_dot(eye, win_ref[:, :features]).astype(bf16)


def window_kernel(
    packet,
    own_ref,
    near_ref,
    near_diag_ref,
    lat_ref,
    gain_ref,
    win_ref,
    win_t_ref,
    wout_ref,
    bias_ref,
    place_ref,
    keep_ref,
    send_ref,
    scores_ref,
    right,
    normalized_ref,
    inv_std_ref,
    cot_ref,
    left,
):
    features = win_ref.shape[0]
    head_dim = features // HEADS
    group_heads = LANES // head_dim
    score_scale = head_dim ** (-0.5)
    near = near_ref[...].astype(f32)
    quarters = (near, own_ref[...].astype(f32), near_diag_ref[...].astype(f32), lat_ref[...].astype(f32))
    sides = [jnp.concatenate([quarter[at : at + QUARTER] for quarter in quarters], axis=0) for at in (0, QUARTER)]
    cell, lane = counted((CELLS, CELLS), 0), counted((CELLS, CELLS), 1)
    source = lax.rem(cell, PLANE) * WIN_LON + lax.div(cell, PLANE)
    ids = near[2 * QUARTER : 2 * QUARTER + 1, :CELLS]
    region_col = jnp.sum(jnp.where(source == lane, ids, 0.0), axis=1, keepdims=True)
    region_row = jnp.sum(jnp.where(cell == lane, region_col, 0.0), axis=0, keepdims=True)
    same = region_col == region_row
    placed = nn_dot(place_ref[...], jnp.concatenate(sides, axis=1).astype(bf16))
    field, cot_f32 = placed[:, :features], placed[:, features:]
    cot = cot_f32.astype(bf16)
    cot_ref[...] = cot
    gain = gain_ref[...].reshape(1, features)

    centred = field - jnp.mean(field, axis=-1, keepdims=True)
    inv_std = lax.rsqrt(jnp.mean(centred * centred, axis=-1, keepdims=True) + norm_eps)
    normalized = centred * inv_std
    normalized_ref[...] = normalized
    inv_std_ref[...] = inv_std
    normed = (normalized * gain).astype(bf16)

    query_t = nt_dot(win_t_ref[...], normed).astype(bf16)
    wide_keys_values = nn_dot(normed, win_ref[:, features:])
    keys_values = wide_keys_values.astype(bf16)
    grad_att_t = nt_dot(wout_ref[...], cot).astype(bf16)
    key_value_t = jnp.transpose(wide_keys_values).astype(bf16)
    left[0] = jnp.transpose(normed.astype(f32)).astype(bf16)
    right[3] = jnp.transpose(cot_f32).astype(bf16)

    def spread(head_rows, slot):
        parts = []
        if slot:
            parts.append(jnp.zeros((slot * head_dim, CELLS), bf16))
        parts.append(head_rows)
        if slot < group_heads - 1:
            parts.append(jnp.zeros(((group_heads - 1 - slot) * head_dim, CELLS), bf16))
        return jnp.concatenate(parts, axis=0)

    def rows_of(head):
        return slice(head * head_dim, (head + 1) * head_dim)

    def part(head, index):
        if index == 0:
            return query_t[rows_of(head)]
        first = (index - 1) * features + head * head_dim
        return key_value_t[first : first + head_dim]

    def scores_of(head):
        group, slot = divmod(head, group_heads)
        keys = keys_values[:, group * LANES : (group + 1) * LANES]
        values = keys_values[:, features + group * LANES : features + (group + 1) * LANES]
        scores = nn_dot(keys, spread(part(head, 0), slot))
        return scores, nn_dot(values, spread(grad_att_t[rows_of(head)], slot))

    def softmax_of(head, scores, grad_probs):
        scores = jnp.where(same, scores * score_scale + bias_ref[head].astype(f32), masked_score)
        grown = jnp.exp(scores - jnp.max(scores, axis=0, keepdims=True))
        probs = grown * (1.0 / jnp.sum(grown, axis=0, keepdims=True))
        weighted = probs * grad_probs
        grad_scores = weighted - probs * jnp.sum(weighted, axis=0, keepdims=True)
        return probs.astype(bf16), (grad_scores * score_scale).astype(bf16)

    def products_of(head, probs_low, scores_low):
        rows = rows_of(head)
        scores_ref[head] = scores_low
        left[1, rows] = nn_dot(part(head, 2), probs_low).astype(bf16)
        right[0, rows] = nn_dot(part(head, 1), scores_low).astype(bf16)
        right[1, rows] = nt_dot(part(head, 0), scores_low).astype(bf16)
        right[2, rows] = nt_dot(grad_att_t[rows], probs_low).astype(bf16)

    raw, soft = {}, {}
    for turn in range(HEADS + 2):
        if turn < HEADS:
            raw[turn] = scores_of(turn)
        if turn >= 2:
            products_of(turn - 2, *soft.pop(turn - 2))
        if 1 <= turn <= HEADS:
            soft[turn - 1] = softmax_of(turn - 1, *raw.pop(turn - 1))

    odd = lax.rem(lax.axis_index("lat"), 2)

    for out_ref, half in ((send_ref, 1 - odd), (keep_ref, odd)):
        low = nt_dot(left[0], right[2 * half])
        high = nt_dot(left[half], right[2 * half + 1])
        for owner in range(packet.lon_count):
            rows = slice(owner * packet.weight_rows, (owner + 1) * packet.weight_rows)
            pieces = [
                block[rows, tile * LANES : (tile + 1) * LANES] for block in (low, high) for tile in range(3)
            ]
            if packet.weight_size > packet.weight_used:
                pieces.append(jnp.zeros((packet.weight_size - packet.weight_used, LANES), f32))
            first = owner * packet.weight_size
            out_ref[first : first + packet.weight_size] = jnp.concatenate(pieces, axis=0).astype(bf16)


def field_kernel(
    win_ref,
    grad_projected_ref,
    normalized_ref,
    inv_std_ref,
    cot_ref,
    gain_ref,
    place_t_ref,
    eye_ref,
    back_own_ref,
    back_near_ref,
    back_lat_ref,
    gain_out_ref,
):
    features = win_ref.shape[0]
    grad_shifted_t = sum(
        nn_dot(win_ref[:, block * features : (block + 1) * features], grad_projected_ref[block]) for block in range(3)
    ).astype(bf16)
    grad_normed = nt_dot(eye_ref[:CELLS, :CELLS], grad_shifted_t)
    normalized = normalized_ref[...]
    scaled = grad_normed * gain_ref[...].reshape(1, features)
    grad_field = cot_ref[...].astype(f32) + inv_std_ref[...] * (
        scaled
        - jnp.mean(scaled, axis=-1, keepdims=True)
        - normalized * jnp.mean(scaled * normalized, axis=-1, keepdims=True)
    )
    back = nn_dot(place_t_ref[...], grad_field.astype(bf16))
    quarters = [back[quarter * QUARTER : (quarter + 1) * QUARTER] for quarter in range(4)]
    back_own_ref[...] = quarters[1].astype(bf16)
    back_near_ref[...] = jnp.concatenate(quarters[::2], axis=0).astype(bf16)
    back_lat_ref[...] = quarters[3].astype(bf16)
    gain_sum = jnp.sum(grad_normed * normalized, axis=0, keepdims=True)
    gain_rows = [gain_sum[:, tile * LANES : (tile + 1) * LANES] for tile in range(3)]
    gain_out_ref[...] = jnp.concatenate(gain_rows + [jnp.zeros((13, LANES), f32)], axis=0).astype(bf16)


def fold_kernel(packet, scores_ref, lanes_ref, rows_ref, out_ref, wide, table, flat):
    wide[...] = jnp.zeros(wide.shape, f32)
    table[...] = jnp.zeros(table.shape, f32)
    flat[...] = jnp.zeros(flat.shape, bf16)
    for head in range(HEADS):
        wide[head % 2, :, :CELLS] = scores_ref[head].astype(f32)
        total = wide[head % 2, :PLANE, :]
        for col in range(1, WIN_LON):
            total = pltpu.roll(total, PLANE, 1) + wide[head % 2, PLANE * col : PLANE * (col + 1), :]
        table[16 * head : 16 * head + PLANE, :] = total
    moved = nn_dot(rows_ref[...], table[...].astype(bf16)).astype(bf16)
    moved = nt_dot(moved, lanes_ref[...]).astype(bf16)
    reach = SPAN // PLANE
    for first, plane_i, plane_j in segments():
        flat[:, first : first + reach] = moved[16 * plane_j : 16 * (plane_j + 1), reach * plane_i : reach * (plane_i + 1)]
    tiles = [
        flat[:, tile * LANES : (tile + 1) * LANES].astype(f32)[:HEADS] for tile in range(packet.table_tiles)
    ]
    tiles.append(jnp.zeros((packet.table_size - packet.table_rows, LANES), f32))
    out_ref[...] = jnp.concatenate(tiles, axis=0).astype(bf16)


def first_exchange_kernel(packet, keep_ref, recv_ref, table_ref, *out_refs):
    low = lax.rem(lax.axis_index("lon"), 4)
    size, quarter = packet.weight_size, packet.quarter
    for step, out_ref in enumerate(out_refs):
        digit = lax.bitwise_xor(low, step)
        for upper in range(packet.lon_count // 4):
            rows = pl.ds(pl.multiple_of((upper * 4 + digit) * size, 16), size)
            out_ref[upper * size : (upper + 1) * size] = keep_ref[rows] + recv_ref[rows]
        first = packet.lon_count // 4 * size
        out_ref[first:] = table_ref[pl.ds(pl.multiple_of(digit * quarter, 16), quarter)]


def summed(refs, rows):
    terms = [ref[rows] for ref in refs]
    while len(terms) > 1:
        terms = [left + right for left, right in zip(terms[::2], terms[1::2])]
    return terms[0]


def next_exchange_kernel(packet, shift, gains, *refs):
    gain_refs, held, out_refs = refs[:gains], refs[gains:-4], refs[-4:]
    size, quarter = packet.weight_size, packet.quarter
    digit = lax.rem(lax.shift_right_logical(lax.axis_index("lon"), shift), 4)
    groups = (out_refs[0].shape[0] - quarter - 16) // size
    rest = 4 * groups * size
    table = summed(held, slice(rest, rest + quarter))
    gain = summed(gain_refs, slice(0, 16)) if gains else summed(held, slice(rest + quarter, rest + quarter + 16))
    for step, out_ref in enumerate(out_refs):
        for upper in range(groups):
            owner = upper * 4 + lax.bitwise_xor(digit, step)
            out_ref[upper * size : (upper + 1) * size] = summed(held, pl.ds(pl.multiple_of(owner * size, 16), size))
        out_ref[groups * size : groups * size + quarter] = table
        out_ref[groups * size + quarter :] = gain


def last_sum_kernel(packet, a_ref, b_ref, c_ref, d_ref, upper_ref, lower_ref, table_ref):
    refs, cut = (a_ref, b_ref, c_ref, d_ref), upper_ref.shape[0]
    upper_ref[...] = summed(refs, slice(0, cut))
    lower_ref[...] = summed(refs, slice(cut, packet.weight_size))
    table_ref[...] = summed(refs, slice(packet.weight_size, packet.weight_size + packet.quarter + 16))


def weights_out_kernel(packet, factor, upper_ref, lower_ref, other_upper_ref, other_lower_ref, grad_in_ref, grad_out_ref):
    odd = lax.rem(lax.axis_index("lat"), 2) == 1
    own = jnp.concatenate([upper_ref[...], lower_ref[...]], axis=0).astype(f32) * factor
    other = jnp.concatenate([other_upper_ref[...], other_lower_ref[...]], axis=0).astype(f32) * factor
    halves = (jnp.where(odd, other, own), jnp.where(odd, own, other))
    size = packet.weight_rows
    tiles = [half[tile * size : (tile + 1) * size] for half in halves for tile in range(6)]
    grad_in_ref[...] = jnp.concatenate(tiles[:9], axis=1).astype(bf16)
    grad_out_ref[...] = jnp.concatenate(tiles[9:], axis=1).astype(bf16)


def table_out_kernel(packet, table_scale, factor, a_ref, b_ref, c_ref, d_ref, grad_table_ref, grad_gain_ref, quarters):
    low = lax.rem(lax.axis_index("lon"), 4)
    parts = (a_ref, b_ref, c_ref, d_ref)
    for step, ref in enumerate(parts):
        quarters[lax.bitwise_xor(low, step)] = ref[: packet.quarter].astype(f32)
    total = quarters[...].reshape(packet.table_size, LANES)
    for tile in range(packet.table_tiles):
        first = tile * LANES
        width = min(LANES, grad_table_ref.shape[2] - first)
        block = total[HEADS * tile : HEADS * (tile + 1), :width] * table_scale
        for head in range(HEADS):
            grad_table_ref[head, :, first : first + width] = block[head : head + 1]
    gain = sum(ref[packet.quarter :].astype(f32) for ref in parts) * factor
    grad_gain_ref[...] = jnp.concatenate([gain[tile : tile + 1] for tile in range(3)], axis=1).reshape(
        grad_gain_ref.shape
    )


def whole(count):
    return [pl.BlockSpec(memory_space=pltpu.VMEM)] * count


def call(kernel, name, in_specs, outs, scratch=(), flops=0, moved=0):
    return pl.pallas_call(
        kernel,
        name=name,
        out_shape=outs,
        in_specs=in_specs,
        out_specs=jax.tree.map(lambda _: pl.BlockSpec(memory_space=pltpu.VMEM), outs),
        scratch_shapes=list(scratch),
        compiler_params=pltpu.CompilerParams(vmem_limit_bytes=20 * 1024 * 1024),
        cost_estimate=pl.CostEstimate(flops=flops, bytes_accessed=moved, transcendentals=0),
    )


def on_device(lon_count, lat_count, latent_field, cotangent, norm_gain, input_weight, output_weight, bias_table, regions):
    features = latent_field.shape[3]
    head_dim = features // HEADS
    packet = Packet(lon_count, features)

    def move(value, lon_step, lat_step):
        pairs = []
        for lon in range(lon_count):
            for lat in range(lat_count):
                target = ((lon + lon_step) % lon_count) * lat_count + (lat + lat_step) % lat_count
                pairs.append((lon * lat_count + lat, target))
        return lax.ppermute(value, ("lon", "lat"), pairs)

    def swap(value, axis, mask):
        count = lon_count if axis == "lon" else lat_count
        return lax.ppermute(value, axis, [(source, source ^ mask) for source in range(count)])

    struct = jax.ShapeDtypeStruct
    def in_hbm(*arrays):
        return [pltpu.with_memory_space_constraint(array, pltpu.HBM) for array in arrays]

    def space_for(array):
        return pltpu.VMEM(array.shape, array.dtype)

    hbm = pl.BlockSpec(memory_space=pltpu.HBM)
    field, cot = jnp.transpose(latent_field, (1, 2, 0, 3)), jnp.transpose(cotangent, (1, 2, 0, 3))
    small = (jnp.transpose(regions, (1, 0, 2)), bias_table[0], norm_gain)
    same, others = struct((SAME, features), bf16), struct((2 * QUARTER, features), bf16)
    own, far, far_others, to_lat, table, gain = call(
        load_kernel,
        "load",
        [hbm] * 5,
        [others, same, others, others] + [struct(array.shape, array.dtype) for array in small[1:]],
        [space_for(field), space_for(cot), space_for(small[0]), pltpu.SemaphoreType.DMA((5,))],
        moved=1 << 20,
    )(*in_hbm(field, cot, *small))
    from_near = move(far, 1, 0)
    from_near_diag = move(far_others, 1, -1)
    from_lat = move(to_lat, 0, -1)

    bias_full, input_weight_t, lane_moves, row_moves, eye, place, place_t, weight_in, weight_out = call(
        bias_kernel,
        "expand_bias",
        whole(1) + [hbm] * 2,
        [
            struct((HEADS, CELLS, CELLS), bf16),
            struct((features, features), bf16),
            struct((WIDE, WIDE), bf16),
            struct((HEADS * 16, HEADS * 16), bf16),
            struct((features, features), bf16),
            struct((CELLS, CELLS), bf16),
            struct((CELLS, CELLS), bf16),
            struct(input_weight.shape, bf16),
            struct(output_weight.shape, bf16),
        ],
        [
            pltpu.VMEM((HEADS * 16, WIDE), f32),
            pltpu.VMEM((HEADS, CELLS, CELLS), f32),
            pltpu.SemaphoreType.DMA((2,)),
        ],
        moved=1 << 21,
    )(table, *in_hbm(input_weight, output_weight))

    half_sum = struct((lon_count * packet.weight_size, LANES), bf16)
    results = call(
        functools.partial(window_kernel, packet),
        "window",
        whole(10),
        [
            half_sum,
            half_sum,
            struct((HEADS, CELLS, CELLS), bf16),
            struct((4, features, CELLS), bf16),
            struct((CELLS, features), f32),
            struct((CELLS, 1), f32),
            struct((CELLS, features), bf16),
        ],
        [pltpu.VMEM((2, features, CELLS), bf16)],
        flops=10**9,
        moved=5 << 20,
    )(
            own,
        from_near,
        from_near_diag,
        from_lat,
        gain,
        weight_in,
        input_weight_t,
        weight_out,
        bias_full,
        place,
    )
    keep, send, scores_low, *saved = results

    received = swap(send, "lat", 1)
    table_part = call(
        functools.partial(fold_kernel, packet),
        "fold_table",
        whole(3),
        struct((packet.table_size, LANES), bf16),
        [
            pltpu.VMEM((2, CELLS, WIDE), f32),
            pltpu.VMEM((HEADS * 16, WIDE), f32),
            pltpu.VMEM((16, packet.table_tiles * LANES), bf16),
        ],
        moved=1 << 21,
    )(scores_low, lane_moves, row_moves)

    groups = lon_count // 4
    parts = call(
        functools.partial(first_exchange_kernel, packet),
        "add_lat",
        whole(3),
        [struct((groups * packet.weight_size + packet.quarter, LANES), bf16)] * 4,
        moved=2 << 20,
    )(keep, received, table_part)
    parts, saved = lax.optimization_barrier((parts, saved))

    def trade(parts, shift):
        return [swap(parts[step], "lon", step << shift) for step in (3, 2, 1)] + [parts[0]]

    held = trade(parts, 0)
    piece = struct((QUARTER, features), bf16)
    back_own, back_near, back_lat, gain_part = call(
        field_kernel,
        "grad_field",
        whole(8),
        [piece, others, piece, struct((16, LANES), bf16)],
        flops=10**8,
        moved=5 << 20,
    )(weight_in, *saved, gain, place_t, eye)
    home_lat = move(back_lat, 0, 1)
    gain_other = swap(gain_part, "lat", 1)
    held, home_lat, gain_other = lax.optimization_barrier((held, home_lat, gain_other))
    gains = [gain_part, gain_other]
    home_near = move(back_near, -1, 0)
    home_diag = move(home_near, 0, 1)
    for shift in range(2, lon_count.bit_length() - 1, 2):
        groups //= 4
        parts = call(
            functools.partial(next_exchange_kernel, packet, shift, len(gains)),
            "add_lon",
            whole(len(gains) + 4),
            [struct((groups * packet.weight_size + packet.quarter + 16, LANES), bf16)] * 4,
            moved=1 << 20,
        )(*gains, *held)
        gains = []
        held = trade(parts, shift)
    cut = rounded_up(packet.weight_size // 2, 16)
    *weight_sums, table_sum = call(
        functools.partial(last_sum_kernel, packet),
        "add_last",
        whole(4),
        [struct((rows, LANES), bf16) for rows in (cut, packet.weight_size - cut, packet.quarter + 16)],
        moved=1 << 18,
    )(*held)
    table_parts = trade([table_sum] * 4, 0)[::-1]
    for bit in range(1, lat_count.bit_length() - 1):
        weight_sums = [part + swap(part, "lat", 1 << bit) for part in weight_sums]
    weight_others = [swap(part, "lat", 1) for part in weight_sums]

    cells_in_all = latent_field.shape[0] * latent_field.shape[1] * latent_field.shape[2]
    factor = 1.0 / math.sqrt(cells_in_all * lon_count * lat_count)
    grad_input_weight, grad_output_weight = call(
        functools.partial(weights_out_kernel, packet, factor),
        "weights_out",
        whole(4),
        [struct((packet.weight_rows, 3 * features), bf16), struct((packet.weight_rows, features), bf16)],
        moved=1 << 18,
    )(*weight_sums, *weight_others)
    table_parts, grad_input_weight = lax.optimization_barrier((table_parts, grad_input_weight))
    grad_table, gain_sum = call(
        functools.partial(table_out_kernel, packet, math.sqrt(head_dim), factor),
        "table_out",
        whole(4),
        [struct((HEADS, 1, PLANE * SPAN), f32), struct((features,), f32)],
        [pltpu.VMEM((4, packet.quarter, LANES), f32)],
        moved=1 << 19,
    )(*table_parts)
    for bit in range(1, lat_count.bit_length() - 1):
        gain_sum = gain_sum + swap(gain_sum, "lat", 1 << bit)

    grad_field = call(
        unpack_kernel,
        "unpack_quarters",
        whole(4),
        struct((WIN_LAT, WIN_LON, LEV, features), bf16),
        moved=4 << 20,
    )(back_own, home_near, home_lat, home_diag)
    return (
        jnp.transpose(grad_field, (2, 0, 1, 3)),
        grad_input_weight,
        grad_output_weight,
        gain_sum,
        jnp.transpose(grad_table, (1, 0, 2)),
    )


def solution(mesh):
    in_specs = (
        P(None, "lat", "lon", None),
        P(None, "lat", "lon", None),
        P(),
        P(),
        P(),
        P("lat", None, None),
        P(None, "lat", "lon"),
    )
    out_specs = (
        P(None, "lat", "lon", None),
        P("lon", None),
        P("lon", None),
        P(),
        P("lat", None, None),
    )
    return jax.shard_map(
        functools.partial(on_device, mesh.shape["lon"], mesh.shape["lat"]),
        mesh=mesh,
        in_specs=in_specs,
        out_specs=out_specs,
        check_vma=False,
    )
```

```python
import functools
import math

import jax
import jax.numpy as jnp
from jax import lax
from jax.experimental import pallas as pl
from jax.experimental.pallas import tpu as pltpu
from jax.sharding import PartitionSpec as P

HEADS = 12
LEV = 2
WIN_LAT = 6
WIN_LON = 12
PLANE = LEV * WIN_LAT
CELLS = PLANE * WIN_LON
SPAN = (2 * WIN_LON - 1) * PLANE
WIDE = 384
LANES = 128
QUARTER = LEV * (WIN_LAT // 2) * (WIN_LON // 2)

norm_eps = 1e-05
masked_score = -1000000000.0
f32 = jnp.float32
bf16 = jnp.bfloat16

QUARTERS = ((0, 0), (0, 1), (1, 0), (1, 1))


def segments():
    reach = SPAN // PLANE
    first = 0
    for level_i in range(LEV):
        for level_j in range(LEV):
            for row_i in range(WIN_LAT):
                for row_j in range(WIN_LAT):
                    yield first, level_i * WIN_LAT + row_i, level_j * WIN_LAT + row_j
                    first += reach


def rounded_up(value, step):
    return -(-value // step) * step


class Packet:
    def __init__(self, lon_count, features):
        self.lon_count = lon_count
        self.weight_rows = features // lon_count
        self.weight_used = 6 * self.weight_rows
        self.weight_size = rounded_up(self.weight_used, 16)
        self.table_tiles = -(-PLANE * SPAN // LANES)
        self.table_rows = HEADS * self.table_tiles
        self.table_size = rounded_up(self.table_rows, 4 * 16)
        self.quarter = self.table_size // 4


def nt_dot(left, right):
    return lax.dot_general(left, right, (((1,), (1,)), ((), ())), preferred_element_type=f32)


def nn_dot(left, right):
    return jnp.dot(left, right, preferred_element_type=f32)


def fetch(sources, targets, sems):
    copies = [pltpu.make_async_copy(src, dst, sems.at[at]) for at, (src, dst) in enumerate(zip(sources, targets))]
    for copy in copies:
        copy.start()
    return copies


SAME = 80


def load_kernel(field_src, cot_src, *refs):
    sources, out_refs, (table_ref, gain_ref) = refs[:3], refs[3:7], refs[7:9]
    field_ref, cot_ref, regions_ref, sems = refs[9:]
    copies = fetch((field_src, cot_src) + sources, (field_ref, cot_ref, regions_ref, table_ref, gain_ref), sems)
    for copy in copies[:3]:
        copy.wait()
    half_rows, half_cols = WIN_LAT // 2, WIN_LON // 2
    features = field_ref.shape[3]
    ids = [regions_ref[row, level : level + 1, :].astype(f32) for level in range(LEV) for row in range(WIN_LAT)]
    ids.append(jnp.zeros((1, features - CELLS), f32))
    tail = jnp.concatenate([jnp.concatenate(ids, axis=1), jnp.zeros((SAME - 2 * QUARTER - 1, features), f32)], axis=0)
    wanted = ((half_rows, 0), (half_rows, half_cols), (0, half_cols), (0, 0))
    for (first_row, first_col), out_ref in zip(wanted, out_refs):
        pieces = [
            ref[first_row + row, first_col + col].astype(f32)
            for ref in (field_ref, cot_ref)
            for row in range(half_rows)
            for col in range(half_cols)
        ]
        if out_ref.shape[0] == SAME:
            pieces.append(tail)
        out_ref[...] = jnp.concatenate(pieces, axis=0).astype(bf16)
    for copy in copies[3:]:
        copy.wait()


def one_hot(flags):
    return flags.astype(f32).astype(bf16)


def counted(shape, axis):
    return lax.broadcasted_iota(jnp.int32, shape, axis)


def cell_source(cell, stride):
    col, level, row = lax.div(cell, PLANE), lax.rem(lax.div(cell, WIN_LAT), LEV), lax.rem(cell, WIN_LAT)
    half_rows, half_cols = WIN_LAT // 2, WIN_LON // 2
    quarter = 2 * lax.div(row, half_rows) + lax.div(col, half_cols)
    place = lax.rem(row, half_rows) * half_cols + lax.rem(col, half_cols)
    return quarter * stride + place * LEV + lax.rem(level + LEV // 2, LEV)


def unpack_kernel(own_ref, near_ref, lat_ref, near_diag_ref, out_ref):
    half_rows, half_cols = WIN_LAT // 2, WIN_LON // 2
    quarters = (
        near_ref[...].astype(f32)[:QUARTER],
        own_ref[...].astype(f32),
        near_diag_ref[...].astype(f32)[QUARTER:],
        lat_ref[...].astype(f32),
    )
    for (lat_half, lon_half), cells in zip(QUARTERS, quarters):
        first_row, first_col = (1 - lat_half) * half_rows, (1 - lon_half) * half_cols
        for row in range(half_rows):
            for col in range(half_cols):
                first = (row * half_cols + col) * LEV
                out_ref[first_row + row, first_col + col] = cells[first : first + LEV].astype(bf16)


def bias_kernel(
    table_ref,
    win_src,
    wout_src,
    out_ref,
    win_t_ref,
    lanes_ref,
    rows_ref,
    eye_ref,
    place_ref,
    place_t_ref,
    win_ref,
    wout_ref,
    stage,
    full,
    sems,
):
    copies = fetch((win_src, wout_src), (win_ref, wout_ref), sems)
    features = win_ref.shape[0]
    square = (features, features)
    eye = one_hot(counted(square, 0) == counted(square, 1))
    eye_ref[...] = eye
    place_ref[...] = one_hot(cell_source(counted((CELLS, 1), 0), QUARTER) == counted((CELLS, CELLS), 1))
    place_t_ref[...] = one_hot(cell_source(counted((1, CELLS), 1), QUARTER) == counted((CELLS, CELLS), 0))
    lane = counted((1, WIDE), 1)
    target = jnp.where(lane < SPAN, lax.rem(lane, PLANE) * (SPAN // PLANE) + lax.div(lane, PLANE), -1)
    lanes_ref[...] = one_hot(target == counted((WIDE, WIDE), 0))
    sixteens = HEADS * 16
    row = counted((sixteens, 1), 0)
    target = jnp.where(lax.rem(row, 16) < PLANE, lax.rem(row, 16) * 16 + lax.div(row, 16), -1)
    rows_ref[...] = one_hot(target == counted((sixteens, sixteens), 1))

    stage[...] = jnp.zeros(stage.shape, f32)
    reach = SPAN // PLANE
    table = table_ref[...].astype(f32)
    for first, plane_i, plane_j in segments():
        stage[16 * plane_j : 16 * plane_j + HEADS, reach * plane_i : reach * (plane_i + 1)] = table[
            :, first : first + reach
        ]
    moved = nn_dot(stage[...].astype(bf16), lanes_ref[...]).astype(bf16)
    rows = nn_dot(rows_ref[...], moved)

    for col in range(WIN_LON):
        shift = PLANE * (WIN_LON - 1 - col)
        moved = rows if shift == 0 else pltpu.roll(rows, WIDE - shift, 1)
        for head in range(HEADS):
            full[head, PLANE * col : PLANE * (col + 1), :] = moved[16 * head : 16 * head + PLANE, :CELLS]
    for head in range(HEADS):
        out_ref[head] = full[head].astype(bf16)
    for copy in copies:
        copy.wait()
    win_t_ref[...] = nt_dot(eye, win_ref[:, :features]).astype(bf16)


def window_kernel(
    packet,
    own_ref,
    near_ref,
    near_diag_ref,
    lat_ref,
    gain_ref,
    win_ref,
    win_t_ref,
    wout_ref,
    bias_ref,
    place_ref,
    keep_ref,
    send_ref,
    scores_ref,
    right,
    normalized_ref,
    inv_std_ref,
    cot_ref,
    left,
):
    features = win_ref.shape[0]
    head_dim = features // HEADS
    group_heads = LANES // head_dim
    score_scale = head_dim ** (-0.5)
    near = near_ref[...].astype(f32)
    quarters = (near, own_ref[...].astype(f32), near_diag_ref[...].astype(f32), lat_ref[...].astype(f32))
    sides = [jnp.concatenate([quarter[at : at + QUARTER] for quarter in quarters], axis=0) for at in (0, QUARTER)]
    cell, lane = counted((CELLS, CELLS), 0), counted((CELLS, CELLS), 1)
    source = lax.rem(cell, PLANE) * WIN_LON + lax.div(cell, PLANE)
    ids = near[2 * QUARTER : 2 * QUARTER + 1, :CELLS]
    region_col = jnp.sum(jnp.where(source == lane, ids, 0.0), axis=1, keepdims=True)
    region_row = jnp.sum(jnp.where(cell == lane, region_col, 0.0), axis=0, keepdims=True)
    same = region_col == region_row
    placed = nn_dot(place_ref[...], jnp.concatenate(sides, axis=1).astype(bf16))
    field, cot_f32 = placed[:, :features], placed[:, features:]
    cot = cot_f32.astype(bf16)
    cot_ref[...] = cot
    gain = gain_ref[...].reshape(1, features)

    centred = field - jnp.mean(field, axis=-1, keepdims=True)
    inv_std = lax.rsqrt(jnp.mean(centred * centred, axis=-1, keepdims=True) + norm_eps)
    normalized = centred * inv_std
    normalized_ref[...] = normalized
    inv_std_ref[...] = inv_std
    normed = (normalized * gain).astype(bf16)

    query_t = nt_dot(win_t_ref[...], normed).astype(bf16)
    wide_keys_values = nn_dot(normed, win_ref[:, features:])
    keys_values = wide_keys_values.astype(bf16)
    grad_att_t = nt_dot(wout_ref[...], cot).astype(bf16)
    key_value_t = jnp.transpose(wide_keys_values).astype(bf16)
    left[0] = jnp.transpose(normed.astype(f32)).astype(bf16)
    right[3] = jnp.transpose(cot_f32).astype(bf16)

    def spread(head_rows, slot):
        parts = []
        if slot:
            parts.append(jnp.zeros((slot * head_dim, CELLS), bf16))
        parts.append(head_rows)
        if slot < group_heads - 1:
            parts.append(jnp.zeros(((group_heads - 1 - slot) * head_dim, CELLS), bf16))
        return jnp.concatenate(parts, axis=0)

    def rows_of(head):
        return slice(head * head_dim, (head + 1) * head_dim)

    def part(head, index):
        if index == 0:
            return query_t[rows_of(head)]
        first = (index - 1) * features + head * head_dim
        return key_value_t[first : first + head_dim]

    def scores_of(head):
        group, slot = divmod(head, group_heads)
        keys = keys_values[:, group * LANES : (group + 1) * LANES]
        values = keys_values[:, features + group * LANES : features + (group + 1) * LANES]
        scores = nn_dot(keys, spread(part(head, 0), slot))
        return scores, nn_dot(values, spread(grad_att_t[rows_of(head)], slot))

    def softmax_of(head, scores, grad_probs):
        scores = jnp.where(same, scores * score_scale + bias_ref[head].astype(f32), masked_score)
        grown = jnp.exp(scores - jnp.max(scores, axis=0, keepdims=True))
        probs = grown * (1.0 / jnp.sum(grown, axis=0, keepdims=True))
        weighted = probs * grad_probs
        grad_scores = weighted - probs * jnp.sum(weighted, axis=0, keepdims=True)
        return probs.astype(bf16), (grad_scores * score_scale).astype(bf16)

    def products_of(head, probs_low, scores_low):
        rows = rows_of(head)
        scores_ref[head] = scores_low
        left[1, rows] = nn_dot(part(head, 2), probs_low).astype(bf16)
        right[0, rows] = nn_dot(part(head, 1), scores_low).astype(bf16)
        right[1, rows] = nt_dot(part(head, 0), scores_low).astype(bf16)
        right[2, rows] = nt_dot(grad_att_t[rows], probs_low).astype(bf16)

    raw, soft = {}, {}
    for turn in range(HEADS + 2):
        if turn < HEADS:
            raw[turn] = scores_of(turn)
        if 1 <= turn <= HEADS:
            soft[turn - 1] = softmax_of(turn - 1, *raw.pop(turn - 1))
        if turn >= 2:
            products_of(turn - 2, *soft.pop(turn - 2))

    odd = lax.rem(lax.axis_index("lat"), 2)

    for out_ref, half in ((send_ref, 1 - odd), (keep_ref, odd)):
        low = nt_dot(left[0], right[2 * half])
        high = nt_dot(left[half], right[2 * half + 1])
        for owner in range(packet.lon_count):
            rows = slice(owner * packet.weight_rows, (owner + 1) * packet.weight_rows)
            pieces = [
                block[rows, tile * LANES : (tile + 1) * LANES] for block in (low, high) for tile in range(3)
            ]
            if packet.weight_size > packet.weight_used:
                pieces.append(jnp.zeros((packet.weight_size - packet.weight_used, LANES), f32))
            first = owner * packet.weight_size
            out_ref[first : first + packet.weight_size] = jnp.concatenate(pieces, axis=0).astype(bf16)


def field_kernel(
    win_ref,
    grad_projected_ref,
    normalized_ref,
    inv_std_ref,
    cot_ref,
    gain_ref,
    place_t_ref,
    eye_ref,
    back_own_ref,
    back_near_ref,
    back_lat_ref,
    gain_out_ref,
):
    features = win_ref.shape[0]
    grad_shifted_t = sum(
        nn_dot(win_ref[:, block * features : (block + 1) * features], grad_projected_ref[block]) for block in range(3)
    ).astype(bf16)
    grad_normed = nt_dot(eye_ref[:CELLS, :CELLS], grad_shifted_t)
    normalized = normalized_ref[...]
    scaled = grad_normed * gain_ref[...].reshape(1, features)
    grad_field = cot_ref[...].astype(f32) + inv_std_ref[...] * (
        scaled
        - jnp.mean(scaled, axis=-1, keepdims=True)
        - normalized * jnp.mean(scaled * normalized, axis=-1, keepdims=True)
    )
    back = nn_dot(place_t_ref[...], grad_field.astype(bf16))
    quarters = [back[quarter * QUARTER : (quarter + 1) * QUARTER] for quarter in range(4)]
    back_own_ref[...] = quarters[1].astype(bf16)
    back_near_ref[...] = jnp.concatenate(quarters[::2], axis=0).astype(bf16)
    back_lat_ref[...] = quarters[3].astype(bf16)
    gain_sum = jnp.sum(grad_normed * normalized, axis=0, keepdims=True)
    gain_rows = [gain_sum[:, tile * LANES : (tile + 1) * LANES] for tile in range(3)]
    gain_out_ref[...] = jnp.concatenate(gain_rows + [jnp.zeros((13, LANES), f32)], axis=0).astype(bf16)


def fold_kernel(packet, scores_ref, lanes_ref, rows_ref, out_ref, wide, table, flat):
    wide[...] = jnp.zeros(wide.shape, f32)
    table[...] = jnp.zeros(table.shape, f32)
    flat[...] = jnp.zeros(flat.shape, bf16)
    for head in range(HEADS):
        wide[head % 2, :, :CELLS] = scores_ref[head].astype(f32)
        total = wide[head % 2, :PLANE, :]
        for col in range(1, WIN_LON):
            total = pltpu.roll(total, PLANE, 1) + wide[head % 2, PLANE * col : PLANE * (col + 1), :]
        table[16 * head : 16 * head + PLANE, :] = total
    moved = nn_dot(rows_ref[...], table[...].astype(bf16)).astype(bf16)
    moved = nt_dot(moved, lanes_ref[...]).astype(bf16)
    reach = SPAN // PLANE
    for first, plane_i, plane_j in segments():
        flat[:, first : first + reach] = moved[16 * plane_j : 16 * (plane_j + 1), reach * plane_i : reach * (plane_i + 1)]
    tiles = [
        flat[:, tile * LANES : (tile + 1) * LANES].astype(f32)[:HEADS] for tile in range(packet.table_tiles)
    ]
    tiles.append(jnp.zeros((packet.table_size - packet.table_rows, LANES), f32))
    out_ref[...] = jnp.concatenate(tiles, axis=0).astype(bf16)


def first_exchange_kernel(packet, keep_ref, recv_ref, table_ref, *out_refs):
    low = lax.rem(lax.axis_index("lon"), 4)
    size, quarter = packet.weight_size, packet.quarter
    for step, out_ref in enumerate(out_refs):
        digit = lax.bitwise_xor(low, step)
        for upper in range(packet.lon_count // 4):
            rows = pl.ds(pl.multiple_of((upper * 4 + digit) * size, 16), size)
            out_ref[upper * size : (upper + 1) * size] = keep_ref[rows] + recv_ref[rows]
        first = packet.lon_count // 4 * size
        out_ref[first:] = table_ref[pl.ds(pl.multiple_of(digit * quarter, 16), quarter)]


def summed(refs, rows):
    terms = [ref[rows] for ref in refs]
    while len(terms) > 1:
        terms = [left + right for left, right in zip(terms[::2], terms[1::2])]
    return terms[0]


def next_exchange_kernel(packet, shift, gains, *refs):
    gain_refs, held, out_refs = refs[:gains], refs[gains:-4], refs[-4:]
    size, quarter = packet.weight_size, packet.quarter
    digit = lax.rem(lax.shift_right_logical(lax.axis_index("lon"), shift), 4)
    groups = (out_refs[0].shape[0] - quarter - 16) // size
    rest = 4 * groups * size
    table = summed(held, slice(rest, rest + quarter))
    gain = summed(gain_refs, slice(0, 16)) if gains else summed(held, slice(rest + quarter, rest + quarter + 16))
    for step, out_ref in enumerate(out_refs):
        for upper in range(groups):
            owner = upper * 4 + lax.bitwise_xor(digit, step)
            out_ref[upper * size : (upper + 1) * size] = summed(held, pl.ds(pl.multiple_of(owner * size, 16), size))
        out_ref[groups * size : groups * size + quarter] = table
        out_ref[groups * size + quarter :] = gain


def last_sum_kernel(packet, a_ref, b_ref, c_ref, d_ref, upper_ref, lower_ref, table_ref):
    refs, cut = (a_ref, b_ref, c_ref, d_ref), upper_ref.shape[0]
    upper_ref[...] = summed(refs, slice(0, cut))
    lower_ref[...] = summed(refs, slice(cut, packet.weight_size))
    table_ref[...] = summed(refs, slice(packet.weight_size, packet.weight_size + packet.quarter + 16))


def weights_out_kernel(packet, factor, upper_ref, lower_ref, other_upper_ref, other_lower_ref, grad_in_ref, grad_out_ref):
    odd = lax.rem(lax.axis_index("lat"), 2) == 1
    own = jnp.concatenate([upper_ref[...], lower_ref[...]], axis=0).astype(f32) * factor
    other = jnp.concatenate([other_upper_ref[...], other_lower_ref[...]], axis=0).astype(f32) * factor
    halves = (jnp.where(odd, other, own), jnp.where(odd, own, other))
    size = packet.weight_rows
    tiles = [half[tile * size : (tile + 1) * size] for half in halves for tile in range(6)]
    grad_in_ref[...] = jnp.concatenate(tiles[:9], axis=1).astype(bf16)
    grad_out_ref[...] = jnp.concatenate(tiles[9:], axis=1).astype(bf16)


def table_out_kernel(packet, table_scale, factor, a_ref, b_ref, c_ref, d_ref, grad_table_ref, grad_gain_ref, quarters):
    low = lax.rem(lax.axis_index("lon"), 4)
    parts = (a_ref, b_ref, c_ref, d_ref)
    for step, ref in enumerate(parts):
        quarters[lax.bitwise_xor(low, step)] = ref[: packet.quarter].astype(f32)
    total = quarters[...].reshape(packet.table_size, LANES)
    for tile in range(packet.table_tiles):
        first = tile * LANES
        width = min(LANES, grad_table_ref.shape[2] - first)
        block = total[HEADS * tile : HEADS * (tile + 1), :width] * table_scale
        for head in range(HEADS):
            grad_table_ref[head, :, first : first + width] = block[head : head + 1]
    gain = sum(ref[packet.quarter :].astype(f32) for ref in parts) * factor
    grad_gain_ref[...] = jnp.concatenate([gain[tile : tile + 1] for tile in range(3)], axis=1).reshape(
        grad_gain_ref.shape
    )


def whole(count):
    return [pl.BlockSpec(memory_space=pltpu.VMEM)] * count


def call(kernel, name, in_specs, outs, scratch=(), flops=0, moved=0):
    return pl.pallas_call(
        kernel,
        name=name,
        out_shape=outs,
        in_specs=in_specs,
        out_specs=jax.tree.map(lambda _: pl.BlockSpec(memory_space=pltpu.VMEM), outs),
        scratch_shapes=list(scratch),
        compiler_params=pltpu.CompilerParams(vmem_limit_bytes=20 * 1024 * 1024),
        cost_estimate=pl.CostEstimate(flops=flops, bytes_accessed=moved, transcendentals=0),
    )


def on_device(lon_count, lat_count, latent_field, cotangent, norm_gain, input_weight, output_weight, bias_table, regions):
    features = latent_field.shape[3]
    head_dim = features // HEADS
    packet = Packet(lon_count, features)

    def move(value, lon_step, lat_step):
        pairs = []
        for lon in range(lon_count):
            for lat in range(lat_count):
                target = ((lon + lon_step) % lon_count) * lat_count + (lat + lat_step) % lat_count
                pairs.append((lon * lat_count + lat, target))
        return lax.ppermute(value, ("lon", "lat"), pairs)

    def swap(value, axis, mask):
        count = lon_count if axis == "lon" else lat_count
        return lax.ppermute(value, axis, [(source, source ^ mask) for source in range(count)])

    struct = jax.ShapeDtypeStruct
    def in_hbm(*arrays):
        return [pltpu.with_memory_space_constraint(array, pltpu.HBM) for array in arrays]

    def space_for(array):
        return pltpu.VMEM(array.shape, array.dtype)

    hbm = pl.BlockSpec(memory_space=pltpu.HBM)
    field, cot = jnp.transpose(latent_field, (1, 2, 0, 3)), jnp.transpose(cotangent, (1, 2, 0, 3))
    small = (jnp.transpose(regions, (1, 0, 2)), bias_table[0], norm_gain)
    same, others = struct((SAME, features), bf16), struct((2 * QUARTER, features), bf16)
    own, far, far_others, to_lat, table, gain = call(
        load_kernel,
        "load",
        [hbm] * 5,
        [others, same, others, others] + [struct(array.shape, array.dtype) for array in small[1:]],
        [space_for(field), space_for(cot), space_for(small[0]), pltpu.SemaphoreType.DMA((5,))],
        moved=1 << 20,
    )(*in_hbm(field, cot, *small))
    from_near = move(far, 1, 0)
    from_near_diag = move(far_others, 1, -1)
    from_lat = move(to_lat, 0, -1)

    bias_full, input_weight_t, lane_moves, row_moves, eye, place, place_t, weight_in, weight_out = call(
        bias_kernel,
        "expand_bias",
        whole(1) + [hbm] * 2,
        [
            struct((HEADS, CELLS, CELLS), bf16),
            struct((features, features), bf16),
            struct((WIDE, WIDE), bf16),
            struct((HEADS * 16, HEADS * 16), bf16),
            struct((features, features), bf16),
            struct((CELLS, CELLS), bf16),
            struct((CELLS, CELLS), bf16),
            struct(input_weight.shape, bf16),
            struct(output_weight.shape, bf16),
        ],
        [
            pltpu.VMEM((HEADS * 16, WIDE), f32),
            pltpu.VMEM((HEADS, CELLS, CELLS), f32),
            pltpu.SemaphoreType.DMA((2,)),
        ],
        moved=1 << 21,
    )(table, *in_hbm(input_weight, output_weight))

    half_sum = struct((lon_count * packet.weight_size, LANES), bf16)
    results = call(
        functools.partial(window_kernel, packet),
        "window",
        whole(10),
        [
            half_sum,
            half_sum,
            struct((HEADS, CELLS, CELLS), bf16),
            struct((4, features, CELLS), bf16),
            struct((CELLS, features), f32),
            struct((CELLS, 1), f32),
            struct((CELLS, features), bf16),
        ],
        [pltpu.VMEM((2, features, CELLS), bf16)],
        flops=10**9,
        moved=5 << 20,
    )(
            own,
        from_near,
        from_near_diag,
        from_lat,
        gain,
        weight_in,
        input_weight_t,
        weight_out,
        bias_full,
        place,
    )
    keep, send, scores_low, *saved = results

    received = swap(send, "lat", 1)
    table_part = call(
        functools.partial(fold_kernel, packet),
        "fold_table",
        whole(3),
        struct((packet.table_size, LANES), bf16),
        [
            pltpu.VMEM((2, CELLS, WIDE), f32),
            pltpu.VMEM((HEADS * 16, WIDE), f32),
            pltpu.VMEM((16, packet.table_tiles * LANES), bf16),
        ],
        moved=1 << 21,
    )(scores_low, lane_moves, row_moves)

    groups = lon_count // 4
    parts = call(
        functools.partial(first_exchange_kernel, packet),
        "add_lat",
        whole(3),
        [struct((groups * packet.weight_size + packet.quarter, LANES), bf16)] * 4,
        moved=2 << 20,
    )(keep, received, table_part)
    parts, saved = lax.optimization_barrier((parts, saved))

    def trade(parts, shift):
        return [swap(parts[step], "lon", step << shift) for step in (3, 2, 1)] + [parts[0]]

    held = trade(parts, 0)
    piece = struct((QUARTER, features), bf16)
    back_own, back_near, back_lat, gain_part = call(
        field_kernel,
        "grad_field",
        whole(8),
        [piece, others, piece, struct((16, LANES), bf16)],
        flops=10**8,
        moved=5 << 20,
    )(weight_in, *saved, gain, place_t, eye)
    home_lat = move(back_lat, 0, 1)
    gain_other = swap(gain_part, "lat", 1)
    held, home_lat, gain_other = lax.optimization_barrier((held, home_lat, gain_other))
    gains = [gain_part, gain_other]
    home_near = move(back_near, -1, 0)
    home_diag = move(home_near, 0, 1)
    for shift in range(2, lon_count.bit_length() - 1, 2):
        groups //= 4
        parts = call(
            functools.partial(next_exchange_kernel, packet, shift, len(gains)),
            "add_lon",
            whole(len(gains) + 4),
            [struct((groups * packet.weight_size + packet.quarter + 16, LANES), bf16)] * 4,
            moved=1 << 20,
        )(*gains, *held)
        gains = []
        held = trade(parts, shift)
    cut = rounded_up(packet.weight_size // 2, 16)
    *weight_sums, table_sum = call(
        functools.partial(last_sum_kernel, packet),
        "add_last",
        whole(4),
        [struct((rows, LANES), bf16) for rows in (cut, packet.weight_size - cut, packet.quarter + 16)],
        moved=1 << 18,
    )(*held)
    table_parts = trade([table_sum] * 4, 0)[::-1]
    for bit in range(1, lat_count.bit_length() - 1):
        weight_sums = [part + swap(part, "lat", 1 << bit) for part in weight_sums]
    weight_others = [swap(part, "lat", 1) for part in weight_sums]

    cells_in_all = latent_field.shape[0] * latent_field.shape[1] * latent_field.shape[2]
    factor = 1.0 / math.sqrt(cells_in_all * lon_count * lat_count)
    grad_input_weight, grad_output_weight = call(
        functools.partial(weights_out_kernel, packet, factor),
        "weights_out",
        whole(4),
        [struct((packet.weight_rows, 3 * features), bf16), struct((packet.weight_rows, features), bf16)],
        moved=1 << 18,
    )(*weight_sums, *weight_others)
    table_parts, grad_input_weight = lax.optimization_barrier((table_parts, grad_input_weight))
    grad_table, gain_sum = call(
        functools.partial(table_out_kernel, packet, math.sqrt(head_dim), factor),
        "table_out",
        whole(4),
        [struct((HEADS, 1, PLANE * SPAN), f32), struct((features,), f32)],
        [pltpu.VMEM((4, packet.quarter, LANES), f32)],
        moved=1 << 19,
    )(*table_parts)
    for bit in range(1, lat_count.bit_length() - 1):
        gain_sum = gain_sum + swap(gain_sum, "lat", 1 << bit)

    grad_field = call(
        unpack_kernel,
        "unpack_quarters",
        whole(4),
        struct((WIN_LAT, WIN_LON, LEV, features), bf16),
        moved=4 << 20,
    )(back_own, home_near, home_lat, home_diag)
    return (
        jnp.transpose(grad_field, (2, 0, 1, 3)),
        grad_input_weight,
        grad_output_weight,
        gain_sum,
        jnp.transpose(grad_table, (1, 0, 2)),
    )


def solution(mesh):
    in_specs = (
        P(None, "lat", "lon", None),
        P(None, "lat", "lon", None),
        P(),
        P(),
        P(),
        P("lat", None, None),
        P(None, "lat", "lon"),
    )
    out_specs = (
        P(None, "lat", "lon", None),
        P("lon", None),
        P("lon", None),
        P(),
        P("lat", None, None),
    )
    return jax.shard_map(
        functools.partial(on_device, mesh.shape["lon"], mesh.shape["lat"]),
        mesh=mesh,
        in_specs=in_specs,
        out_specs=out_specs,
        check_vma=False,
    )
```
